512 devices in a mesh: seq: 16 (over y, core), ep: 32 (over z, x).
Axes of the slice: x: 4, y: 8, z: 8, core: 2. Of those that a mesh axis runs over, the one named last changes fastest.
Arguments:
- latent: bfloat16 [256, 2048, 576], P('ep', 'seq'), may hold values from -6 to 6
- lengths: int32 [32, 8], P('ep'), may hold values from 1 to 2048, 13107 in all within a row
- queries: bfloat16 [256, 128, 576], P('ep', 'seq'), may hold values from -30 to 30
- fresh_latent: bfloat16 [256, 576], P('ep'), may hold values from -7 to 7
- tokens: bfloat16 [1024, 3584], P('ep', 'seq'), may hold values from -6 to 6
- routes: int32 [1024, 8], P('ep'), may hold values from 0 to 31, all different within a row; in each aligned block of 32 rows (0 to 31, 32 to 63, ...) at most 16 rows name the same one
- gates: float32 [1024, 8], P('ep'), may hold values from 0.05 to 0.5
- w_gate: bfloat16 [32, 3584, 2048], P('ep', None, 'seq'), may hold values from -0.09375 to 0.09375
- w_up: bfloat16 [32, 3584, 2048], P('ep', None, 'seq'), may hold values from -0.09375 to 0.09375
- w_down: bfloat16 [32, 2048, 3584], P('ep', 'seq'), may hold values from -0.125 to 0.125
Outputs:
- context: bfloat16 [256, 128, 512], P('ep', 'seq')
- mixed_out: bfloat16 [1024, 3584], P('ep', 'seq')
The draws below stay inside these ranges and needn't reach their ends.
Inputs may be any that keep to these rules, and one draw needn't show every extreme that they name: `routes`: in the 32 tokens of one index of ep no expert is named more than 16 times. Each row of 8 lengths sums to 13107.
All inputs are finite; a program needn't handle non-finite values.
Results may differ from the reference program's by a relative error of at most 0.025.
Values may be sent and summed in bfloat16 or wider, within the bound.
A program may use at most 128 MiB of HBM per device.

```python
import math
import jax
import jax.numpy as jnp
import numpy as np
from jax import lax

D = 3584
FF = 2048
LAT = 512
ROPE = 64
HEADS = 128
TOPK = 8
EXPERTS = 32
TC = 32
PLEN = 2048
REQ = 8
CAP = 16
TOKENS = 1024
N_SEQ = 16
N_EP = 32


def shared_rows(key):
    return jnp.clip(jax.random.normal(key, (N_EP * REQ, PLEN, LAT + ROPE), jnp.float32), -6.0, 6.0)


def fresh_parts(key):
    first_rows = shared_rows(key)[:, 0, :]
    return first_rows


def draw_latent(key, part):
    values = shared_rows(key)
    return values.astype(jnp.bfloat16)


def draw_fresh_latent(key, part):
    first_rows = fresh_parts(key)
    key = jax.random.fold_in(key, 2)
    values = jax.random.normal(key, first_rows.shape, jnp.float32)
    return jnp.clip(values, -7.0, 7.0).astype(jnp.bfloat16)


def draw_queries(key, part):
    key = jax.random.fold_in(key, 3)
    drawn_draw = 0.5 * jax.random.normal(key, (N_EP * REQ, HEADS, LAT + ROPE), jnp.float32)
    return jnp.clip(drawn_draw, -30.0, 30.0).astype(jnp.bfloat16)


def steps_of(key, dims, cuts, smallest, high):
    gain, own = 1.0, jax.random.fold_in(key, 6)
    for axis_at, parts in cuts:
        steps = jnp.exp(jax.random.uniform(jax.random.fold_in(own, axis_at), (parts,), jnp.float32, smallest / len(cuts), high / len(cuts)))
        gain = gain * jnp.repeat(steps, dims[axis_at] // parts).reshape([-1 if axis == axis_at else 1 for axis in range(len(dims))])
    return gain


def split_up(count, total, most, slope):
    portions = [(1 << 20) // math.isqrt(rank ** slope) + 1 for rank in range(2, count + 1)]
    rest, given = total - most - (count - 1), [1] * (count - 1)
    while rest > 0:
        free = [i for i in range(count - 1) if given[i] < most]
        mass, remaining = sum([portions[i] for i in free]), rest
        for i in free:
            extra = min(most - given[i], max(1, remaining * portions[i] // mass), rest)
            given[i] = given[i] + extra
            rest = rest - extra
    return np.array([most] + given)


def ragged(own_key, amount, total, limit, skew):
    if amount == 2:
        one = jax.random.randint(own_key, (), max(1, total - limit), min(limit, total - 1) + 1)
        return jnp.stack([one, total - one])
    sizes = jnp.asarray(split_up(amount, total, limit, skew), jnp.int32)
    couples = (amount - 1) // 2
    donor, sink = sizes[1:1 + 2 * couples:2], sizes[2:2 + 2 * couples:2]
    margin = jnp.minimum(donor - 1, limit - sink)
    passed = jax.random.randint(jax.random.fold_in(own_key, 1), (couples,), 0, 1 << 20) % (margin + 1)
    sizes = sizes.at[1:1 + 2 * couples:2].set(donor - passed).at[2:2 + 2 * couples:2].set(sink + passed)
    return sizes[jax.random.permutation(jax.random.fold_in(own_key, 2), amount)]


def deal_out(rng, own, number, rows, count, top, bound, lean):
    order = jax.random.permutation(rng, count)
    packed, ordinary = portions_of(count, rows * top, bound, lean, True), portions_of(count, rows * top, bound, lean, False)
    places = jnp.arange(count)

    def named(tallies, rotation):
        used = int((tallies > 0).sum())
        fixed = max(1, used // 4)
        shifted = fixed + (places - fixed + rotation * (used - fixed)) % max(1, count - fixed)
        return jnp.zeros((count,), jnp.int32).at[order[jnp.where(places < fixed, places, shifted)]].set(jnp.asarray(tallies, jnp.int32))

    tallies = jnp.where(number % 4 == 0, named(packed, number // 4), named(ordinary, number - number // 4 - 1))
    mixed = jax.random.permutation(jax.random.fold_in(own, 3), count)
    source_of, sink = mixed[0:count // 2 * 2:2], mixed[1:count // 2 * 2:2]
    margin = jnp.minimum(tallies[source_of] - 1, bound - tallies[sink]) // 2
    margin = jnp.where((source_of == order[0]) | (sink == order[0]) | (tallies[sink] == 0), 0, jnp.maximum(margin, 0))
    shifted = jax.random.randint(jax.random.fold_in(own, 4), (count // 2,), 0, 1 << 20) % (margin + 1)
    tallies = tallies.at[source_of].add(-shifted).at[sink].add(shifted)
    items = jnp.searchsorted(jnp.cumsum(tallies), jnp.arange(rows * top), side="right").astype(jnp.int32)
    grid = items.reshape(top, rows).T
    grid = grid[jax.random.permutation(jax.random.fold_in(own, 1), rows)]
    rotation = jax.random.randint(jax.random.fold_in(own, 2), (rows, 1), 0, top)
    return jnp.take_along_axis(grid, (jnp.arange(top)[None, :] + rotation) % top, axis=1)


def portions_of(number_of, total, bound, slope, full):
    portions = [(1 << 20) // math.isqrt(grade ** slope) + 1 for grade in range(1, number_of + 1)]
    largest = bound if full else min(bound, max(-(-total // number_of), total * portions[0] // sum(portions)))
    least = 1 if total - largest >= number_of - 1 else 0
    counts, rest = [largest] + [least] * (number_of - 1), total - largest - least * (number_of - 1)
    while rest > 0:
        free = [i for i in range(1, number_of) if counts[i] < largest] or [i for i in range(1, number_of) if counts[i] < bound]
        whole, left = sum([portions[i] for i in free]), rest
        for i in free:
            more = min(bound - counts[i], max(1, left * portions[i] // whole), rest)
            counts[i] = counts[i] + more
            rest = rest - more
    return np.array(counts)


def scatter_about(own_key, extent, scale, reach, pieces=(), held_as=jnp.bfloat16):
    entries = scale * jax.random.normal(own_key, extent, jnp.float32)
    if pieces:
        entries = entries * steps_of(own_key, extent, pieces, -0.22, 0.18)
    return jnp.clip(entries, -reach, reach).astype(held_as)


def setup_inputs(seed: int = 0) -> dict:
    seeds = jax.random.split(jax.random.key(seed), 11)
    latent = draw_latent(jax.random.fold_in(seeds[10], 71), 0)
    lengths = jax.vmap(lambda own: ragged(own, REQ, REQ * PLEN * 4 // 5, PLEN, 2))(jax.random.split(seeds[1], N_EP)).reshape((N_EP, REQ)).astype(jnp.int32)
    queries = draw_queries(jax.random.fold_in(seeds[10], 71), 0)
    fresh_latent = draw_fresh_latent(jax.random.fold_in(seeds[10], 71), 0)
    tokens = scatter_about(seeds[4], (TOKENS, D), 1.0, 6.0, ((0, 32), (1, 16)))
    routes_keys = jax.random.split(jax.random.fold_in(seeds[5], 1), TOKENS // TC)
    routes_turns = jax.random.permutation(jax.random.fold_in(seeds[5], 3), TOKENS // TC)
    routes = jax.vmap(lambda own, number: deal_out(jax.random.fold_in(seeds[5], 2), own, number, TC, EXPERTS, TOPK, CAP, 2))(routes_keys, routes_turns).reshape((TOKENS, TOPK))
    gates = jnp.clip(jnp.exp(math.log(0.5) - 2.3025851 * jax.random.uniform(seeds[6], (TOKENS, TOPK), jnp.float32) ** steps_of(seeds[6], (TOKENS, TOPK), ((0, 32),), -0.2, 0.2)), 0.05, 0.5)
    w_gate = scatter_about(seeds[7], (EXPERTS, D, FF), D ** -0.5, 0.09375, ((0, 32), (2, 16)))
    w_up = scatter_about(seeds[8], (EXPERTS, D, FF), D ** -0.5, 0.09375, ((0, 32), (2, 16)))
    w_down = scatter_about(seeds[9], (EXPERTS, FF, D), FF ** -0.5, 0.125, ((0, 32), (1, 16)))
    return dict(latent=latent, lengths=lengths, queries=queries, fresh_latent=fresh_latent, tokens=tokens, routes=routes, gates=gates, w_gate=w_gate, w_up=w_up, w_down=w_down)


score_scale = 0.07216878364870322
neg_fill = -1.0e30


def slot_table(route_rows, experts, capacity):
    flat_rows = route_rows.reshape(-1)
    one_hot = (flat_rows[:, None] == jnp.arange(experts, dtype=jnp.int32)[None, :]).astype(jnp.int32)
    before = jnp.cumsum(one_hot, axis=0) - one_hot
    position = jnp.sum(before * one_hot, axis=1)
    return (flat_rows * capacity + position).astype(jnp.int32).reshape(route_rows.shape)


def attend(query_rows, cache_rows, fresh_key, length):
    scores = jnp.einsum("hc,sc->hs", query_rows, cache_rows, preferred_element_type=jnp.float32) * score_scale
    position = jnp.arange(cache_rows.shape[0], dtype=jnp.int32)
    scores = jnp.where(position[None, :] < length, scores, neg_fill)
    own_score = jnp.dot(query_rows, fresh_key, preferred_element_type=jnp.float32) * score_scale
    highest = jnp.maximum(jnp.max(scores, axis=1), own_score)
    weights = jnp.exp(scores - highest[:, None])
    own_weight = jnp.exp(own_score - highest)
    totals = jnp.sum(weights, axis=1) + own_weight
    probability = (weights / totals[:, None]).astype(jnp.bfloat16)
    own_prob = (own_weight / totals).astype(jnp.bfloat16)
    summed = jnp.dot(probability, cache_rows[:, :LAT], preferred_element_type=jnp.float32)
    summed = summed + own_prob.astype(jnp.float32)[:, None] * fresh_key[:LAT].astype(jnp.float32)[None, :]
    return summed.astype(jnp.bfloat16)


def reference(latent, lengths, queries, fresh_latent, tokens, routes, gates, w_gate, w_up, w_down):
    flat_len = lengths.reshape(-1)

    def one_request(inputs):
        return attend(inputs[0], inputs[1], inputs[2], inputs[3])

    context = lax.map(one_request, (queries, latent, fresh_latent, flat_len))

    columns = routes.reshape(N_EP, TC, TOPK)
    slot_ids = jax.vmap(lambda route_rows: slot_table(route_rows, EXPERTS, CAP))(columns)
    expert_ids = slot_ids // CAP
    position = slot_ids % CAP
    column_ids = jnp.broadcast_to(jnp.arange(N_EP, dtype=jnp.int32)[:, None, None], expert_ids.shape)
    spread_rows = jnp.broadcast_to(tokens.reshape(N_EP, TC, 1, D), (N_EP, TC, TOPK, D))
    bucket = jnp.zeros((EXPERTS, N_EP, CAP, D), jnp.bfloat16).at[expert_ids, column_ids, position].set(spread_rows)

    def one_expert(inputs):
        slot_rows = inputs[0].reshape(N_EP * CAP, D)
        gate_sum = jnp.dot(slot_rows, inputs[1], preferred_element_type=jnp.float32)
        up_sum = jnp.dot(slot_rows, inputs[2], preferred_element_type=jnp.float32)
        hidden = (jax.nn.silu(gate_sum) * up_sum).astype(jnp.bfloat16)
        hidden_blocks = hidden.reshape(N_EP * CAP, N_SEQ, FF // N_SEQ).astype(jnp.float32)
        down_blocks = inputs[3].reshape(N_SEQ, FF // N_SEQ, D).astype(jnp.float32)
        block_terms = jnp.einsum("rjf,jfd->jrd", hidden_blocks, down_blocks, precision=lax.Precision.HIGHEST).astype(jnp.bfloat16)
        return jnp.sum(block_terms.astype(jnp.float32), axis=0).astype(jnp.bfloat16)

    expert_out = lax.map(one_expert, (bucket, w_gate, w_up, w_down)).reshape(EXPERTS, N_EP, CAP, D)
    picked = expert_out[expert_ids, column_ids, position]
    weighted = gates.reshape(N_EP, TC, TOPK)[..., None] * picked.astype(jnp.float32)
    mixed_out = jnp.sum(weighted, axis=2).reshape(TOKENS, D).astype(jnp.bfloat16)
    return context, mixed_out
```

```python
import functools
import heapq

import jax
import jax.numpy as jnp
from jax import lax
from jax.experimental import pallas as pl
from jax.experimental.pallas import tpu as pltpu
from jax.sharding import PartitionSpec as P

MESH = pl.DeviceIdType.MESH
LAT = 512
NX = 4
LANE = 128
HALF_TOK = 16
SCALE = 0.07216878364870322
NEG = -1.0e30
F32 = jnp.float32
BF16 = jnp.bfloat16

LINK_RATE = 45.0e3
HOP = 1.5


def mod(value, n):
    return lax.rem(value + n, n)


class Net:
    def __init__(self, send, recv):
        self.send, self.recv = send, recv
        self.count, self.now = 0, 0.0
        self.links, self.copies = {}, []

    def copy(self, src, dst, device, link):
        at = self.count
        self.count += 1
        made = pltpu.make_async_remote_copy(
            src_ref=src,
            dst_ref=dst,
            send_sem=self.send.at[at],
            recv_sem=self.recv.at[at],
            device_id=device,
            device_id_type=MESH,
        )
        made.start()
        size = 2
        for extent in src.shape:
            size *= extent
        begin = max(self.links.get(link, 0.0), self.now)
        self.links[link] = begin + size / LINK_RATE
        self.copies.append(made)
        return made, self.links[link] + HOP

    def run(self, tasks):
        heap, order = [], 0
        for task in tasks:
            heap.append((self.now, order, task))
            order += 1
        heapq.heapify(heap)
        while heap:
            at, _, task = heapq.heappop(heap)
            self.now = max(self.now, at)
            try:
                ready = next(task)
            except StopIteration:
                continue
            order += 1
            heapq.heappush(heap, (ready, order, task))


def ring_gather(net, piece, cut, pos, n, device, axis, landed):
    far = n // 2
    up, down = device(mod(pos + 1, n)), device(mod(pos - 1, n))

    def part(ref, side, step):
        return cut(ref, side) if step == far else ref

    own = piece(pos)
    first = part(own, 0, 1)
    cu, tu = net.copy(first, first, up, axis + "+")
    first = part(own, 1, 1)
    cd, td = net.copy(first, first, down, axis + "-")
    landed(pos)
    for k in range(1, far):
        yield tu
        cu.wait_recv()
        at = mod(pos - k, n)
        src = part(piece(at), 0, k + 1)
        cu, tu = net.copy(src, src, up, axis + "+")
        landed(at)
        yield td
        cd.wait_recv()
        at = mod(pos + k, n)
        src = part(piece(at), 1, k + 1)
        cd, td = net.copy(src, src, down, axis + "-")
        landed(at)
    yield max(tu, td)
    cu.wait_recv()
    cd.wait_recv()
    landed(mod(pos + far, n))


def add_into(ref, other):
    ref[...] = (ref[...].astype(F32) + other[...].astype(F32)).astype(BF16)


def ring_scatter(net, piece, cut, arrived, pos, n, device, axis, ready, finish):
    far = n // 2
    up, down = device(mod(pos + 1, n)), device(mod(pos - 1, n))
    while not ready(far):
        yield net.now + 0.01
    src = cut(piece(mod(pos + far, n)), 0)
    cu, tu = net.copy(src, cut(arrived(0, 0), 0), up, axis + "+")
    src = cut(piece(mod(pos + far, n)), 1)
    cd, td = net.copy(src, cut(arrived(1, 0), 1), down, axis + "-")
    for k in range(1, far):
        d = far - k
        while not (ready(d) and ready(-d)):
            yield net.now + 0.01
        yield tu
        cu.wait_recv()
        mine, came = piece(mod(pos + d, n)), arrived(0, k - 1)
        if k == 1:
            add_into(cut(mine, 0), cut(came, 0))
        else:
            add_into(mine, came)
        cu, tu = net.copy(mine, arrived(0, k), up, axis + "+")
        yield td
        cd.wait_recv()
        mine, came = piece(mod(pos - d, n)), arrived(1, k - 1)
        if k == 1:
            add_into(cut(mine, 1), cut(came, 1))
        else:
            add_into(mine, came)
        cd, td = net.copy(mine, arrived(1, k), down, axis + "-")
    while not ready(0):
        yield net.now + 0.01
    yield max(tu, td)
    cu.wait_recv()
    cd.wait_recv()
    if far > 1:
        total = (
            piece(pos)[...].astype(F32)
            + arrived(0, far - 1)[...].astype(F32)
            + arrived(1, far - 1)[...].astype(F32)
        )
        finish(total)
    else:
        add_into(cut(piece(pos), 0), cut(arrived(0, 0), 0))
        add_into(cut(piece(pos), 1), cut(arrived(1, 0), 1))
        finish(piece(pos)[...].astype(F32))


def kernel(
    cfg,
    latent, queries, wg, wu, wd, lengths, fresh, tokens, routes, gates,
    ctx_out, mix_out,
    tokpad, tokbuf, line, xa, xb, wcat, wdcat, acc, hid, ya, yb,
    ra, rax, rbx, rb, ebuf, erecv,
    lbuf, qbuf, qf, obuf, orecv, cf, cb, crecv,
    local_sem, send_sem, recv_sem, t_send, t_recv, q_send, q_recv, e_send, e_recv,
):
    n_seq, n_z, wide_a, wide_b, share, heads = cfg
    n_y = n_seq // 2
    s, e = lax.axis_index("seq"), lax.axis_index("ep")
    y, c = s // 2, lax.rem(s, 2)
    z, x = e // NX, lax.rem(e, NX)
    other = 1 - c
    sibling = (2 * y + other, e)
    experts = n_z * NX
    rows = experts * HALF_TOK
    n_req = lengths.shape[1]
    half_req = n_req // 2
    q_rows = half_req * heads

    def at_x(i):
        return (s, z * NX + i)

    def at_z(i):
        return (s, i * NX + x)

    def local(src, dst, i):
        made = pltpu.make_async_copy(src, dst, local_sem.at[i])
        made.start()
        return made

    mine_q = queries.at[pl.ds(pl.multiple_of(c * q_rows, q_rows), q_rows)]
    loads = [
        local(mine_q, qbuf.at[s], 0),
        local(latent.at[pl.ds(c * half_req, half_req)], lbuf.at[0], 1),
        local(wg, wcat.at[:, pl.ds(0, LANE)], 2),
        local(wu, wcat.at[:, pl.ds(2 * LANE, LANE)], 3),
        local(wd, wdcat.at[pl.ds(0, LANE)], 4),
    ]
    for half in range(2):
        tokpad[half] = jnp.zeros_like(tokpad[half])
        tokpad[half, :, 0:share] = tokens[half * HALF_TOK:(half + 1) * HALF_TOK, :]

    barrier = pltpu.get_barrier_semaphore()

    def greet(j, carry):
        pl.semaphore_signal(
            barrier, inc=1, device_id=(lax.rem(s + j, n_seq), e), device_id_type=MESH
        )
        return carry

    lax.fori_loop(1, n_seq, greet, 0)
    for who in (at_x(mod(x + 1, NX)), at_x(mod(x - 1, NX)), at_z(mod(z + 1, n_z)), at_z(mod(z - 1, n_z))):
        pl.semaphore_signal(barrier, inc=1, device_id=who, device_id_type=MESH)
    pl.semaphore_wait(barrier, n_seq - 1 + 4)

    def token_copy(j):
        to = lax.rem(s + j, n_seq)
        return pltpu.make_async_remote_copy(
            src_ref=tokpad.at[lax.rem(to, 2)],
            dst_ref=tokbuf.at[s],
            send_sem=t_send.at[j],
            recv_sem=t_recv.at[j],
            device_id=(to, e),
            device_id_type=MESH,
        )

    def query_copy(j):
        to = lax.rem(s + j, n_seq)
        begin = pl.multiple_of(lax.rem(to, 2) * q_rows, q_rows)
        return pltpu.make_async_remote_copy(
            src_ref=queries.at[pl.ds(begin, q_rows)],
            dst_ref=qbuf.at[s],
            send_sem=q_send.at[j],
            recv_sem=q_recv.at[j],
            device_id=(to, e),
            device_id_type=MESH,
        )

    def end_copy(j):
        to = lax.rem(s + j, n_seq)
        return pltpu.make_async_remote_copy(
            src_ref=ebuf.at[to],
            dst_ref=erecv.at[s],
            send_sem=e_send.at[j],
            recv_sem=e_recv.at[j],
            device_id=(to, e),
            device_id_type=MESH,
        )

    def each(act):
        def body(j, carry):
            act(j)
            return carry

        lax.fori_loop(1, n_seq, body, 0)

    net = Net(send_sem, recv_sem)
    each(lambda j: token_copy(j).start())
    each(lambda j: query_copy(j).start())
    lat_copy, _ = net.copy(latent.at[pl.ds(other * half_req, half_req)], lbuf.at[1], sibling, "core")
    wg_copy, _ = net.copy(wg, wcat.at[:, pl.ds(LANE, LANE)], sibling, "core")
    wu_copy, _ = net.copy(wu, wcat.at[:, pl.ds(3 * LANE, LANE)], sibling, "core")
    wd_copy, _ = net.copy(wd, wdcat.at[pl.ds(LANE, LANE)], sibling, "core")

    first_row = pl.multiple_of(c * HALF_TOK, HALF_TOK)
    my_routes = routes[pl.ds(first_row, HALF_TOK), :]
    my_gates = gates[pl.ds(first_row, HALF_TOK), :]
    lane = lax.broadcasted_iota(jnp.int32, (HALF_TOK, LANE), 1)
    named = jnp.where(lane < experts, lane, lane - experts)
    weight = jnp.zeros((HALF_TOK, LANE), F32)
    for k in range(my_routes.shape[1]):
        weight = weight + jnp.where(named == my_routes[:, k:k + 1], my_gates[:, k:k + 1], 0.0)
    high = weight.astype(BF16).astype(F32)
    weight = jnp.where(lane < experts, high, jnp.where(lane < 2 * experts, weight - high, 0.0))

    tokbuf[s] = tokpad[c]
    line[...] = jnp.zeros_like(line)
    each(lambda j: token_copy(j).wait_recv())
    for i in range(n_seq):
        begin, turn = share * i // LANE * LANE, share * i % LANE
        span = tokpad.shape[2] + LANE
        value = jnp.concatenate(
            [tokbuf[i].astype(F32), jnp.zeros((HALF_TOK, LANE), F32)], axis=1
        )
        if turn:
            value = pltpu.roll(value, turn, 1)
        line[:, begin:begin + span] = line[:, begin:begin + span] + value
    xa[z, x] = line[:, 0:wide_a].astype(BF16)
    xb[z, x, :, 0:wide_b] = line[:, wide_a:wide_a + wide_b].astype(BF16)
    xb[z, x, :, wide_b:wide_b + LANE] = weight.astype(BF16)

    position = lax.broadcasted_iota(jnp.int32, (n_seq * heads, LANE), 1)

    def attend():
        yield net.now + 5.0
        loads[0].wait()
        loads[1].wait()
        each(lambda j: query_copy(j).wait_recv())
        lat_copy.wait_recv()
        qf[...] = qbuf[...].astype(F32)
        for i in range(half_req):
            q = qf[:, i * heads:(i + 1) * heads, :].reshape(n_seq * heads, qf.shape[2]).astype(BF16)
            length = lengths[0, c * half_req + i]
            parts = []
            for side, base in ((0, s), (1, 2 * y + other)):
                score = lax.dot_general(
                    q, lbuf[side, i], (((1,), (0,)), ((), ())), preferred_element_type=F32
                ) * SCALE
                valid = position + base * LANE < length
                parts.append((jnp.where(valid, score, NEG), valid))
            top = jnp.maximum(
                jnp.max(parts[0][0], axis=1, keepdims=True),
                jnp.max(parts[1][0], axis=1, keepdims=True),
            ).astype(BF16).astype(F32)
            total = jnp.zeros((n_seq * heads, 1), F32)
            context = jnp.zeros((n_seq * heads, LAT), F32)
            for side in range(2):
                score, valid = parts[side]
                w = jnp.where(valid, jnp.exp(score - top), 0.0)
                total = total + jnp.sum(w, axis=1, keepdims=True)
                context = context + lax.dot_general(
                    w.astype(BF16), lbuf[side, i, 0:LAT, :], (((1,), (1,)), ((), ())),
                    preferred_element_type=F32,
                )
            total_high = total.astype(BF16).astype(F32)
            note = jnp.where(
                position == 0,
                top,
                jnp.where(position == 1, total_high, jnp.where(position == 2, total - total_high, 0.0)),
            )
            at = pl.ds(2 * heads * i, 2 * heads)
            obuf[:, at, 0:LAT] = context.astype(BF16).reshape(n_y, 2 * heads, LAT)
            obuf[:, at, LAT:LAT + LANE] = note.astype(BF16).reshape(n_y, 2 * heads, LANE)
        came = []
        for j in range(1, n_y):
            to = lax.rem(y + j, n_y)
            came.append(net.copy(obuf.at[to], orecv.at[y], (2 * to + c, e), "y"))
        orecv[y] = obuf[y]
        yield net.now + 25.0
        for one, _ in came:
            one.wait_recv()
        row = lax.broadcasted_iota(jnp.int32, fresh.shape, 0)
        all_fresh = fresh[...].astype(F32)
        own_q = qf[pl.ds(2 * y, 2)]
        for i in range(half_req):
            at = pl.ds(2 * heads * i, 2 * heads)
            key = jnp.sum(jnp.where(row == c * half_req + i, all_fresh, 0.0), axis=0, keepdims=True)
            q = own_q[:, i * heads:(i + 1) * heads, :].reshape(2 * heads, qf.shape[2])
            own = jnp.sum(q * key, axis=1, keepdims=True) * SCALE
            notes = [orecv[j, at, LAT:LAT + LANE].astype(F32) for j in range(n_y)]
            top = own
            for note in notes:
                top = jnp.maximum(top, note[:, 0:1])
            w = jnp.exp(own - top)
            total, context = w, w * key[:, 0:LAT]
            for j, note in enumerate(notes):
                w = jnp.exp(note[:, 0:1] - top)
                total = total + w * (note[:, 1:2] + note[:, 2:3])
                context = context + w * orecv[j, at, 0:LAT].astype(F32)
            context = context / total
            for core in range(2):
                cf[core, i * heads:(i + 1) * heads, :] = context[core * heads:(core + 1) * heads]
        cb[...] = cf[...].astype(BF16)
        back, when = net.copy(cb.at[other], crecv, sibling, "core")
        ctx_out[pl.ds(pl.multiple_of(c * q_rows, q_rows), q_rows), :] = cb[c]
        yield when + 5.0
        back.wait_recv()
        ctx_out[pl.ds(pl.multiple_of(other * q_rows, q_rows), q_rows), :] = crecv[...]

    attention = attend()
    next(attention)

    half_a, half_b = wide_a // 2, wide_b // 2

    def cut_a(ref, side):
        lead = (slice(None),) * (len(ref.shape) - 1)
        return ref.at[lead + (pl.ds(side * half_a, half_a),)]

    def cut_b(ref, side):
        lead = (slice(None),) * (len(ref.shape) - 1)
        size = half_b if side == 0 else ref.shape[-1] - half_b
        return ref.at[lead + (pl.ds(side * half_b, size),)]

    def nothing(at):
        return None

    def gather_a():
        yield from ring_gather(net, lambda i: xa.at[z, i], cut_a, x, NX, at_x, "x", nothing)
        yield from ring_gather(net, lambda i: xa.at[i], cut_a, z, n_z, at_z, "z", nothing)

    def gather_b():
        got = []

        def row_of(zz):
            return ring_gather(net, lambda i: xb.at[zz, i], cut_b, x, NX, at_x, "x", nothing)

        def landed(zz):
            got.append(zz)

        inner = ring_gather(net, lambda i: xb.at[i, x], cut_b, z, n_z, at_z, "z", landed)
        waiting = []
        done = False
        inner_time = None
        while True:
            if not done and (inner_time is None or not waiting or inner_time <= waiting[0][0]):
                if inner_time is not None:
                    yield inner_time
                try:
                    inner_time = next(inner)
                except StopIteration:
                    done = True
                for zz in got:
                    task = row_of(zz)
                    heapq.heappush(waiting, (next(task), len(net.copies), task))
                got.clear()
            elif waiting:
                at, _, task = heapq.heappop(waiting)
                yield at
                try:
                    heapq.heappush(waiting, (next(task), len(net.copies), task))
                except StopIteration:
                    pass
            else:
                break

    def middle():
        yield net.now + 6.0
        next(attention)

    net.run([gather_a(), gather_b(), middle()])

    for load in loads[2:]:
        load.wait()
    wg_copy.wait_recv()
    wu_copy.wait_recv()
    wd_copy.wait_recv()
    step_a, step_b = wide_a // 3, wide_b // 4
    for k in range(3):
        cols = slice(k * step_a, (k + 1) * step_a)
        term = jnp.dot(
            xa[:, :, :, cols].reshape(rows, step_a), wcat[cols, :], preferred_element_type=F32
        )
        acc[...] = term if k == 0 else acc[...] + term
    for k in range(4):
        cols = slice(k * step_b, (k + 1) * step_b)
        down = slice(wide_a + k * step_b, wide_a + (k + 1) * step_b)
        acc[...] = acc[...] + jnp.dot(
            xb[:, :, :, cols].reshape(rows, step_b), wcat[down, :], preferred_element_type=F32
        )
    tile = xb[:, :, :, wide_b:wide_b + LANE].reshape(rows, LANE).astype(F32)
    lane = lax.broadcasted_iota(jnp.int32, (rows, LANE), 1)
    gate = jnp.sum(jnp.where((lane == e) | (lane == e + experts), tile, 0.0), axis=1, keepdims=True)
    g = acc[:, 0:2 * LANE]
    hid[...] = (g / (1.0 + jnp.exp(-g)) * acc[:, 2 * LANE:4 * LANE] * gate).astype(BF16)
    for k in range(4):
        down = slice(wide_a + k * step_b, wide_a + (k + 1) * step_b)
        term = jnp.dot(hid[...], wdcat[:, down], preferred_element_type=F32)
        yb[:, :, :, k * step_b:(k + 1) * step_b] = term.astype(BF16).reshape(n_z, NX, HALF_TOK, step_b)

    net.links, net.now = {}, 0.0
    far = n_z // 2
    ahead = [far]
    for d in range(far - 1, 0, -1):
        ahead += [d, -d]
    ahead.append(0)
    ended = set()

    def row_sum(index, d):
        zz = mod(z + d, n_z)

        def finish(total):
            yb[zz, x] = total.astype(BF16)
            ended.add(d)

        return ring_scatter(
            net,
            lambda i: yb.at[zz, i],
            cut_b,
            lambda way, k: rbx.at[index, way, k],
            x, NX, at_x, "x",
            lambda d: True,
            finish,
        )

    row_tasks = [row_sum(index, d) for index, d in enumerate(ahead)]
    started = []
    for task in row_tasks:
        started.append((next(task), task))

    def resume(at, task):
        yield at
        yield from task

    for k in range(3):
        cols = slice(k * step_a, (k + 1) * step_a)
        term = jnp.dot(hid[...], wdcat[:, cols], preferred_element_type=F32)
        ya[:, :, :, cols] = term.astype(BF16).reshape(n_z, NX, HALF_TOK, step_a)

    def sum_a():
        def keep(total):
            ya[z] = total.astype(BF16)

        yield from ring_scatter(
            net, lambda i: ya.at[i], cut_a, lambda way, k: ra.at[way, k], z, n_z, at_z, "z",
            lambda d: True, keep,
        )

        def finish(total):
            line[:, 0:wide_a] = total

        yield from ring_scatter(
            net, lambda i: ya.at[z, i], cut_a, lambda way, k: rax.at[way, k], x, NX, at_x, "x",
            lambda d: True, finish,
        )

    def sum_b():
        def finish(total):
            line[:, wide_a:wide_a + wide_b] = total

        yield from ring_scatter(
            net, lambda i: yb.at[i, x], cut_b, lambda way, k: rb.at[way, k], z, n_z, at_z, "z",
            lambda d: d in ended, finish,
        )

    def rest():
        yield net.now + 4.0
        when = next(attention)
        yield when
        for _ in attention:
            pass

    net.run([sum_a()] + [resume(at, task) for at, task in started] + [sum_b(), rest()])

    for i in range(n_seq):
        begin, turn = share * i // LANE * LANE, share * i % LANE
        span = tokpad.shape[2] + LANE
        value = line[:, begin:begin + span]
        if turn:
            value = pltpu.roll(value, span - turn, 1)
        ebuf[i] = value[:, 0:tokpad.shape[2]].astype(BF16)
    each(lambda j: end_copy(j).start())
    erecv[s] = ebuf[s]
    each(lambda j: end_copy(j).wait_recv())
    for half in range(2):
        total = erecv[half].astype(F32)
        for i in range(1, n_y):
            total = total + erecv[2 * i + half].astype(F32)
        mix_out[half * HALF_TOK:(half + 1) * HALF_TOK, :] = total[:, 0:share].astype(BF16)

    each(lambda j: token_copy(j).wait_send())
    each(lambda j: query_copy(j).wait_send())
    each(lambda j: end_copy(j).wait_send())
    for made in net.copies:
        made.wait_send()


def on_device(latent, lengths, queries, fresh_latent, tokens, routes, gates, w_gate, w_up, w_down):
    n_seq, n_ep = lax.axis_size("seq"), lax.axis_size("ep")
    n_z, n_y = n_ep // NX, n_seq // 2
    n_req, heads, width = queries.shape
    share = tokens.shape[1]
    features = share * n_seq
    wide_a = features // 7 * 3
    wide_b = features - wide_a
    padded = -(-share // LANE) * LANE
    rows = n_ep * HALF_TOK
    half_req = n_req // 2
    q_rows = half_req * heads
    far_z, far_x = n_z // 2, NX // 2
    cfg = (n_seq, n_z, wide_a, wide_b, share, heads)
    vmem = pl.BlockSpec(memory_space=pltpu.VMEM)
    hbm = pl.BlockSpec(memory_space=pl.ANY)
    dma = pltpu.SemaphoreType.DMA
    ffn = 2 * rows * features * 6 * LANE
    context, mixed = pl.pallas_call(
        functools.partial(kernel, cfg),
        out_shape=(
            jax.ShapeDtypeStruct((n_req * heads, LAT), BF16),
            jax.ShapeDtypeStruct(tokens.shape, BF16),
        ),
        in_specs=[hbm, hbm, hbm, hbm, hbm, pl.BlockSpec(memory_space=pltpu.SMEM), vmem, vmem, vmem, vmem],
        out_specs=(vmem, vmem),
        scratch_shapes=[
            pltpu.VMEM((2, HALF_TOK, padded), BF16),
            pltpu.VMEM((n_seq, HALF_TOK, padded), BF16),
            pltpu.VMEM((HALF_TOK, features + 2 * LANE), F32),
            pltpu.VMEM((n_z, NX, HALF_TOK, wide_a), BF16),
            pltpu.VMEM((n_z, NX, HALF_TOK, wide_b + LANE), BF16),
            pltpu.VMEM((features, 4 * LANE), BF16),
            pltpu.VMEM((2 * LANE, features), BF16),
            pltpu.VMEM((rows, 4 * LANE), F32),
            pltpu.VMEM((rows, 2 * LANE), BF16),
            pltpu.VMEM((n_z, NX, HALF_TOK, wide_a), BF16),
            pltpu.VMEM((n_z, NX, HALF_TOK, wide_b), BF16),
            pltpu.VMEM((2, far_z, NX, HALF_TOK, wide_a), BF16),
            pltpu.VMEM((2, far_x, HALF_TOK, wide_a), BF16),
            pltpu.VMEM((n_z, 2, far_x, HALF_TOK, wide_b), BF16),
            pltpu.VMEM((2, far_z, HALF_TOK, wide_b), BF16),
            pltpu.VMEM((n_seq, HALF_TOK, padded), BF16),
            pltpu.VMEM((n_seq, HALF_TOK, padded), BF16),
            pltpu.VMEM((2, half_req, width, LANE), BF16),
            pltpu.VMEM((n_seq, q_rows, width), BF16),
            pltpu.VMEM((n_seq, q_rows, width), F32),
            pltpu.VMEM((n_y, 2 * q_rows, LAT + LANE), BF16),
            pltpu.VMEM((n_y, 2 * q_rows, LAT + LANE), BF16),
            pltpu.VMEM((2, q_rows, LAT), F32),
            pltpu.VMEM((2, q_rows, LAT), BF16),
            pltpu.VMEM((q_rows, LAT), BF16),
            dma((5,)),
            dma((140,)),
            dma((140,)),
            dma((n_seq,)),
            dma((n_seq,)),
            dma((n_seq,)),
            dma((n_seq,)),
            dma((n_seq,)),
            dma((n_seq,)),
        ],
        compiler_params=pltpu.CompilerParams(
            collective_id=0, has_side_effects=True, vmem_limit_bytes=56 * 1024 * 1024
        ),
        cost_estimate=pl.CostEstimate(flops=ffn, bytes_accessed=6 * 2**20, transcendentals=rows * 512),
    )(
        latent.transpose(0, 2, 1),
        queries.reshape(n_req * heads, width),
        w_gate[0],
        w_up[0],
        w_down[0],
        lengths,
        fresh_latent,
        tokens,
        routes,
        gates,
    )
    return context.reshape(n_req, heads, LAT), mixed


def solution(mesh):
    placed = (
        P("ep", "seq", None),
        P("ep", None),
        P("ep", "seq", None),
        P("ep", None),
        P("ep", "seq"),
        P("ep", None),
        P("ep", None),
        P("ep", None, "seq"),
        P("ep", None, "seq"),
        P("ep", "seq", None),
    )
    return jax.shard_map(
        on_device,
        mesh=mesh,
        in_specs=placed,
        out_specs=(P("ep", "seq", None), P("ep", "seq")),
        check_vma=False,
    )
```

```python
import functools
import heapq

import jax
import jax.numpy as jnp
from jax import lax
from jax.experimental import pallas as pl
from jax.experimental.pallas import tpu as pltpu
from jax.sharding import PartitionSpec as P

MESH = pl.DeviceIdType.MESH
LAT = 512
NX = 4
LANE = 128
HALF_TOK = 16
SCALE = 0.07216878364870322
NEG = -1.0e30
F32 = jnp.float32
BF16 = jnp.bfloat16

LINK_RATE = 45.0e3
HOP = 1.5


def mod(value, n):
    return lax.rem(value + n, n)


class Net:
    def __init__(self, send, recv):
        self.send, self.recv = send, recv
        self.count, self.now = 0, 0.0
        self.links, self.copies = {}, []

    def copy(self, src, dst, device, link):
        at = self.count
        self.count += 1
        made = pltpu.make_async_remote_copy(
            src_ref=src,
            dst_ref=dst,
            send_sem=self.send.at[at],
            recv_sem=self.recv.at[at],
            device_id=device,
            device_id_type=MESH,
        )
        made.start()
        size = 2
        for extent in src.shape:
            size *= extent
        begin = max(self.links.get(link, 0.0), self.now)
        self.links[link] = begin + size / LINK_RATE
        self.copies.append(made)
        return made, self.links[link] + HOP

    def run(self, tasks):
        self.heap, self.order = [], 0
        for task in tasks:
            self.add(self.now, task)
        while self.heap:
            at, _, task = heapq.heappop(self.heap)
            self.now = max(self.now, at)
            try:
                ready = next(task)
            except StopIteration:
                continue
            self.add(ready, task)

    def add(self, at, task):
        self.order += 1
        heapq.heappush(self.heap, (at, self.order, task))


def around(n):
    offsets = [0]
    for k in range(1, n // 2):
        offsets += [k, -k]
    return offsets + [n // 2]


def ring_gather(net, piece, cut, n, up, down, axis, landed):
    far = n // 2

    def pass_on(side, k):
        src, dst = piece((k, -k)[1 - side]), piece(far if k + 1 == far else (k + 1, -k - 1)[1 - side])
        if k + 1 == far:
            src, dst = cut(src, side), cut(dst, side)
        return net.copy(src, dst, (up, down)[side], axis + "+-"[side])

    cu, tu = pass_on(0, 0)
    cd, td = pass_on(1, 0)
    landed(0)
    for k in range(1, far):
        yield tu
        cu.wait_recv()
        cu, tu = pass_on(0, k)
        landed(-k)
        yield td
        cd.wait_recv()
        cd, td = pass_on(1, k)
        landed(k)
    yield max(tu, td)
    cu.wait_recv()
    cd.wait_recv()
    landed(far)


def add_into(ref, other):
    ref[...] = ref[...] + other[...]


def ring_scatter(net, piece, cut, arrived, n, up, down, axis, ready, finish):
    far = n // 2
    while not ready(far):
        yield net.now + 0.01
    cu, tu = net.copy(cut(piece(far), 0), cut(arrived(0, 0), 0), up, axis + "+")
    cd, td = net.copy(cut(piece(far), 1), cut(arrived(1, 0), 1), down, axis + "-")
    for k in range(1, far):
        d = far - k
        while not (ready(d) and ready(-d)):
            yield net.now + 0.01
        yield tu
        cu.wait_recv()
        mine, came = piece(d), arrived(0, k - 1)
        if k == 1:
            mine, came = cut(mine, 0), cut(came, 0)
        add_into(mine, came)
        cu, tu = net.copy(piece(d), arrived(0, k), up, axis + "+")
        yield td
        cd.wait_recv()
        mine, came = piece(-d), arrived(1, k - 1)
        if k == 1:
            mine, came = cut(mine, 1), cut(came, 1)
        add_into(mine, came)
        cd, td = net.copy(piece(-d), arrived(1, k), down, axis + "-")
    while not ready(0):
        yield net.now + 0.01
    yield max(tu, td)
    cu.wait_recv()
    cd.wait_recv()
    if far == 1:
        add_into(cut(piece(0), 0), cut(arrived(0, 0), 0))
        add_into(cut(piece(0), 1), cut(arrived(1, 0), 1))
        finish(piece(0)[...].astype(F32))
    else:
        finish(
            piece(0)[...].astype(F32)
            + arrived(0, far - 1)[...].astype(F32)
            + arrived(1, far - 1)[...].astype(F32)
        )


def kernel(
    cfg,
    latent, queries, wg, wu, wd, lengths, fresh, tokens, routes, gates,
    ctx_out, mix_out,
    tokpad, tokbuf, line, square, xa, xb, wcat, wdcat, acc, hid, ya, yb,
    ra, rax, rbx, rb, ebuf, erecv,
    lbuf, qbuf, qf, obuf, orecv, cf, cb, crecv,
    local_sem, send_sem, recv_sem, t_send, t_recv, q_send, q_recv, e_send, e_recv,
):
    n_seq, n_z, wide_a, wide_b, share, heads = cfg
    n_y = n_seq // 2
    s, e = lax.axis_index("seq"), lax.axis_index("ep")
    y, c = s // 2, lax.rem(s, 2)
    z, x = e // NX, lax.rem(e, NX)
    other = 1 - c
    sibling = (2 * y + other, e)
    experts = n_z * NX
    n_req = lengths.shape[1]
    half_req = n_req // 2
    q_rows = half_req * heads
    x_up, x_down = (s, z * NX + mod(x + 1, NX)), (s, z * NX + mod(x - 1, NX))
    z_up, z_down = (s, mod(z + 1, n_z) * NX + x), (s, mod(z - 1, n_z) * NX + x)
    slot_z = {d: i for i, d in enumerate(around(n_z))}
    slot_x = {d: i for i, d in enumerate(around(NX))}

    def local(src, dst, i):
        made = pltpu.make_async_copy(src, dst, local_sem.at[i])
        made.start()
        return made

    for half in range(2):
        tokpad[half] = jnp.zeros_like(tokpad[half])
        tokpad[half, :, 0:share] = tokens[half * HALF_TOK:(half + 1) * HALF_TOK, :]

    barrier = pltpu.get_barrier_semaphore()

    def greet(j, carry):
        pl.semaphore_signal(
            barrier, inc=1, device_id=(lax.rem(s + j, n_seq), e), device_id_type=MESH
        )
        return carry

    lax.fori_loop(1, n_seq, greet, 0)
    for who in (x_up, x_down, z_up, z_down):
        pl.semaphore_signal(barrier, inc=1, device_id=who, device_id_type=MESH)

    mine_q = queries.at[pl.ds(pl.multiple_of(c * q_rows, q_rows), q_rows)]
    loads = [
        local(mine_q, qbuf.at[s], 0),
        local(latent.at[pl.ds(c * half_req, half_req)], lbuf.at[0], 1),
        local(wg, wcat.at[:, pl.ds(0, LANE)], 2),
        local(wu, wcat.at[:, pl.ds(2 * LANE, LANE)], 3),
        local(wd, wdcat.at[pl.ds(0, LANE)], 4),
    ]

    row = lax.broadcasted_iota(jnp.int32, (LANE, routes.shape[1]), 0)
    named = jnp.where(row < experts, row, row - experts)
    weight = jnp.zeros(named.shape, F32)
    for k in range(routes.shape[0]):
        weight = weight + jnp.where(named == routes[k:k + 1, :], gates[k:k + 1, :], 0.0)
    high = weight.astype(BF16).astype(F32)
    weight = jnp.where(row < experts, high, jnp.where(row < 2 * experts, weight - high, 0.0))
    square[...] = jnp.zeros_like(square)
    square[:, 0:routes.shape[1]] = weight
    square[...] = jnp.transpose(square[...])

    pl.semaphore_wait(barrier, n_seq - 1 + 4)

    def token_copy(j):
        to = lax.rem(s + j, n_seq)
        return pltpu.make_async_remote_copy(
            src_ref=tokpad.at[lax.rem(to, 2)],
            dst_ref=tokbuf.at[s],
            send_sem=t_send.at[j],
            recv_sem=t_recv.at[j],
            device_id=(to, e),
            device_id_type=MESH,
        )

    def query_copy(j):
        to = lax.rem(s + j, n_seq)
        begin = pl.multiple_of(lax.rem(to, 2) * q_rows, q_rows)
        return pltpu.make_async_remote_copy(
            src_ref=queries.at[pl.ds(begin, q_rows)],
            dst_ref=qbuf.at[s],
            send_sem=q_send.at[j],
            recv_sem=q_recv.at[j],
            device_id=(to, e),
            device_id_type=MESH,
        )

    def end_copy(j):
        to = lax.rem(s + j, n_seq)
        return pltpu.make_async_remote_copy(
            src_ref=ebuf.at[to],
            dst_ref=erecv.at[s],
            send_sem=e_send.at[j],
            recv_sem=e_recv.at[j],
            device_id=(to, e),
            device_id_type=MESH,
        )

    def each(act):
        def body(j, carry):
            act(j)
            return carry

        lax.fori_loop(1, n_seq, body, 0)

    net = Net(send_sem, recv_sem)
    each(lambda j: token_copy(j).start())
    each(lambda j: query_copy(j).start())
    lat_copy, _ = net.copy(latent.at[pl.ds(other * half_req, half_req)], lbuf.at[1], sibling, "core")

    tokbuf[s] = tokpad[c]
    line[...] = jnp.zeros_like(line)
    first_row = pl.multiple_of(c * HALF_TOK, HALF_TOK)
    xb[0, 0, :, wide_b:wide_b + LANE] = square[pl.ds(first_row, HALF_TOK), :].astype(BF16)
    each(lambda j: token_copy(j).wait_recv())
    for i in range(n_seq):
        begin, turn = share * i // LANE * LANE, share * i % LANE
        span = tokpad.shape[2] + LANE
        value = jnp.concatenate(
            [tokbuf[i].astype(F32), jnp.zeros((HALF_TOK, LANE), F32)], axis=1
        )
        if turn:
            value = pltpu.roll(value, turn, 1)
        line[:, begin:begin + span] = line[:, begin:begin + span] + value
    xa[0, 0] = line[:, 0:wide_a].astype(BF16)
    xb[0, 0, :, 0:wide_b] = line[:, wide_a:wide_a + wide_b].astype(BF16)

    position = lax.broadcasted_iota(jnp.int32, (n_seq * heads, LANE), 1)

    def one_request(i, carry):
        head_rows = pl.ds(pl.multiple_of(i * heads, heads), heads)
        q = qf[:, head_rows, :].reshape(n_seq * heads, qf.shape[2]).astype(BF16)
        length = lengths[0, c * half_req + i]
        parts = []
        for side, base in ((0, s), (1, 2 * y + other)):
            score = jnp.dot(q, lbuf[side, i], preferred_element_type=F32) * SCALE
            valid = position + base * LANE < length
            parts.append((jnp.where(valid, score, NEG), valid))
        top = jnp.maximum(
            jnp.max(parts[0][0], axis=1, keepdims=True),
            jnp.max(parts[1][0], axis=1, keepdims=True),
        ).astype(BF16).astype(F32)
        total = jnp.zeros((n_seq * heads, 1), F32)
        context = jnp.zeros((n_seq * heads, LAT), F32)
        for side in range(2):
            score, valid = parts[side]
            w = jnp.where(valid, jnp.exp(score - top), 0.0)
            total = total + jnp.sum(w, axis=1, keepdims=True)
            context = context + lax.dot_general(
                w.astype(BF16), lbuf[side, i, 0:LAT, :], (((1,), (1,)), ((), ())),
                preferred_element_type=F32,
            )
        total_high = total.astype(BF16).astype(F32)
        note = jnp.where(
            position == 0,
            top,
            jnp.where(position == 1, total_high, jnp.where(position == 2, total - total_high, 0.0)),
        )
        at = pl.ds(pl.multiple_of(2 * heads * i, 2 * heads), 2 * heads)
        obuf[:, at, 0:LAT] = context.astype(BF16).reshape(n_y, 2 * heads, LAT)
        obuf[:, at, LAT:LAT + LANE] = note.astype(BF16).reshape(n_y, 2 * heads, LANE)
        return carry

    def one_context(i, carry):
        at = pl.ds(pl.multiple_of(2 * heads * i, 2 * heads), 2 * heads)
        head_rows = pl.ds(pl.multiple_of(i * heads, heads), heads)
        line_of = lax.broadcasted_iota(jnp.int32, fresh.shape, 0)
        chosen = jnp.where(line_of == c * half_req + i, fresh[...].astype(F32), 0.0)
        key = jnp.sum(chosen, axis=0, keepdims=True)
        q = qf[pl.ds(2 * y, 2), head_rows, :].reshape(2 * heads, qf.shape[2])
        own = jnp.sum(q * key, axis=1, keepdims=True) * SCALE
        notes = [orecv[j, at, LAT:LAT + LANE].astype(F32) for j in range(n_y)]
        top = own
        for note in notes:
            top = jnp.maximum(top, note[:, 0:1])
        w = jnp.exp(own - top)
        total, context = w, w * key[:, 0:LAT]
        for j, note in enumerate(notes):
            w = jnp.exp(note[:, 0:1] - top)
            total = total + w * (note[:, 1:2] + note[:, 2:3])
            context = context + w * orecv[j, at, 0:LAT].astype(F32)
        context = context / total
        for core in range(2):
            cf[core, head_rows, :] = context[core * heads:(core + 1) * heads]
        return carry

    def attend():
        yield net.now + 8.0
        loads[0].wait()
        loads[1].wait()
        each(lambda j: query_copy(j).wait_recv())
        lat_copy.wait_recv()
        qf[...] = qbuf[...].astype(F32)
        lax.fori_loop(0, half_req // 2, one_request, 0)
        net.now += 2.0
        yield net.now + 0.5
        lax.fori_loop(half_req // 2, half_req, one_request, 0)
        net.now += 2.0
        came = []
        for j in range(1, n_y):
            to = lax.rem(y + j, n_y)
            came.append(net.copy(obuf.at[to], orecv.at[y], (2 * to + c, e), "y"))
        orecv[y] = obuf[y]
        yield net.now + 25.0
        for one, _ in came:
            one.wait_recv()
        lax.fori_loop(0, half_req, one_context, 0)
        net.now += 1.0
        cb[...] = cf[...].astype(BF16)
        back, when = net.copy(cb.at[other], crecv, sibling, "core")
        ctx_out[pl.ds(pl.multiple_of(c * q_rows, q_rows), q_rows), :] = cb[c]
        yield when + 5.0
        back.wait_recv()
        ctx_out[pl.ds(pl.multiple_of(other * q_rows, q_rows), q_rows), :] = crecv[...]

    half_a, half_b = wide_a // 2, wide_b // 2

    def cut_a(ref, side):
        return ref.at[:, pl.ds(side * half_a, half_a)]

    def cut_b(ref, side):
        return ref.at[:, pl.ds(side * half_b, half_b if side == 0 else ref.shape[-1] - half_b)]

    landed = {d: 0 for d in slot_z}

    def count(d):
        landed[d] += 1

    def gather_a():
        def start(dx):
            at = slot_x[dx]
            net.add(net.now, ring_gather(
                net, lambda d: xa.at[slot_z[d], at], cut_a, n_z, z_up, z_down, "z", count
            ))

        yield from ring_gather(
            net, lambda d: xa.at[0, slot_x[d]], cut_a, NX, x_up, x_down, "x", start
        )

    def gather_b():
        def start(dz):
            at = slot_z[dz]
            net.add(net.now, ring_gather(
                net, lambda d: xb.at[at, slot_x[d]], cut_b, NX, x_up, x_down, "x", lambda d: count(dz)
            ))

        yield from ring_gather(
            net, lambda d: xb.at[slot_z[d], 0], cut_b, n_z, z_up, z_down, "z", start
        )

    step_a, step_b = wide_a // 3, wide_b // 4
    weights = []

    def load_weights():
        yield net.now + 0.5
        for src, dst in (
            (wg, wcat.at[:, pl.ds(LANE, LANE)]),
            (wu, wcat.at[:, pl.ds(3 * LANE, LANE)]),
            (wd, wdcat.at[pl.ds(LANE, LANE)]),
        ):
            weights.append(net.copy(src, dst, sibling, "core")[0])

    def experts_of(first, last):
        rows = (last - first) * NX * HALF_TOK

        def up_a(k, carry):
            cols = pl.ds(pl.multiple_of(k * step_a, step_a), step_a)
            value = xa[first:last, :, :, cols].reshape(rows, step_a)
            acc[0:rows, :] += jnp.dot(value, wcat[cols, :], preferred_element_type=F32)
            return carry

        def up_b(k, carry):
            cols = pl.ds(pl.multiple_of(k * step_b, step_b), step_b)
            down = pl.ds(pl.multiple_of(wide_a + k * step_b, step_b), step_b)
            value = xb[first:last, :, :, cols].reshape(rows, step_b)
            acc[0:rows, :] += jnp.dot(value, wcat[down, :], preferred_element_type=F32)
            return carry

        def down_a(k, carry):
            cols = pl.ds(pl.multiple_of(k * step_a, step_a), step_a)
            value = jnp.dot(hid[0:rows, :], wdcat[:, cols], preferred_element_type=F32)
            ya[first:last, :, :, cols] = value.astype(BF16).reshape(last - first, NX, HALF_TOK, step_a)
            return carry

        def down_b(k, carry):
            cols = pl.ds(pl.multiple_of(k * step_b, step_b), step_b)
            down = pl.ds(pl.multiple_of(wide_a + k * step_b, step_b), step_b)
            value = jnp.dot(hid[0:rows, :], wdcat[:, down], preferred_element_type=F32)
            yb[first:last, :, :, cols] = value.astype(BF16).reshape(last - first, NX, HALF_TOK, step_b)
            return carry

        acc[0:rows, :] = jnp.zeros((rows, 4 * LANE), F32)
        lax.fori_loop(0, 3, up_a, 0)
        lax.fori_loop(0, 4, up_b, 0)
        tile = xb[first:last, :, :, wide_b:wide_b + LANE].reshape(rows, LANE).astype(F32)
        lane = lax.broadcasted_iota(jnp.int32, (rows, LANE), 1)
        gate = jnp.sum(
            jnp.where((lane == e) | (lane == e + experts), tile, 0.0), axis=1, keepdims=True
        )
        g = acc[0:rows, 0:2 * LANE]
        value = g / (1.0 + jnp.exp(-g)) * acc[0:rows, 2 * LANE:4 * LANE] * gate
        hid[0:rows, :] = value.astype(BF16)
        lax.fori_loop(0, 4, down_b, 0)
        lax.fori_loop(0, 3, down_a, 0)

    def compute():
        offsets = around(n_z)
        groups = [(0, 3), (3, 5), (5, 7), (7, 8)] if n_z == 8 else [(0, len(offsets))]
        for first, last in groups:
            while any(landed[d] < 2 * NX for d in offsets[first:last]):
                yield net.now + 0.01
            if first == 0:
                for load in loads[2:]:
                    load.wait()
                for made in weights:
                    made.wait_recv()
            experts_of(first, last)
            net.now += 1.0

    attention = attend()
    net.run([gather_a(), gather_b(), load_weights(), sample(attention, 3), compute()])

    net.links, net.now = {}, 0.0
    ended = set()

    def always(d):
        return True

    def row_sum(dz):
        at = slot_z[dz]

        def finish(total):
            yb[at, 0] = total.astype(BF16)
            ended.add(dz)

        return ring_scatter(
            net, lambda d: yb.at[at, slot_x[d]], cut_b, lambda way, k: rbx.at[at, way, k],
            NX, x_up, x_down, "x", always, finish,
        )

    done_a = set()

    def column_sum(dx):
        at = slot_x[dx]

        def finish(total):
            ya[0, at] = total.astype(BF16)
            done_a.add(dx)

        return ring_scatter(
            net, lambda d: ya.at[slot_z[d], at], cut_a, lambda way, k: ra.at[at, way, k],
            n_z, z_up, z_down, "z", always, finish,
        )

    def end_a(total):
        line[:, 0:wide_a] = total

    def end_b(total):
        line[:, wide_a:wide_a + wide_b] = total

    sum_a = ring_scatter(
        net, lambda d: ya.at[0, slot_x[d]], cut_a, lambda way, k: rax.at[way, k],
        NX, x_up, x_down, "x", lambda d: d in done_a, end_a,
    )
    sum_b = ring_scatter(
        net, lambda d: yb.at[slot_z[d], 0], cut_b, lambda way, k: rb.at[way, k],
        n_z, z_up, z_down, "z", lambda d: d in ended, end_b,
    )
    rows_first = [row_sum(d) for d in reversed(around(n_z))]
    columns_first = [column_sum(d) for d in reversed(around(NX))]
    mixed = []
    while rows_first or columns_first:
        if rows_first:
            mixed.append(rows_first.pop(0))
        if columns_first:
            mixed.append(columns_first.pop(0))
    net.run(mixed + [sum_a, sum_b, sample(attention, 9)])

    for i in range(n_seq):
        begin, turn = share * i // LANE * LANE, share * i % LANE
        span = tokpad.shape[2] + LANE
        value = line[:, begin:begin + span]
        if turn:
            value = pltpu.roll(value, span - turn, 1)
        ebuf[i] = value[:, 0:tokpad.shape[2]].astype(BF16)
    each(lambda j: end_copy(j).start())
    erecv[s] = ebuf[s]
    each(lambda j: end_copy(j).wait_recv())
    for half in range(2):
        total = erecv[half].astype(F32)
        for i in range(1, n_y):
            total = total + erecv[2 * i + half].astype(F32)
        mix_out[half * HALF_TOK:(half + 1) * HALF_TOK, :] = total[:, 0:share].astype(BF16)

    each(lambda j: token_copy(j).wait_send())
    each(lambda j: query_copy(j).wait_send())
    each(lambda j: end_copy(j).wait_send())
    for made in net.copies:
        made.wait_send()


def sample(task, most):
    for _ in range(most):
        try:
            ready = next(task)
        except StopIteration:
            return
        yield ready


def on_device(latent, lengths, queries, fresh_latent, tokens, routes, gates, w_gate, w_up, w_down):
    n_seq, n_ep = lax.axis_size("seq"), lax.axis_size("ep")
    n_z, n_y = n_ep // NX, n_seq // 2
    n_req, heads, width = queries.shape
    share = tokens.shape[1]
    features = share * n_seq
    wide_a = features // 7 * 3
    wide_b = features - wide_a
    padded = -(-share // LANE) * LANE
    rows = n_ep * HALF_TOK
    half_req = n_req // 2
    q_rows = half_req * heads
    far_z, far_x = n_z // 2, NX // 2
    cfg = (n_seq, n_z, wide_a, wide_b, share, heads)
    vmem = pl.BlockSpec(memory_space=pltpu.VMEM)
    hbm = pl.BlockSpec(memory_space=pl.ANY)
    dma = pltpu.SemaphoreType.DMA
    ffn = 2 * rows * features * 6 * LANE
    context, mixed = pl.pallas_call(
        functools.partial(kernel, cfg),
        out_shape=(
            jax.ShapeDtypeStruct((n_req * heads, LAT), BF16),
            jax.ShapeDtypeStruct(tokens.shape, BF16),
        ),
        in_specs=[hbm, hbm, hbm, hbm, hbm, pl.BlockSpec(memory_space=pltpu.SMEM), vmem, vmem, vmem, vmem],
        out_specs=(vmem, vmem),
        scratch_shapes=[
            pltpu.VMEM((2, HALF_TOK, padded), BF16),
            pltpu.VMEM((n_seq, HALF_TOK, padded), BF16),
            pltpu.VMEM((HALF_TOK, features + 2 * LANE), F32),
            pltpu.VMEM((LANE, LANE), F32),
            pltpu.VMEM((n_z, NX, HALF_TOK, wide_a), BF16),
            pltpu.VMEM((n_z, NX, HALF_TOK, wide_b + LANE), BF16),
            pltpu.VMEM((features, 4 * LANE), BF16),
            pltpu.VMEM((2 * LANE, features), BF16),
            pltpu.VMEM((rows, 4 * LANE), F32),
            pltpu.VMEM((rows, 2 * LANE), BF16),
            pltpu.VMEM((n_z, NX, HALF_TOK, wide_a), BF16),
            pltpu.VMEM((n_z, NX, HALF_TOK, wide_b), BF16),
            pltpu.VMEM((NX, 2, far_z, HALF_TOK, wide_a), BF16),
            pltpu.VMEM((2, far_x, HALF_TOK, wide_a), BF16),
            pltpu.VMEM((n_z, 2, far_x, HALF_TOK, wide_b), BF16),
            pltpu.VMEM((2, far_z, HALF_TOK, wide_b), BF16),
            pltpu.VMEM((n_seq, HALF_TOK, padded), BF16),
            pltpu.VMEM((n_seq, HALF_TOK, padded), BF16),
            pltpu.VMEM((2, half_req, width, LANE), BF16),
            pltpu.VMEM((n_seq, q_rows, width), BF16),
            pltpu.VMEM((n_seq, q_rows, width), F32),
            pltpu.VMEM((n_y, 2 * q_rows, LAT + LANE), BF16),
            pltpu.VMEM((n_y, 2 * q_rows, LAT + LANE), BF16),
            pltpu.VMEM((2, q_rows, LAT), F32),
            pltpu.VMEM((2, q_rows, LAT), BF16),
            pltpu.VMEM((q_rows, LAT), BF16),
            dma((5,)),
            dma((200,)),
            dma((200,)),
            dma((n_seq,)),
            dma((n_seq,)),
            dma((n_seq,)),
            dma((n_seq,)),
            dma((n_seq,)),
            dma((n_seq,)),
        ],
        compiler_params=pltpu.CompilerParams(
            collective_id=0, has_side_effects=True, vmem_limit_bytes=56 * 1024 * 1024
        ),
        cost_estimate=pl.CostEstimate(flops=ffn, bytes_accessed=6 * 2**20, transcendentals=rows * 512),
    )(
        latent.transpose(0, 2, 1),
        queries.reshape(n_req * heads, width),
        w_gate[0],
        w_up[0],
        w_down[0],
        lengths,
        fresh_latent,
        tokens,
        routes.T,
        gates.T,
    )
    return context.reshape(n_req, heads, LAT), mixed


def solution(mesh):
    placed = (
        P("ep", "seq", None),
        P("ep", None),
        P("ep", "seq", None),
        P("ep", None),
        P("ep", "seq"),
        P("ep", None),
        P("ep", None),
        P("ep", None, "seq"),
        P("ep", None, "seq"),
        P("ep", "seq", None),
    )
    return jax.shard_map(
        on_device,
        mesh=mesh,
        in_specs=placed,
        out_specs=(P("ep", "seq", None), P("ep", "seq")),
        check_vma=False,
    )
```

```python
import functools
import heapq

import jax
import jax.numpy as jnp
from jax import lax
from jax.experimental import pallas as pl
from jax.experimental.pallas import tpu as pltpu
from jax.sharding import PartitionSpec as P

MESH = pl.DeviceIdType.MESH
LAT = 512
NX = 4
LANE = 128
HALF_TOK = 16
SCALE = 0.07216878364870322
NEG = -1.0e30
F32 = jnp.float32
BF16 = jnp.bfloat16

LINK_RATE = 45.0e3
HOP = 1.5


def mod(value, n):
    return lax.rem(value + n, n)


class Net:
    def __init__(self, send, recv):
        self.send, self.recv = send, recv
        self.count, self.now = 0, 0.0
        self.links, self.copies = {}, []

    def copy(self, src, dst, device, link):
        at = self.count
        self.count += 1
        made = pltpu.make_async_remote_copy(
            src_ref=src,
            dst_ref=dst,
            send_sem=self.send.at[at],
            recv_sem=self.recv.at[at],
            device_id=device,
            device_id_type=MESH,
        )
        made.start()
        size = 2
        for extent in src.shape:
            size *= extent
        begin = max(self.links.get(link, 0.0), self.now)
        self.links[link] = begin + size / LINK_RATE
        self.copies.append(made)
        return made, self.links[link] + HOP

    def run(self, tasks):
        self.heap, self.order = [], 0
        for task in tasks:
            self.add(self.now, task)
        while self.heap:
            at, _, task = heapq.heappop(self.heap)
            self.now = max(self.now, at)
            try:
                ready = next(task)
            except StopIteration:
                continue
            self.add(ready, task)

    def add(self, at, task):
        self.order += 1
        heapq.heappush(self.heap, (at, self.order, task))


def around(n):
    offsets = [0]
    for k in range(1, n // 2):
        offsets += [k, -k]
    return offsets + [n // 2]


def ring_gather(net, piece, cut, n, up, down, axis, landed):
    far = n // 2

    def pass_on(side, k):
        src, dst = piece((k, -k)[1 - side]), piece(far if k + 1 == far else (k + 1, -k - 1)[1 - side])
        if k + 1 == far:
            src, dst = cut(src, side), cut(dst, side)
        return net.copy(src, dst, (up, down)[side], axis + "+-"[side])

    cu, tu = pass_on(0, 0)
    cd, td = pass_on(1, 0)
    landed(0)
    for k in range(1, far):
        yield tu
        cu.wait_recv()
        cu, tu = pass_on(0, k)
        landed(-k)
        yield td
        cd.wait_recv()
        cd, td = pass_on(1, k)
        landed(k)
    yield max(tu, td)
    cu.wait_recv()
    cd.wait_recv()
    landed(far)


def add_into(ref, other):
    ref[...] = ref[...] + other[...]


def ring_scatter(net, piece, cut, arrived, n, up, down, axis, ready, finish):
    far = n // 2
    while not ready(far):
        yield net.now + 0.01
    cu, tu = net.copy(cut(piece(far), 0), cut(arrived(0, 0), 0), up, axis + "+")
    cd, td = net.copy(cut(piece(far), 1), cut(arrived(1, 0), 1), down, axis + "-")
    for k in range(1, far):
        d = far - k
        while not (ready(d) and ready(-d)):
            yield net.now + 0.01
        yield tu
        cu.wait_recv()
        mine, came = piece(d), arrived(0, k - 1)
        if k == 1:
            mine, came = cut(mine, 0), cut(came, 0)
        add_into(mine, came)
        cu, tu = net.copy(piece(d), arrived(0, k), up, axis + "+")
        yield td
        cd.wait_recv()
        mine, came = piece(-d), arrived(1, k - 1)
        if k == 1:
            mine, came = cut(mine, 1), cut(came, 1)
        add_into(mine, came)
        cd, td = net.copy(piece(-d), arrived(1, k), down, axis + "-")
    while not ready(0):
        yield net.now + 0.01
    yield max(tu, td)
    cu.wait_recv()
    cd.wait_recv()
    if far == 1:
        add_into(cut(piece(0), 0), cut(arrived(0, 0), 0))
        add_into(cut(piece(0), 1), cut(arrived(1, 0), 1))
        finish(piece(0)[...].astype(F32))
    else:
        finish(
            piece(0)[...].astype(F32)
            + arrived(0, far - 1)[...].astype(F32)
            + arrived(1, far - 1)[...].astype(F32)
        )


def kernel(
    cfg,
    latent, queries, wg, wu, wd, lengths, fresh, tokens, routes, gates,
    ctx_out, mix_out,
    tokpad, tokbuf, line, square, xa, xb, wcat, wdcat, acc, hid, ya, yb,
    ra, rax, rbx, rb, ebuf, erecv,
    lbuf, qbuf, qf, obuf, orecv, cf, cb, crecv,
    local_sem, send_sem, recv_sem, t_send, t_recv, q_send, q_recv, e_send, e_recv,
):
    n_seq, n_z, wide_a, wide_b, share, heads = cfg
    n_y = n_seq // 2
    s, e = lax.axis_index("seq"), lax.axis_index("ep")
    y, c = s // 2, lax.rem(s, 2)
    z, x = e // NX, lax.rem(e, NX)
    other = 1 - c
    sibling = (2 * y + other, e)
    experts = n_z * NX
    n_req = lengths.shape[1]
    half_req = n_req // 2
    q_rows = half_req * heads
    x_up, x_down = (s, z * NX + mod(x + 1, NX)), (s, z * NX + mod(x - 1, NX))
    z_up, z_down = (s, mod(z + 1, n_z) * NX + x), (s, mod(z - 1, n_z) * NX + x)
    slot_z = {d: i for i, d in enumerate(around(n_z))}
    slot_x = {d: i for i, d in enumerate(around(NX))}

    def local(src, dst, i):
        made = pltpu.make_async_copy(src, dst, local_sem.at[i])
        made.start()
        return made

    for half in range(2):
        tokpad[half] = jnp.zeros_like(tokpad[half])
        tokpad[half, :, 0:share] = tokens[half * HALF_TOK:(half + 1) * HALF_TOK, :]

    barrier = pltpu.get_barrier_semaphore()

    def greet(j, carry):
        pl.semaphore_signal(
            barrier, inc=1, device_id=(lax.rem(s + j, n_seq), e), device_id_type=MESH
        )
        return carry

    lax.fori_loop(1, n_seq, greet, 0)
    for who in (x_up, x_down, z_up, z_down):
        pl.semaphore_signal(barrier, inc=1, device_id=who, device_id_type=MESH)

    mine_q = queries.at[pl.ds(pl.multiple_of(c * q_rows, q_rows), q_rows)]
    loads = [
        local(mine_q, qbuf.at[s], 0),
        local(latent.at[pl.ds(c * half_req, half_req)], lbuf.at[0], 1),
        local(wg, wcat.at[:, pl.ds(0, LANE)], 2),
        local(wu, wcat.at[:, pl.ds(2 * LANE, LANE)], 3),
        local(wd, wdcat.at[pl.ds(0, LANE)], 4),
    ]

    row = lax.broadcasted_iota(jnp.int32, (LANE, routes.shape[1]), 0)
    named = jnp.where(row < experts, row, row - experts)
    weight = jnp.zeros(named.shape, F32)
    for k in range(routes.shape[0]):
        weight = weight + jnp.where(named == routes[k:k + 1, :], gates[k:k + 1, :], 0.0)
    high = weight.astype(BF16).astype(F32)
    weight = jnp.where(row < experts, high, jnp.where(row < 2 * experts, weight - high, 0.0))
    square[...] = jnp.zeros_like(square)
    square[:, 0:routes.shape[1]] = weight
    square[...] = jnp.transpose(square[...])

    pl.semaphore_wait(barrier, n_seq - 1 + 4)

    def token_copy(j):
        to = lax.rem(s + j, n_seq)
        return pltpu.make_async_remote_copy(
            src_ref=tokpad.at[lax.rem(to, 2)],
            dst_ref=tokbuf.at[s],
            send_sem=t_send.at[j],
            recv_sem=t_recv.at[j],
            device_id=(to, e),
            device_id_type=MESH,
        )

    def query_copy(j):
        to = lax.rem(s + j, n_seq)
        begin = pl.multiple_of(lax.rem(to, 2) * q_rows, q_rows)
        return pltpu.make_async_remote_copy(
            src_ref=queries.at[pl.ds(begin, q_rows)],
            dst_ref=qbuf.at[s],
            send_sem=q_send.at[j],
            recv_sem=q_recv.at[j],
            device_id=(to, e),
            device_id_type=MESH,
        )

    def end_copy(j):
        to = lax.rem(s + j, n_seq)
        return pltpu.make_async_remote_copy(
            src_ref=ebuf.at[to],
            dst_ref=erecv.at[s],
            send_sem=e_send.at[j],
            recv_sem=e_recv.at[j],
            device_id=(to, e),
            device_id_type=MESH,
        )

    def each(act):
        def body(j, carry):
            act(j)
            return carry

        lax.fori_loop(1, n_seq, body, 0)

    net = Net(send_sem, recv_sem)
    each(lambda j: token_copy(j).start())
    each(lambda j: query_copy(j).start())
    lat_copy, _ = net.copy(latent.at[pl.ds(other * half_req, half_req)], lbuf.at[1], sibling, "core")

    tokbuf[s] = tokpad[c]
    line[...] = jnp.zeros_like(line)
    first_row = pl.multiple_of(c * HALF_TOK, HALF_TOK)
    xb[0, 0, :, wide_b:wide_b + LANE] = square[pl.ds(first_row, HALF_TOK), :].astype(BF16)
    each(lambda j: token_copy(j).wait_recv())
    for i in range(n_seq):
        begin, turn = share * i // LANE * LANE, share * i % LANE
        span = tokpad.shape[2] + LANE
        value = jnp.concatenate(
            [tokbuf[i].astype(F32), jnp.zeros((HALF_TOK, LANE), F32)], axis=1
        )
        if turn:
            value = pltpu.roll(value, turn, 1)
        line[:, begin:begin + span] = line[:, begin:begin + span] + value
    xa[0, 0] = line[:, 0:wide_a].astype(BF16)
    xb[0, 0, :, 0:wide_b] = line[:, wide_a:wide_a + wide_b].astype(BF16)

    position = lax.broadcasted_iota(jnp.int32, (n_seq * heads, LANE), 1)

    def one_request(i, carry):
        head_rows = pl.ds(pl.multiple_of(i * heads, heads), heads)
        q = qf[:, head_rows, :].reshape(n_seq * heads, qf.shape[2]).astype(BF16)
        length = lengths[0, c * half_req + i]
        parts = []
        for side, base in ((0, s), (1, 2 * y + other)):
            score = jnp.dot(q, lbuf[side, i], preferred_element_type=F32) * SCALE
            valid = position + base * LANE < length
            parts.append((jnp.where(valid, score, NEG), valid))
        top = jnp.maximum(
            jnp.max(parts[0][0], axis=1, keepdims=True),
            jnp.max(parts[1][0], axis=1, keepdims=True),
        ).astype(BF16).astype(F32)
        total = jnp.zeros((n_seq * heads, 1), F32)
        context = jnp.zeros((n_seq * heads, LAT), F32)
        for side in range(2):
            score, valid = parts[side]
            w = jnp.where(valid, jnp.exp(score - top), 0.0)
            total = total + jnp.sum(w, axis=1, keepdims=True)
            context = context + lax.dot_general(
                w.astype(BF16), lbuf[side, i, 0:LAT, :], (((1,), (1,)), ((), ())),
                preferred_element_type=F32,
            )
        total_high = total.astype(BF16).astype(F32)
        note = jnp.where(
            position == 0,
            top,
            jnp.where(position == 1, total_high, jnp.where(position == 2, total - total_high, 0.0)),
        )
        at = pl.ds(pl.multiple_of(2 * heads * i, 2 * heads), 2 * heads)
        obuf[:, at, 0:LAT] = context.astype(BF16).reshape(n_y, 2 * heads, LAT)
        obuf[:, at, LAT:LAT + LANE] = note.astype(BF16).reshape(n_y, 2 * heads, LANE)
        return carry

    def one_context(i, carry):
        at = pl.ds(pl.multiple_of(2 * heads * i, 2 * heads), 2 * heads)
        head_rows = pl.ds(pl.multiple_of(i * heads, heads), heads)
        line_of = lax.broadcasted_iota(jnp.int32, fresh.shape, 0)
        chosen = jnp.where(line_of == c * half_req + i, fresh[...].astype(F32), 0.0)
        key = jnp.sum(chosen, axis=0, keepdims=True)
        q = qf[pl.ds(2 * y, 2), head_rows, :].reshape(2 * heads, qf.shape[2])
        own = jnp.sum(q * key, axis=1, keepdims=True) * SCALE
        notes = [orecv[j, at, LAT:LAT + LANE].astype(F32) for j in range(n_y)]
        top = own
        for note in notes:
            top = jnp.maximum(top, note[:, 0:1])
        w = jnp.exp(own - top)
        total, context = w, w * key[:, 0:LAT]
        for j, note in enumerate(notes):
            w = jnp.exp(note[:, 0:1] - top)
            total = total + w * (note[:, 1:2] + note[:, 2:3])
            context = context + w * orecv[j, at, 0:LAT].astype(F32)
        context = context / total
        for core in range(2):
            cf[core, head_rows, :] = context[core * heads:(core + 1) * heads]
        return carry

    def attend():
        yield net.now + 8.0
        loads[0].wait()
        loads[1].wait()
        each(lambda j: query_copy(j).wait_recv())
        lat_copy.wait_recv()
        qf[...] = qbuf[...].astype(F32)
        lax.fori_loop(0, half_req // 2, one_request, 0)
        net.now += 2.0
        yield net.now + 0.5
        lax.fori_loop(half_req // 2, half_req, one_request, 0)
        net.now += 2.0
        came = []
        for j in range(1, n_y):
            to = lax.rem(y + j, n_y)
            came.append(net.copy(obuf.at[to], orecv.at[y], (2 * to + c, e), "y"))
        orecv[y] = obuf[y]
        yield net.now + 25.0
        for one, _ in came:
            one.wait_recv()
        lax.fori_loop(0, half_req, one_context, 0)
        net.now += 1.0
        cb[...] = cf[...].astype(BF16)
        back, when = net.copy(cb.at[other], crecv, sibling, "core")
        ctx_out[pl.ds(pl.multiple_of(c * q_rows, q_rows), q_rows), :] = cb[c]
        yield when + 5.0
        back.wait_recv()
        ctx_out[pl.ds(pl.multiple_of(other * q_rows, q_rows), q_rows), :] = crecv[...]

    half_a, half_b = wide_a // 2, wide_b // 2

    def cut_a(ref, side):
        lead = (slice(None),) * (len(ref.shape) - 1)
        return ref.at[lead + (pl.ds(side * half_a, half_a),)]

    def cut_b(ref, side):
        lead = (slice(None),) * (len(ref.shape) - 1)
        size = half_b if side == 0 else ref.shape[-1] - half_b
        return ref.at[lead + (pl.ds(side * half_b, size),)]

    teams = [(0,)] + [(d, -d) for d in range(1, n_z // 2)] + [(n_z // 2,)]

    def slots(team):
        return pl.ds(slot_z[team[0]], len(team))

    landed = {d: 0 for d in slot_z}

    def count(team):
        for d in team:
            landed[d] += 1

    def gather_a():
        yield from ring_gather(
            net, lambda d: xa.at[0, slot_x[d]], cut_a, NX, x_up, x_down, "x", lambda d: None
        )
        yield from ring_gather(
            net, lambda d: xa.at[slot_z[d]], cut_a, n_z, z_up, z_down, "z", lambda d: count((d,))
        )

    def gather_b():
        here = set()

        def start(dz):
            here.add(dz)
            team = [team for team in teams if dz in team][0]
            if here.issuperset(team):
                net.add(net.now, ring_gather(
                    net, lambda d: xb.at[slots(team), slot_x[d]], cut_b, NX, x_up, x_down, "x",
                    lambda d: count(team),
                ))

        yield from ring_gather(
            net, lambda d: xb.at[slot_z[d], 0], cut_b, n_z, z_up, z_down, "z", start
        )

    step_a, step_b = wide_a // 3, wide_b // 4
    weights = []

    def load_weights():
        yield net.now + 0.5
        for src, dst in (
            (wg, wcat.at[:, pl.ds(LANE, LANE)]),
            (wu, wcat.at[:, pl.ds(3 * LANE, LANE)]),
            (wd, wdcat.at[pl.ds(LANE, LANE)]),
        ):
            weights.append(net.copy(src, dst, sibling, "core")[0])

    def experts_of(first, last):
        rows = (last - first) * NX * HALF_TOK

        def up_a(k, carry):
            cols = pl.ds(pl.multiple_of(k * step_a, step_a), step_a)
            value = xa[first:last, :, :, cols].reshape(rows, step_a)
            acc[0:rows, :] += jnp.dot(value, wcat[cols, :], preferred_element_type=F32)
            return carry

        def up_b(k, carry):
            cols = pl.ds(pl.multiple_of(k * step_b, step_b), step_b)
            down = pl.ds(pl.multiple_of(wide_a + k * step_b, step_b), step_b)
            value = xb[first:last, :, :, cols].reshape(rows, step_b)
            acc[0:rows, :] += jnp.dot(value, wcat[down, :], preferred_element_type=F32)
            return carry

        def down_a(k, carry):
            cols = pl.ds(pl.multiple_of(k * step_a, step_a), step_a)
            value = jnp.dot(hid[0:rows, :], wdcat[:, cols], preferred_element_type=F32)
            ya[first:last, :, :, cols] = value.astype(BF16).reshape(last - first, NX, HALF_TOK, step_a)
            return carry

        def down_b(k, carry):
            cols = pl.ds(pl.multiple_of(k * step_b, step_b), step_b)
            down = pl.ds(pl.multiple_of(wide_a + k * step_b, step_b), step_b)
            value = jnp.dot(hid[0:rows, :], wdcat[:, down], preferred_element_type=F32)
            yb[first:last, :, :, cols] = value.astype(BF16).reshape(last - first, NX, HALF_TOK, step_b)
            return carry

        acc[0:rows, :] = jnp.zeros((rows, 4 * LANE), F32)
        lax.fori_loop(0, 3, up_a, 0)
        lax.fori_loop(0, 4, up_b, 0)
        tile = xb[first:last, :, :, wide_b:wide_b + LANE].reshape(rows, LANE).astype(F32)
        lane = lax.broadcasted_iota(jnp.int32, (rows, LANE), 1)
        gate = jnp.sum(
            jnp.where((lane == e) | (lane == e + experts), tile, 0.0), axis=1, keepdims=True
        )
        g = acc[0:rows, 0:2 * LANE]
        value = g / (1.0 + jnp.exp(-g)) * acc[0:rows, 2 * LANE:4 * LANE] * gate
        hid[0:rows, :] = value.astype(BF16)
        lax.fori_loop(0, 4, down_b, 0)
        lax.fori_loop(0, 3, down_a, 0)

    def compute():
        offsets = around(n_z)
        groups = [(0, 3), (3, 5), (5, 7), (7, 8)] if n_z == 8 else [(0, len(offsets))]
        for first, last in groups:
            while any(landed[d] < 1 + NX for d in offsets[first:last]):
                yield net.now + 0.01
            if first == 0:
                for load in loads[2:]:
                    load.wait()
                for made in weights:
                    made.wait_recv()
            experts_of(first, last)
            net.now += 1.0

    attention = attend()
    net.run([gather_a(), gather_b(), load_weights(), sample(attention, 3), compute()])

    net.links, net.now = {}, 0.0
    ended = set()

    def always(d):
        return True

    def row_sum(team):
        at = slots(team)

        def finish(total):
            yb[at, 0] = total.astype(BF16)
            ended.update(team)

        return ring_scatter(
            net, lambda d: yb.at[at, slot_x[d]], cut_b, lambda way, k: rbx.at[way, k, at],
            NX, x_up, x_down, "x", always, finish,
        )

    def keep_a(total):
        ya[0] = total.astype(BF16)

    def end_a(total):
        line[:, 0:wide_a] = total

    def end_b(total):
        line[:, wide_a:wide_a + wide_b] = total

    def sum_a():
        yield from ring_scatter(
            net, lambda d: ya.at[slot_z[d]], cut_a, lambda way, k: ra.at[way, k],
            n_z, z_up, z_down, "z", always, keep_a,
        )
        yield from ring_scatter(
            net, lambda d: ya.at[0, slot_x[d]], cut_a, lambda way, k: rax.at[way, k],
            NX, x_up, x_down, "x", always, end_a,
        )

    sum_b = ring_scatter(
        net, lambda d: yb.at[slot_z[d], 0], cut_b, lambda way, k: rb.at[way, k],
        n_z, z_up, z_down, "z", lambda d: d in ended, end_b,
    )
    before = list(net.copies)

    def settle():
        yield net.now + 1.0
        each(lambda j: token_copy(j).wait_send())
        each(lambda j: query_copy(j).wait_send())
        for made in before:
            made.wait_send()

    first_rows = [row_sum(team) for team in reversed(teams)]
    net.run(first_rows[:1] + [sum_a()] + first_rows[1:] + [sum_b, sample(attention, 9), settle()])

    for i in range(n_seq):
        begin, turn = share * i // LANE * LANE, share * i % LANE
        span = tokpad.shape[2] + LANE
        value = line[:, begin:begin + span]
        if turn:
            value = pltpu.roll(value, span - turn, 1)
        ebuf[i] = value[:, 0:tokpad.shape[2]].astype(BF16)
    each(lambda j: end_copy(j).start())
    erecv[s] = ebuf[s]
    each(lambda j: end_copy(j).wait_recv())
    for half in range(2):
        total = erecv[half].astype(F32)
        for i in range(1, n_y):
            total = total + erecv[2 * i + half].astype(F32)
        mix_out[half * HALF_TOK:(half + 1) * HALF_TOK, :] = total[:, 0:share].astype(BF16)

    each(lambda j: end_copy(j).wait_send())
    for made in net.copies[len(before):]:
        made.wait_send()


def sample(task, most):
    for _ in range(most):
        try:
            ready = next(task)
        except StopIteration:
            return
        yield ready


def on_device(latent, lengths, queries, fresh_latent, tokens, routes, gates, w_gate, w_up, w_down):
    n_seq, n_ep = lax.axis_size("seq"), lax.axis_size("ep")
    n_z, n_y = n_ep // NX, n_seq // 2
    n_req, heads, width = queries.shape
    share = tokens.shape[1]
    features = share * n_seq
    wide_a = features // 7 * 3
    wide_b = features - wide_a
    padded = -(-share // LANE) * LANE
    rows = n_ep * HALF_TOK
    half_req = n_req // 2
    q_rows = half_req * heads
    far_z, far_x = n_z // 2, NX // 2
    cfg = (n_seq, n_z, wide_a, wide_b, share, heads)
    vmem = pl.BlockSpec(memory_space=pltpu.VMEM)
    hbm = pl.BlockSpec(memory_space=pl.ANY)
    dma = pltpu.SemaphoreType.DMA
    ffn = 2 * rows * features * 6 * LANE
    context, mixed = pl.pallas_call(
        functools.partial(kernel, cfg),
        out_shape=(
            jax.ShapeDtypeStruct((n_req * heads, LAT), BF16),
            jax.ShapeDtypeStruct(tokens.shape, BF16),
        ),
        in_specs=[hbm, hbm, hbm, hbm, hbm, pl.BlockSpec(memory_space=pltpu.SMEM), vmem, vmem, vmem, vmem],
        out_specs=(vmem, vmem),
        scratch_shapes=[
            pltpu.VMEM((2, HALF_TOK, padded), BF16),
            pltpu.VMEM((n_seq, HALF_TOK, padded), BF16),
            pltpu.VMEM((HALF_TOK, features + 2 * LANE), F32),
            pltpu.VMEM((LANE, LANE), F32),
            pltpu.VMEM((n_z, NX, HALF_TOK, wide_a), BF16),
            pltpu.VMEM((n_z, NX, HALF_TOK, wide_b + LANE), BF16),
            pltpu.VMEM((features, 4 * LANE), BF16),
            pltpu.VMEM((2 * LANE, features), BF16),
            pltpu.VMEM((rows, 4 * LANE), F32),
            pltpu.VMEM((rows, 2 * LANE), BF16),
            pltpu.VMEM((n_z, NX, HALF_TOK, wide_a), BF16),
            pltpu.VMEM((n_z, NX, HALF_TOK, wide_b), BF16),
            pltpu.VMEM((2, far_z, NX, HALF_TOK, wide_a), BF16),
            pltpu.VMEM((2, far_x, HALF_TOK, wide_a), BF16),
            pltpu.VMEM((2, far_x, n_z, HALF_TOK, wide_b), BF16),
            pltpu.VMEM((2, far_z, HALF_TOK, wide_b), BF16),
            pltpu.VMEM((n_seq, HALF_TOK, padded), BF16),
            pltpu.VMEM((n_seq, HALF_TOK, padded), BF16),
            pltpu.VMEM((2, half_req, width, LANE), BF16),
            pltpu.VMEM((n_seq, q_rows, width), BF16),
            pltpu.VMEM((n_seq, q_rows, width), F32),
            pltpu.VMEM((n_y, 2 * q_rows, LAT + LANE), BF16),
            pltpu.VMEM((n_y, 2 * q_rows, LAT + LANE), BF16),
            pltpu.VMEM((2, q_rows, LAT), F32),
            pltpu.VMEM((2, q_rows, LAT), BF16),
            pltpu.VMEM((q_rows, LAT), BF16),
            dma((5,)),
            dma((120,)),
            dma((120,)),
            dma((n_seq,)),
            dma((n_seq,)),
            dma((n_seq,)),
            dma((n_seq,)),
            dma((n_seq,)),
            dma((n_seq,)),
        ],
        compiler_params=pltpu.CompilerParams(
            collective_id=0, has_side_effects=True, vmem_limit_bytes=56 * 1024 * 1024
        ),
        cost_estimate=pl.CostEstimate(flops=ffn, bytes_accessed=6 * 2**20, transcendentals=rows * 512),
    )(
        latent.transpose(0, 2, 1),
        queries.reshape(n_req * heads, width),
        w_gate[0],
        w_up[0],
        w_down[0],
        lengths,
        fresh_latent,
        tokens,
        routes.T,
        gates.T,
    )
    return context.reshape(n_req, heads, LAT), mixed


def solution(mesh):
    placed = (
        P("ep", "seq", None),
        P("ep", None),
        P("ep", "seq", None),
        P("ep", None),
        P("ep", "seq"),
        P("ep", None),
        P("ep", None),
        P("ep", None, "seq"),
        P("ep", None, "seq"),
        P("ep", "seq", None),
    )
    return jax.shard_map(
        on_device,
        mesh=mesh,
        in_specs=placed,
        out_specs=(P("ep", "seq", None), P("ep", "seq")),
        check_vma=False,
    )
```

```python
import functools
import heapq

import jax
import jax.numpy as jnp
from jax import lax
from jax.experimental import pallas as pl
from jax.experimental.pallas import tpu as pltpu
from jax.sharding import PartitionSpec as P

MESH = pl.DeviceIdType.MESH
LAT = 512
NX = 4
LANE = 128
HALF_TOK = 16
SCALE = 0.07216878364870322
NEG = -1.0e30
F32 = jnp.float32
BF16 = jnp.bfloat16

LINK_RATE = 45.0e3
HOP = 1.5


def mod(value, n):
    return lax.rem(value + n, n)


class Net:
    def __init__(self, send, recv):
        self.send, self.recv = send, recv
        self.count, self.now = 0, 0.0
        self.links, self.copies = {}, []

    def copy(self, src, dst, device, link):
        at = self.count
        self.count += 1
        made = pltpu.make_async_remote_copy(
            src_ref=src,
            dst_ref=dst,
            send_sem=self.send.at[at],
            recv_sem=self.recv.at[at],
            device_id=device,
            device_id_type=MESH,
        )
        made.start()
        size = 2
        for extent in src.shape:
            size *= extent
        begin = max(self.links.get(link, 0.0), self.now)
        self.links[link] = begin + size / LINK_RATE
        self.copies.append(made)
        return made, self.links[link] + HOP

    def run(self, tasks):
        self.heap, self.order = [], 0
        for task in tasks:
            self.add(self.now, task)
        while self.heap:
            at, _, task = heapq.heappop(self.heap)
            self.now = max(self.now, at)
            try:
                ready = next(task)
            except StopIteration:
                continue
            self.add(ready, task)

    def add(self, at, task):
        self.order += 1
        heapq.heappush(self.heap, (at, self.order, task))


def around(n):
    offsets = [0]
    for k in range(1, n // 2):
        offsets += [k, -k]
    return offsets + [n // 2]


def ring_gather(net, piece, cut, n, up, down, axis, landed):
    far = n // 2

    def pass_on(side, k):
        src, dst = piece((k, -k)[1 - side]), piece(far if k + 1 == far else (k + 1, -k - 1)[1 - side])
        if k + 1 == far:
            src, dst = cut(src, side), cut(dst, side)
        return net.copy(src, dst, (up, down)[side], axis + "+-"[side])

    cu, tu = pass_on(0, 0)
    cd, td = pass_on(1, 0)
    landed(0)
    for k in range(1, far):
        yield tu
        cu.wait_recv()
        cu, tu = pass_on(0, k)
        landed(-k)
        yield td
        cd.wait_recv()
        cd, td = pass_on(1, k)
        landed(k)
    yield max(tu, td)
    cu.wait_recv()
    cd.wait_recv()
    landed(far)


def add_into(ref, other):
    ref[...] = ref[...] + other[...]


def ring_scatter(net, piece, cut, arrived, n, up, down, axis, ready, finish):
    far = n // 2
    while not ready(far):
        yield net.now + 0.01
    cu, tu = net.copy(cut(piece(far), 0), cut(arrived(0, 0), 0), up, axis + "+")
    cd, td = net.copy(cut(piece(far), 1), cut(arrived(1, 0), 1), down, axis + "-")
    for k in range(1, far):
        d = far - k
        while not (ready(d) and ready(-d)):
            yield net.now + 0.01
        yield tu
        cu.wait_recv()
        mine, came = piece(d), arrived(0, k - 1)
        if k == 1:
            mine, came = cut(mine, 0), cut(came, 0)
        add_into(mine, came)
        cu, tu = net.copy(piece(d), arrived(0, k), up, axis + "+")
        yield td
        cd.wait_recv()
        mine, came = piece(-d), arrived(1, k - 1)
        if k == 1:
            mine, came = cut(mine, 1), cut(came, 1)
        add_into(mine, came)
        cd, td = net.copy(piece(-d), arrived(1, k), down, axis + "-")
    while not ready(0):
        yield net.now + 0.01
    yield max(tu, td)
    cu.wait_recv()
    cd.wait_recv()
    if far == 1:
        add_into(cut(piece(0), 0), cut(arrived(0, 0), 0))
        add_into(cut(piece(0), 1), cut(arrived(1, 0), 1))
        finish(piece(0)[...].astype(F32))
    else:
        finish(
            piece(0)[...].astype(F32)
            + arrived(0, far - 1)[...].astype(F32)
            + arrived(1, far - 1)[...].astype(F32)
        )


def kernel(
    cfg,
    latent, queries, wg, wu, wd, lengths, fresh, tokens, routes, gates,
    ctx_out, mix_out,
    tokpad, tokbuf, line, square, xa, xb, wcat, wdcat, acc, hid, ya, yb,
    ra, rax, rbx, rb, ebuf, erecv,
    lbuf, qbuf, qf, obuf, orecv, cf, cb, crecv,
    local_sem, send_sem, recv_sem, t_send, t_recv, q_send, q_recv, e_send, e_recv,
):
    n_seq, n_z, wide_a, wide_b, share, heads = cfg
    n_y = n_seq // 2
    s, e = lax.axis_index("seq"), lax.axis_index("ep")
    y, c = s // 2, lax.rem(s, 2)
    z, x = e // NX, lax.rem(e, NX)
    other = 1 - c
    sibling = (2 * y + other, e)
    experts = n_z * NX
    far_x = NX // 2
    n_req = lengths.shape[1]
    half_req = n_req // 2
    q_rows = half_req * heads
    x_up, x_down = (s, z * NX + mod(x + 1, NX)), (s, z * NX + mod(x - 1, NX))
    z_up, z_down = (s, mod(z + 1, n_z) * NX + x), (s, mod(z - 1, n_z) * NX + x)
    slot_z = {d: i for i, d in enumerate(around(n_z))}
    slot_x = {d: i for i, d in enumerate(around(NX))}

    def local(src, dst, i):
        made = pltpu.make_async_copy(src, dst, local_sem.at[i])
        made.start()
        return made

    for half in range(2):
        tokpad[half] = jnp.zeros_like(tokpad[half])
        tokpad[half, :, 0:share] = tokens[half * HALF_TOK:(half + 1) * HALF_TOK, :]

    barrier = pltpu.get_barrier_semaphore()

    def greet(j, carry):
        pl.semaphore_signal(
            barrier, inc=1, device_id=(lax.rem(s + j, n_seq), e), device_id_type=MESH
        )
        return carry

    lax.fori_loop(1, n_seq, greet, 0)
    for who in (x_up, x_down, z_up, z_down):
        pl.semaphore_signal(barrier, inc=1, device_id=who, device_id_type=MESH)

    mine_q = queries.at[pl.ds(pl.multiple_of(c * q_rows, q_rows), q_rows)]
    loads = [
        local(mine_q, qbuf.at[s], 0),
        local(latent.at[pl.ds(c * half_req, half_req)], lbuf.at[0], 1),
        local(wg, wcat.at[:, pl.ds(0, LANE)], 2),
        local(wu, wcat.at[:, pl.ds(2 * LANE, LANE)], 3),
        local(wd, wdcat.at[pl.ds(0, LANE)], 4),
    ]

    row = lax.broadcasted_iota(jnp.int32, (LANE, routes.shape[1]), 0)
    named = jnp.where(row < experts, row, row - experts)
    weight = jnp.zeros(named.shape, F32)
    for k in range(routes.shape[0]):
        weight = weight + jnp.where(named == routes[k:k + 1, :], gates[k:k + 1, :], 0.0)
    high = weight.astype(BF16).astype(F32)
    weight = jnp.where(row < experts, high, jnp.where(row < 2 * experts, weight - high, 0.0))
    square[...] = jnp.zeros_like(square)
    square[:, 0:routes.shape[1]] = weight
    square[...] = jnp.transpose(square[...])

    pl.semaphore_wait(barrier, n_seq - 1 + 4)

    def token_copy(j):
        to = lax.rem(s + j, n_seq)
        return pltpu.make_async_remote_copy(
            src_ref=tokpad.at[lax.rem(to, 2)],
            dst_ref=tokbuf.at[s],
            send_sem=t_send.at[j],
            recv_sem=t_recv.at[j],
            device_id=(to, e),
            device_id_type=MESH,
        )

    def query_copy(j):
        to = lax.rem(s + j, n_seq)
        begin = pl.multiple_of(lax.rem(to, 2) * q_rows, q_rows)
        return pltpu.make_async_remote_copy(
            src_ref=queries.at[pl.ds(begin, q_rows)],
            dst_ref=qbuf.at[s],
            send_sem=q_send.at[j],
            recv_sem=q_recv.at[j],
            device_id=(to, e),
            device_id_type=MESH,
        )

    def end_copy(j):
        to = lax.rem(s + j, n_seq)
        return pltpu.make_async_remote_copy(
            src_ref=ebuf.at[to],
            dst_ref=erecv.at[s],
            send_sem=e_send.at[j],
            recv_sem=e_recv.at[j],
            device_id=(to, e),
            device_id_type=MESH,
        )

    def each(act):
        def body(j, carry):
            act(j)
            return carry

        lax.fori_loop(1, n_seq, body, 0)

    net = Net(send_sem, recv_sem)
    each(lambda j: token_copy(j).start())

    tokbuf[s] = tokpad[c]
    line[...] = jnp.zeros_like(line)
    first_row = pl.multiple_of(c * HALF_TOK, HALF_TOK)
    xb[0, 0, :, wide_b:wide_b + LANE] = square[pl.ds(first_row, HALF_TOK), :].astype(BF16)
    each(lambda j: token_copy(j).wait_recv())
    for i in range(n_seq):
        begin, turn = share * i // LANE * LANE, share * i % LANE
        span = tokpad.shape[2] + LANE
        value = jnp.concatenate(
            [tokbuf[i].astype(F32), jnp.zeros((HALF_TOK, LANE), F32)], axis=1
        )
        if turn:
            value = pltpu.roll(value, turn, 1)
        line[:, begin:begin + span] = line[:, begin:begin + span] + value
    xa[0, 0] = line[:, 0:wide_a].astype(BF16)
    xb[0, 0, :, 0:wide_b] = line[:, wide_a:wide_a + wide_b].astype(BF16)

    position = lax.broadcasted_iota(jnp.int32, (n_seq * heads, LANE), 1)

    def one_request(i, carry):
        head_rows = pl.ds(pl.multiple_of(i * heads, heads), heads)
        q = qf[:, head_rows, :].reshape(n_seq * heads, qf.shape[2]).astype(BF16)
        length = lengths[0, c * half_req + i]
        parts = []
        for side, base in ((0, s), (1, 2 * y + other)):
            score = jnp.dot(q, lbuf[side, i], preferred_element_type=F32) * SCALE
            valid = position + base * LANE < length
            parts.append((jnp.where(valid, score, NEG), valid))
        top = jnp.maximum(
            jnp.max(parts[0][0], axis=1, keepdims=True),
            jnp.max(parts[1][0], axis=1, keepdims=True),
        ).astype(BF16).astype(F32)
        total = jnp.zeros((n_seq * heads, 1), F32)
        context = jnp.zeros((n_seq * heads, LAT), F32)
        for side in range(2):
            score, valid = parts[side]
            w = jnp.where(valid, jnp.exp(score - top), 0.0)
            total = total + jnp.sum(w, axis=1, keepdims=True)
            context = context + lax.dot_general(
                w.astype(BF16), lbuf[side, i, 0:LAT, :], (((1,), (1,)), ((), ())),
                preferred_element_type=F32,
            )
        total_high = total.astype(BF16).astype(F32)
        note = jnp.where(
            position == 0,
            top,
            jnp.where(position == 1, total_high, jnp.where(position == 2, total - total_high, 0.0)),
        )
        at = pl.ds(pl.multiple_of(2 * heads * i, 2 * heads), 2 * heads)
        obuf[:, at, 0:LAT] = context.astype(BF16).reshape(n_y, 2 * heads, LAT)
        obuf[:, at, LAT:LAT + LANE] = note.astype(BF16).reshape(n_y, 2 * heads, LANE)
        return carry

    def one_context(i, carry):
        at = pl.ds(pl.multiple_of(2 * heads * i, 2 * heads), 2 * heads)
        head_rows = pl.ds(pl.multiple_of(i * heads, heads), heads)
        line_of = lax.broadcasted_iota(jnp.int32, fresh.shape, 0)
        chosen = jnp.where(line_of == c * half_req + i, fresh[...].astype(F32), 0.0)
        key = jnp.sum(chosen, axis=0, keepdims=True)
        q = qf[pl.ds(2 * y, 2), head_rows, :].reshape(2 * heads, qf.shape[2])
        own = jnp.sum(q * key, axis=1, keepdims=True) * SCALE
        notes = [orecv[j, at, LAT:LAT + LANE].astype(F32) for j in range(n_y)]
        top = own
        for note in notes:
            top = jnp.maximum(top, note[:, 0:1])
        w = jnp.exp(own - top)
        total, context = w, w * key[:, 0:LAT]
        for j, note in enumerate(notes):
            w = jnp.exp(note[:, 0:1] - top)
            total = total + w * (note[:, 1:2] + note[:, 2:3])
            context = context + w * orecv[j, at, 0:LAT].astype(F32)
        context = context / total
        for core in range(2):
            cf[core, head_rows, :] = context[core * heads:(core + 1) * heads]
        return carry

    def attend():
        lat_copy, _ = net.copy(
            latent.at[pl.ds(other * half_req, half_req)], lbuf.at[1], sibling, "core"
        )
        each(lambda j: query_copy(j).start())
        yield net.now + 12.0
        loads[0].wait()
        loads[1].wait()
        each(lambda j: query_copy(j).wait_recv())
        lat_copy.wait_recv()
        qf[...] = qbuf[...].astype(F32)
        lax.fori_loop(0, half_req // 2, one_request, 0)
        net.now += 2.0
        yield net.now + 0.5
        lax.fori_loop(half_req // 2, half_req, one_request, 0)
        net.now += 2.0
        came = []
        for j in range(1, n_y):
            to = lax.rem(y + j, n_y)
            came.append(net.copy(obuf.at[to], orecv.at[y], (2 * to + c, e), "y"))
        orecv[y] = obuf[y]
        yield net.now + 25.0
        for one, _ in came:
            one.wait_recv()
        lax.fori_loop(0, half_req, one_context, 0)
        net.now += 1.0
        cb[...] = cf[...].astype(BF16)
        back, when = net.copy(cb.at[other], crecv, sibling, "core")
        ctx_out[pl.ds(pl.multiple_of(c * q_rows, q_rows), q_rows), :] = cb[c]
        yield when + 5.0
        back.wait_recv()
        ctx_out[pl.ds(pl.multiple_of(other * q_rows, q_rows), q_rows), :] = crecv[...]

    half_a, half_b = wide_a // 2, wide_b // 2

    def cut_a(ref, side):
        lead = (slice(None),) * (len(ref.shape) - 1)
        return ref.at[lead + (pl.ds(side * half_a, half_a),)]

    def cut_b(ref, side):
        lead = (slice(None),) * (len(ref.shape) - 1)
        size = half_b if side == 0 else ref.shape[-1] - half_b
        return ref.at[lead + (pl.ds(side * half_b, size),)]

    teams = [(0,)] + [(d, -d) for d in range(1, n_z // 2)] + [(n_z // 2,)]

    pairs = [(i, i + 1) for i in range(0, NX, 2)]

    def slots(team):
        return pl.ds(slot_z[team[0]], len(team))

    landed = {d: 0 for d in slot_z}

    def count(team):
        for d in team:
            landed[d] += 1

    def gather_a():
        here = set()

        def start(dx):
            here.add(slot_x[dx])
            for pair in pairs:
                if slot_x[dx] in pair and here.issuperset(pair):
                    net.add(net.now, along_z(pl.ds(pair[0], 2)))

        def along_z(at):
            return ring_gather(
                net, lambda d: xa.at[slot_z[d], at], cut_a, n_z, z_up, z_down, "z",
                lambda d: count((d,)),
            )

        yield from ring_gather(
            net, lambda d: xa.at[0, slot_x[d]], cut_a, NX, x_up, x_down, "x", start
        )

    def gather_b():
        here = set()

        def start(dz):
            here.add(dz)
            team = [team for team in teams if dz in team][0]
            if here.issuperset(team):
                net.add(net.now, ring_gather(
                    net, lambda d: xb.at[slots(team), slot_x[d]], cut_b, NX, x_up, x_down, "x",
                    lambda d: count(team),
                ))

        yield from ring_gather(
            net, lambda d: xb.at[slot_z[d], 0], cut_b, n_z, z_up, z_down, "z", start
        )

    step_a, step_b = wide_a // 2, wide_b // 3
    weights = []

    def load_weights():
        yield net.now + 0.5
        for src, dst in (
            (wg, wcat.at[:, pl.ds(LANE, LANE)]),
            (wu, wcat.at[:, pl.ds(3 * LANE, LANE)]),
            (wd, wdcat.at[pl.ds(LANE, LANE)]),
        ):
            weights.append(net.copy(src, dst, sibling, "core")[0])

    def experts_of(first, last):
        rows = (last - first) * NX * HALF_TOK

        def up_a(k, carry):
            cols = pl.ds(pl.multiple_of(k * step_a, step_a), step_a)
            value = xa[first:last, :, :, cols].reshape(rows, step_a)
            acc[0:rows, :] += jnp.dot(value, wcat[cols, :], preferred_element_type=F32)
            return carry

        def up_b(k, carry):
            cols = pl.ds(pl.multiple_of(k * step_b, step_b), step_b)
            down = pl.ds(pl.multiple_of(wide_a + k * step_b, LANE), step_b)
            value = xb[first:last, :, :, cols].reshape(rows, step_b)
            acc[0:rows, :] += jnp.dot(value, wcat[down, :], preferred_element_type=F32)
            return carry

        def down_a(k, carry):
            cols = pl.ds(pl.multiple_of(k * step_a, step_a), step_a)
            value = jnp.dot(hid[0:rows, :], wdcat[:, cols], preferred_element_type=F32)
            ya[first:last, :, :, cols] = value.astype(BF16).reshape(last - first, NX, HALF_TOK, step_a)
            return carry

        def down_b(k, carry):
            cols = pl.ds(pl.multiple_of(k * step_b, step_b), step_b)
            down = pl.ds(pl.multiple_of(wide_a + k * step_b, LANE), step_b)
            value = jnp.dot(hid[0:rows, :], wdcat[:, down], preferred_element_type=F32)
            yb[first:last, :, :, cols] = value.astype(BF16).reshape(last - first, NX, HALF_TOK, step_b)
            return carry

        acc[0:rows, :] = jnp.zeros((rows, 4 * LANE), F32)
        lax.fori_loop(0, 2, up_a, 0)
        lax.fori_loop(0, 3, up_b, 0)
        tile = xb[first:last, :, :, wide_b:wide_b + LANE].reshape(rows, LANE).astype(F32)
        lane = lax.broadcasted_iota(jnp.int32, (rows, LANE), 1)
        gate = jnp.sum(
            jnp.where((lane == e) | (lane == e + experts), tile, 0.0), axis=1, keepdims=True
        )
        g = acc[0:rows, 0:2 * LANE]
        value = g / (1.0 + jnp.exp(-g)) * acc[0:rows, 2 * LANE:4 * LANE] * gate
        hid[0:rows, :] = value.astype(BF16)
        lax.fori_loop(0, 3, down_b, 0)
        lax.fori_loop(0, 2, down_a, 0)

    def compute():
        offsets = around(n_z)
        groups = [(0, 3), (3, 5), (5, 7), (7, 8)] if n_z == 8 else [(0, len(offsets))]
        for first, last in groups:
            while any(landed[d] < len(pairs) + NX for d in offsets[first:last]):
                yield net.now + 0.01
            if first == 0:
                for load in loads[2:]:
                    load.wait()
                for made in weights:
                    made.wait_recv()
            experts_of(first, last)
            net.now += 1.0

    attention = attend()
    net.run([gather_a(), gather_b(), load_weights(), sample(attention, 4), compute()])

    net.links, net.now = {}, 0.0
    ended = set()

    def always(d):
        return True

    def row_sum(team):
        at = slots(team)

        def finish(total):
            yb[at, 0] = total.astype(BF16)
            ended.update(team)

        return ring_scatter(
            net, lambda d: yb.at[at, slot_x[d]], cut_b, lambda way, k: rbx.at[way, k, at],
            NX, x_up, x_down, "x", always, finish,
        )

    done_a = set()

    def column_sum(pair):
        at = pl.ds(pair[0], 2)

        def finish(total):
            ya[0, at] = total.astype(BF16)
            done_a.update(pair)

        return ring_scatter(
            net, lambda d: ya.at[slot_z[d], at], cut_a, lambda way, k: ra.at[way, k, at],
            n_z, z_up, z_down, "z", always, finish,
        )

    def end_a(total):
        line[:, 0:wide_a] = total

    def end_b(total):
        line[:, wide_a:wide_a + wide_b] = total

    sum_a = ring_scatter(
        net, lambda d: ya.at[0, slot_x[d]], cut_a, lambda way, k: rax.at[way, k],
        NX, x_up, x_down, "x", lambda d: slot_x[far_x if d == -far_x else d] in done_a, end_a,
    )

    sum_b = ring_scatter(
        net, lambda d: yb.at[slot_z[d], 0], cut_b, lambda way, k: rb.at[way, k],
        n_z, z_up, z_down, "z", lambda d: d in ended, end_b,
    )
    before = list(net.copies)

    def settle():
        yield net.now + 1.0
        each(lambda j: token_copy(j).wait_send())
        each(lambda j: query_copy(j).wait_send())
        for made in before:
            made.wait_send()

    first_rows = [row_sum(team) for team in reversed(teams)]
    columns = [column_sum(pair) for pair in reversed(pairs)]
    net.run(first_rows[:1] + columns + first_rows[1:] + [sum_a, sum_b, sample(attention, 9), settle()])

    for i in range(n_seq):
        begin, turn = share * i // LANE * LANE, share * i % LANE
        span = tokpad.shape[2] + LANE
        value = line[:, begin:begin + span]
        if turn:
            value = pltpu.roll(value, span - turn, 1)
        ebuf[i] = value[:, 0:tokpad.shape[2]].astype(BF16)
    each(lambda j: end_copy(j).start())
    erecv[s] = ebuf[s]
    each(lambda j: end_copy(j).wait_recv())
    for half in range(2):
        total = erecv[half].astype(F32)
        for i in range(1, n_y):
            total = total + erecv[2 * i + half].astype(F32)
        mix_out[half * HALF_TOK:(half + 1) * HALF_TOK, :] = total[:, 0:share].astype(BF16)

    each(lambda j: end_copy(j).wait_send())
    for made in net.copies[len(before):]:
        made.wait_send()


def sample(task, most):
    for _ in range(most):
        try:
            ready = next(task)
        except StopIteration:
            return
        yield ready


def hand_out(context, mixed, context_out, mixed_out, sem):
    first = pltpu.make_async_copy(context, context_out, sem.at[0])
    second = pltpu.make_async_copy(mixed, mixed_out, sem.at[1])
    first.start()
    second.start()
    first.wait()
    second.wait()


def on_device(latent, lengths, queries, fresh_latent, tokens, routes, gates, w_gate, w_up, w_down):
    n_seq, n_ep = lax.axis_size("seq"), lax.axis_size("ep")
    n_z, n_y = n_ep // NX, n_seq // 2
    n_req, heads, width = queries.shape
    share = tokens.shape[1]
    features = share * n_seq
    wide_a = features // 14 * 5
    wide_b = features - wide_a
    padded = -(-share // LANE) * LANE
    rows = n_ep * HALF_TOK
    half_req = n_req // 2
    q_rows = half_req * heads
    far_z, far_x = n_z // 2, NX // 2
    cfg = (n_seq, n_z, wide_a, wide_b, share, heads)
    vmem = pl.BlockSpec(memory_space=pltpu.VMEM)
    hbm = pl.BlockSpec(memory_space=pl.ANY)
    dma = pltpu.SemaphoreType.DMA
    ffn = 2 * rows * features * 6 * LANE
    context, mixed = pl.pallas_call(
        functools.partial(kernel, cfg),
        out_shape=(
            jax.ShapeDtypeStruct((n_req * heads, LAT), BF16),
            jax.ShapeDtypeStruct(tokens.shape, BF16),
        ),
        in_specs=[hbm, hbm, hbm, hbm, hbm, pl.BlockSpec(memory_space=pltpu.SMEM), vmem, vmem, vmem, vmem],
        out_specs=(vmem, vmem),
        scratch_shapes=[
            pltpu.VMEM((2, HALF_TOK, padded), BF16),
            pltpu.VMEM((n_seq, HALF_TOK, padded), BF16),
            pltpu.VMEM((HALF_TOK, features + 2 * LANE), F32),
            pltpu.VMEM((LANE, LANE), F32),
            pltpu.VMEM((n_z, NX, HALF_TOK, wide_a), BF16),
            pltpu.VMEM((n_z, NX, HALF_TOK, wide_b + LANE), BF16),
            pltpu.VMEM((features, 4 * LANE), BF16),
            pltpu.VMEM((2 * LANE, features), BF16),
            pltpu.VMEM((rows, 4 * LANE), F32),
            pltpu.VMEM((rows, 2 * LANE), BF16),
            pltpu.VMEM((n_z, NX, HALF_TOK, wide_a), BF16),
            pltpu.VMEM((n_z, NX, HALF_TOK, wide_b), BF16),
            pltpu.VMEM((2, far_z, NX, HALF_TOK, wide_a), BF16),
            pltpu.VMEM((2, far_x, HALF_TOK, wide_a), BF16),
            pltpu.VMEM((2, far_x, n_z, HALF_TOK, wide_b), BF16),
            pltpu.VMEM((2, far_z, HALF_TOK, wide_b), BF16),
            pltpu.VMEM((n_seq, HALF_TOK, padded), BF16),
            pltpu.VMEM((n_seq, HALF_TOK, padded), BF16),
            pltpu.VMEM((2, half_req, width, LANE), BF16),
            pltpu.VMEM((n_seq, q_rows, width), BF16),
            pltpu.VMEM((n_seq, q_rows, width), F32),
            pltpu.VMEM((n_y, 2 * q_rows, LAT + LANE), BF16),
            pltpu.VMEM((n_y, 2 * q_rows, LAT + LANE), BF16),
            pltpu.VMEM((2, q_rows, LAT), F32),
            pltpu.VMEM((2, q_rows, LAT), BF16),
            pltpu.VMEM((q_rows, LAT), BF16),
            dma((5,)),
            dma((120,)),
            dma((120,)),
            dma((n_seq,)),
            dma((n_seq,)),
            dma((n_seq,)),
            dma((n_seq,)),
            dma((n_seq,)),
            dma((n_seq,)),
        ],
        compiler_params=pltpu.CompilerParams(
            collective_id=0, has_side_effects=True, vmem_limit_bytes=56 * 1024 * 1024
        ),
        cost_estimate=pl.CostEstimate(flops=ffn, bytes_accessed=6 * 2**20, transcendentals=rows * 512),
    )(
        latent.transpose(0, 2, 1),
        queries.reshape(n_req * heads, width),
        w_gate[0],
        w_up[0],
        w_down[0],
        lengths,
        fresh_latent,
        tokens,
        routes.T,
        gates.T,
    )
    context, mixed = pl.pallas_call(
        hand_out,
        out_shape=(
            jax.ShapeDtypeStruct(context.shape, BF16),
            jax.ShapeDtypeStruct(mixed.shape, BF16),
        ),
        in_specs=[hbm, hbm],
        out_specs=(hbm, hbm),
        scratch_shapes=[dma((2,))],
        compiler_params=pltpu.CompilerParams(vmem_limit_bytes=60 * 1024 * 1024),
    )(context, mixed)
    return context.reshape(n_req, heads, LAT), mixed


def solution(mesh):
    placed = (
        P("ep", "seq", None),
        P("ep", None),
        P("ep", "seq", None),
        P("ep", None),
        P("ep", "seq"),
        P("ep", None),
        P("ep", None),
        P("ep", None, "seq"),
        P("ep", None, "seq"),
        P("ep", "seq", None),
    )
    return jax.shard_map(
        on_device,
        mesh=mesh,
        in_specs=placed,
        out_specs=(P("ep", "seq", None), P("ep", "seq")),
        check_vma=False,
    )
```

```python
import functools
import heapq

import jax
import jax.numpy as jnp
from jax import lax
from jax.experimental import pallas as pl
from jax.experimental.pallas import tpu as pltpu
from jax.sharding import PartitionSpec as P

MESH = pl.DeviceIdType.MESH
LAT = 512
NX = 4
LANE = 128
HALF_TOK = 16
SCALE = 0.07216878364870322
NEG = -1.0e30
F32 = jnp.float32
BF16 = jnp.bfloat16

LINK_RATE = 45.0e3
HOP = 1.5


def mod(value, n):
    return lax.rem(value + n, n)


class Net:
    def __init__(self, send, recv):
        self.send, self.recv = send, recv
        self.count, self.now = 0, 0.0
        self.links, self.copies = {}, []

    def copy(self, src, dst, device, link):
        at = self.count
        self.count += 1
        made = pltpu.make_async_remote_copy(
            src_ref=src,
            dst_ref=dst,
            send_sem=self.send.at[at],
            recv_sem=self.recv.at[at],
            device_id=device,
            device_id_type=MESH,
        )
        made.start()
        size = 2
        for extent in src.shape:
            size *= extent
        begin = max(self.links.get(link, 0.0), self.now)
        self.links[link] = begin + size / LINK_RATE
        self.copies.append(made)
        return made, self.links[link] + HOP

    def run(self, tasks):
        self.heap, self.order = [], 0
        for task in tasks:
            self.add(self.now, task)
        while self.heap:
            at, _, task = heapq.heappop(self.heap)
            self.now = max(self.now, at)
            try:
                ready = next(task)
            except StopIteration:
                continue
            self.add(ready, task)

    def add(self, at, task):
        self.order += 1
        heapq.heappush(self.heap, (at, self.order, task))


def around(n):
    offsets = [0]
    for k in range(1, n // 2):
        offsets += [k, -k]
    return offsets + [n // 2]


def ring_gather(net, piece, cut, n, up, down, axis, landed):
    far = n // 2

    def pass_on(side, k):
        src, dst = piece((k, -k)[1 - side]), piece(far if k + 1 == far else (k + 1, -k - 1)[1 - side])
        if k + 1 == far:
            src, dst = cut(src, side), cut(dst, side)
        return net.copy(src, dst, (up, down)[side], axis + "+-"[side])

    cu, tu = pass_on(0, 0)
    cd, td = pass_on(1, 0)
    landed(0)
    for k in range(1, far):
        yield tu
        cu.wait_recv()
        cu, tu = pass_on(0, k)
        landed(-k)
        yield td
        cd.wait_recv()
        cd, td = pass_on(1, k)
        landed(k)
    yield max(tu, td)
    cu.wait_recv()
    cd.wait_recv()
    landed(far)


def add_into(ref, other):
    ref[...] = ref[...] + other[...]


def ring_scatter(net, piece, cut, arrived, n, up, down, axis, ready, finish):
    far = n // 2
    while not ready(far):
        yield net.now + 0.01
    cu, tu = net.copy(cut(piece(far), 0), cut(arrived(0, 0), 0), up, axis + "+")
    cd, td = net.copy(cut(piece(far), 1), cut(arrived(1, 0), 1), down, axis + "-")
    for k in range(1, far):
        d = far - k
        while not (ready(d) and ready(-d)):
            yield net.now + 0.01
        yield tu
        cu.wait_recv()
        mine, came = piece(d), arrived(0, k - 1)
        if k == 1:
            mine, came = cut(mine, 0), cut(came, 0)
        add_into(mine, came)
        cu, tu = net.copy(piece(d), arrived(0, k), up, axis + "+")
        yield td
        cd.wait_recv()
        mine, came = piece(-d), arrived(1, k - 1)
        if k == 1:
            mine, came = cut(mine, 1), cut(came, 1)
        add_into(mine, came)
        cd, td = net.copy(piece(-d), arrived(1, k), down, axis + "-")
    while not ready(0):
        yield net.now + 0.01
    yield max(tu, td)
    cu.wait_recv()
    cd.wait_recv()
    if far == 1:
        add_into(cut(piece(0), 0), cut(arrived(0, 0), 0))
        add_into(cut(piece(0), 1), cut(arrived(1, 0), 1))
        finish(piece(0)[...].astype(F32))
    else:
        finish(
            piece(0)[...].astype(F32)
            + arrived(0, far - 1)[...].astype(F32)
            + arrived(1, far - 1)[...].astype(F32)
        )


def kernel(
    cfg,
    latent, queries, wg, wu, wd, lengths, fresh, tokens, routes, gates,
    ctx_out, mix_out,
    tokpad, tokbuf, line, square, xa, xb, wcat, wdcat, acc, hid, ya, yb,
    ra, rax, rbx, rb, ebuf, erecv,
    lbuf, qbuf, qf, obuf, orecv, cf, cb, crecv,
    local_sem, send_sem, recv_sem, t_send, t_recv, q_send, q_recv, e_send, e_recv,
):
    n_seq, n_z, wide_a, wide_b, share, heads = cfg
    n_y = n_seq // 2
    s, e = lax.axis_index("seq"), lax.axis_index("ep")
    y, c = s // 2, lax.rem(s, 2)
    z, x = e // NX, lax.rem(e, NX)
    other = 1 - c
    sibling = (2 * y + other, e)
    experts = n_z * NX
    far_x = NX // 2
    n_req = lengths.shape[1]
    half_req = n_req // 2
    q_rows = half_req * heads
    x_up, x_down = (s, z * NX + mod(x + 1, NX)), (s, z * NX + mod(x - 1, NX))
    z_up, z_down = (s, mod(z + 1, n_z) * NX + x), (s, mod(z - 1, n_z) * NX + x)
    slot_z = {d: i for i, d in enumerate(around(n_z))}
    slot_x = {d: i for i, d in enumerate(around(NX))}

    def local(src, dst, i):
        made = pltpu.make_async_copy(src, dst, local_sem.at[i])
        made.start()
        return made

    for half in range(2):
        tokpad[half] = jnp.zeros_like(tokpad[half])
        tokpad[half, :, 0:share] = tokens[half * HALF_TOK:(half + 1) * HALF_TOK, :]

    barrier = pltpu.get_barrier_semaphore()

    def greet(j, carry):
        pl.semaphore_signal(
            barrier, inc=1, device_id=(lax.rem(s + j, n_seq), e), device_id_type=MESH
        )
        return carry

    lax.fori_loop(1, n_seq, greet, 0)
    for who in (x_up, x_down, z_up, z_down):
        pl.semaphore_signal(barrier, inc=1, device_id=who, device_id_type=MESH)

    mine_q = queries.at[pl.ds(pl.multiple_of(c * q_rows, q_rows), q_rows)]
    loads = [
        local(mine_q, qbuf.at[s], 0),
        local(latent.at[pl.ds(c * half_req, half_req)], lbuf.at[0], 1),
        local(wg, wcat.at[:, pl.ds(0, LANE)], 2),
        local(wu, wcat.at[:, pl.ds(2 * LANE, LANE)], 3),
        local(wd, wdcat.at[pl.ds(0, LANE)], 4),
    ]

    row = lax.broadcasted_iota(jnp.int32, (LANE, routes.shape[1]), 0)
    named = jnp.where(row < experts, row, row - experts)
    weight = jnp.zeros(named.shape, F32)
    for k in range(routes.shape[0]):
        weight = weight + jnp.where(named == routes[k:k + 1, :], gates[k:k + 1, :], 0.0)
    high = weight.astype(BF16).astype(F32)
    weight = jnp.where(row < experts, high, jnp.where(row < 2 * experts, weight - high, 0.0))
    square[...] = jnp.zeros_like(square)
    square[:, 0:routes.shape[1]] = weight
    square[...] = jnp.transpose(square[...])

    pl.semaphore_wait(barrier, n_seq - 1 + 4)

    def token_copy(j):
        to = lax.rem(s + j, n_seq)
        return pltpu.make_async_remote_copy(
            src_ref=tokpad.at[lax.rem(to, 2)],
            dst_ref=tokbuf.at[s],
            send_sem=t_send.at[j],
            recv_sem=t_recv.at[j],
            device_id=(to, e),
            device_id_type=MESH,
        )

    def query_copy(j):
        to = lax.rem(s + j, n_seq)
        begin = pl.multiple_of(lax.rem(to, 2) * q_rows, q_rows)
        return pltpu.make_async_remote_copy(
            src_ref=queries.at[pl.ds(begin, q_rows)],
            dst_ref=qbuf.at[s],
            send_sem=q_send.at[j],
            recv_sem=q_recv.at[j],
            device_id=(to, e),
            device_id_type=MESH,
        )

    def end_copy(j):
        to = lax.rem(s + j, n_seq)
        return pltpu.make_async_remote_copy(
            src_ref=ebuf.at[to],
            dst_ref=erecv.at[s],
            send_sem=e_send.at[j],
            recv_sem=e_recv.at[j],
            device_id=(to, e),
            device_id_type=MESH,
        )

    def each(act):
        def body(j, carry):
            act(j)
            return carry

        lax.fori_loop(1, n_seq, body, 0)

    net = Net(send_sem, recv_sem)
    each(lambda j: token_copy(j).start())

    tokbuf[s] = tokpad[c]
    line[...] = jnp.zeros_like(line)
    first_row = pl.multiple_of(c * HALF_TOK, HALF_TOK)
    xb[0, 0, :, wide_b:wide_b + LANE] = square[pl.ds(first_row, HALF_TOK), :].astype(BF16)
    each(lambda j: token_copy(j).wait_recv())
    for i in range(n_seq):
        begin, turn = share * i // LANE * LANE, share * i % LANE
        span = tokpad.shape[2] + LANE
        value = jnp.concatenate(
            [tokbuf[i].astype(F32), jnp.zeros((HALF_TOK, LANE), F32)], axis=1
        )
        if turn:
            value = pltpu.roll(value, turn, 1)
        line[:, begin:begin + span] = line[:, begin:begin + span] + value
    xa[0, 0] = line[:, 0:wide_a].astype(BF16)
    xb[0, 0, :, 0:wide_b] = line[:, wide_a:wide_a + wide_b].astype(BF16)

    position = lax.broadcasted_iota(jnp.int32, (n_seq * heads, LANE), 1)

    def one_request(i, carry):
        head_rows = pl.ds(pl.multiple_of(i * heads, heads), heads)
        q = qf[:, head_rows, :].reshape(n_seq * heads, qf.shape[2]).astype(BF16)
        length = lengths[0, c * half_req + i]
        parts = []
        for side, base in ((0, s), (1, 2 * y + other)):
            score = jnp.dot(q, lbuf[side, i], preferred_element_type=F32) * SCALE
            valid = position + base * LANE < length
            parts.append((jnp.where(valid, score, NEG), valid))
        top = jnp.maximum(
            jnp.max(parts[0][0], axis=1, keepdims=True),
            jnp.max(parts[1][0], axis=1, keepdims=True),
        ).astype(BF16).astype(F32)
        total = jnp.zeros((n_seq * heads, 1), F32)
        context = jnp.zeros((n_seq * heads, LAT), F32)
        for side in range(2):
            score, valid = parts[side]
            w = jnp.where(valid, jnp.exp(score - top), 0.0)
            total = total + jnp.sum(w, axis=1, keepdims=True)
            context = context + lax.dot_general(
                w.astype(BF16), lbuf[side, i, 0:LAT, :], (((1,), (1,)), ((), ())),
                preferred_element_type=F32,
            )
        total_high = total.astype(BF16).astype(F32)
        note = jnp.where(
            position == 0,
            top,
            jnp.where(position == 1, total_high, jnp.where(position == 2, total - total_high, 0.0)),
        )
        at = pl.ds(pl.multiple_of(2 * heads * i, 2 * heads), 2 * heads)
        obuf[:, at, 0:LAT] = context.astype(BF16).reshape(n_y, 2 * heads, LAT)
        obuf[:, at, LAT:LAT + LANE] = note.astype(BF16).reshape(n_y, 2 * heads, LANE)
        return carry

    def one_context(i, carry):
        at = pl.ds(pl.multiple_of(2 * heads * i, 2 * heads), 2 * heads)
        head_rows = pl.ds(pl.multiple_of(i * heads, heads), heads)
        line_of = lax.broadcasted_iota(jnp.int32, fresh.shape, 0)
        chosen = jnp.where(line_of == c * half_req + i, fresh[...].astype(F32), 0.0)
        key = jnp.sum(chosen, axis=0, keepdims=True)
        q = qf[pl.ds(2 * y, 2), head_rows, :].reshape(2 * heads, qf.shape[2])
        own = jnp.sum(q * key, axis=1, keepdims=True) * SCALE
        notes = [orecv[j, at, LAT:LAT + LANE].astype(F32) for j in range(n_y)]
        top = own
        for note in notes:
            top = jnp.maximum(top, note[:, 0:1])
        w = jnp.exp(own - top)
        total, context = w, w * key[:, 0:LAT]
        for j, note in enumerate(notes):
            w = jnp.exp(note[:, 0:1] - top)
            total = total + w * (note[:, 1:2] + note[:, 2:3])
            context = context + w * orecv[j, at, 0:LAT].astype(F32)
        context = context / total
        for core in range(2):
            cf[core, head_rows, :] = context[core * heads:(core + 1) * heads]
        return carry

    def attend():
        lat_copy, _ = net.copy(
            latent.at[pl.ds(other * half_req, half_req)], lbuf.at[1], sibling, "core"
        )
        each(lambda j: query_copy(j).start())
        yield net.now + 12.0
        loads[0].wait()
        loads[1].wait()
        each(lambda j: query_copy(j).wait_recv())
        lat_copy.wait_recv()
        qf[...] = qbuf[...].astype(F32)
        lax.fori_loop(0, half_req // 2, one_request, 0)
        net.now += 2.0
        yield net.now + 0.5
        lax.fori_loop(half_req // 2, half_req, one_request, 0)
        net.now += 2.0
        came = []
        for j in range(1, n_y):
            to = lax.rem(y + j, n_y)
            came.append(net.copy(obuf.at[to], orecv.at[y], (2 * to + c, e), "y"))
        orecv[y] = obuf[y]
        yield net.now + 25.0
        for one, _ in came:
            one.wait_recv()
        lax.fori_loop(0, half_req, one_context, 0)
        net.now += 1.0
        cb[...] = cf[...].astype(BF16)
        back, when = net.copy(cb.at[other], crecv, sibling, "core")
        ctx_out[pl.ds(pl.multiple_of(c * q_rows, q_rows), q_rows), :] = cb[c]
        yield when + 5.0
        back.wait_recv()
        ctx_out[pl.ds(pl.multiple_of(other * q_rows, q_rows), q_rows), :] = crecv[...]

    half_a, half_b = wide_a // 2, wide_b // 2

    def cut_a(ref, side):
        lead = (slice(None),) * (len(ref.shape) - 1)
        return ref.at[lead + (pl.ds(side * half_a, half_a),)]

    def cut_b(ref, side):
        lead = (slice(None),) * (len(ref.shape) - 1)
        size = half_b if side == 0 else ref.shape[-1] - half_b
        return ref.at[lead + (pl.ds(side * half_b, size),)]

    teams = [(0,)] + [(d, -d) for d in range(1, n_z // 2)] + [(n_z // 2,)]

    pairs = [(i, i + 1) for i in range(0, NX, 2)]

    def slots(team):
        return pl.ds(slot_z[team[0]], len(team))

    landed = {d: 0 for d in slot_z}

    def count(team):
        for d in team:
            landed[d] += 1

    def gather_a():
        here = set()

        def start(dx):
            here.add(slot_x[dx])
            for pair in pairs:
                if slot_x[dx] in pair and here.issuperset(pair):
                    net.add(net.now, along_z(pl.ds(pair[0], 2)))

        def along_z(at):
            return ring_gather(
                net, lambda d: xa.at[slot_z[d], at], cut_a, n_z, z_up, z_down, "z",
                lambda d: count((d,)),
            )

        yield from ring_gather(
            net, lambda d: xa.at[0, slot_x[d]], cut_a, NX, x_up, x_down, "x", start
        )

    def gather_b():
        here = set()

        def start(dz):
            here.add(dz)
            team = [team for team in teams if dz in team][0]
            if here.issuperset(team):
                net.add(net.now, ring_gather(
                    net, lambda d: xb.at[slots(team), slot_x[d]], cut_b, NX, x_up, x_down, "x",
                    lambda d: count(team),
                ))

        yield from ring_gather(
            net, lambda d: xb.at[slot_z[d], 0], cut_b, n_z, z_up, z_down, "z", start
        )

    step_a, step_b = wide_a // 3, wide_b // 2
    weights = []

    def load_weights():
        yield net.now + 0.5
        for src, dst in (
            (wg, wcat.at[:, pl.ds(LANE, LANE)]),
            (wu, wcat.at[:, pl.ds(3 * LANE, LANE)]),
            (wd, wdcat.at[pl.ds(LANE, LANE)]),
        ):
            weights.append(net.copy(src, dst, sibling, "core")[0])

    def experts_of(first, last):
        rows = (last - first) * NX * HALF_TOK

        def up_a(k, carry):
            cols = pl.ds(pl.multiple_of(k * step_a, step_a), step_a)
            value = xa[first:last, :, :, cols].reshape(rows, step_a)
            acc[0:rows, :] += jnp.dot(value, wcat[cols, :], preferred_element_type=F32)
            return carry

        def up_b(k, carry):
            cols = pl.ds(pl.multiple_of(k * step_b, step_b), step_b)
            down = pl.ds(pl.multiple_of(wide_a + k * step_b, LANE), step_b)
            value = xb[first:last, :, :, cols].reshape(rows, step_b)
            acc[0:rows, :] += jnp.dot(value, wcat[down, :], preferred_element_type=F32)
            return carry

        def down_a(k, carry):
            cols = pl.ds(pl.multiple_of(k * step_a, step_a), step_a)
            value = jnp.dot(hid[0:rows, :], wdcat[:, cols], preferred_element_type=F32)
            ya[first:last, :, :, cols] = value.astype(BF16).reshape(last - first, NX, HALF_TOK, step_a)
            return carry

        def down_b(k, carry):
            cols = pl.ds(pl.multiple_of(k * step_b, step_b), step_b)
            down = pl.ds(pl.multiple_of(wide_a + k * step_b, LANE), step_b)
            value = jnp.dot(hid[0:rows, :], wdcat[:, down], preferred_element_type=F32)
            yb[first:last, :, :, cols] = value.astype(BF16).reshape(last - first, NX, HALF_TOK, step_b)
            return carry

        acc[0:rows, :] = jnp.zeros((rows, 4 * LANE), F32)
        lax.fori_loop(0, 3, up_a, 0)
        lax.fori_loop(0, 2, up_b, 0)
        tile = xb[first:last, :, :, wide_b:wide_b + LANE].reshape(rows, LANE).astype(F32)
        lane = lax.broadcasted_iota(jnp.int32, (rows, LANE), 1)
        gate = jnp.sum(
            jnp.where((lane == e) | (lane == e + experts), tile, 0.0), axis=1, keepdims=True
        )
        g = acc[0:rows, 0:2 * LANE]
        value = g / (1.0 + jnp.exp(-g)) * acc[0:rows, 2 * LANE:4 * LANE] * gate
        hid[0:rows, :] = value.astype(BF16)
        lax.fori_loop(0, 2, down_b, 0)
        lax.fori_loop(0, 3, down_a, 0)

    def compute():
        offsets = around(n_z)
        groups = [(0, 3), (3, 5), (5, 7), (7, 8)] if n_z == 8 else [(0, len(offsets))]
        for first, last in groups:
            while any(landed[d] < len(pairs) + NX for d in offsets[first:last]):
                yield net.now + 0.01
            if first == 0:
                for load in loads[2:]:
                    load.wait()
                for made in weights:
                    made.wait_recv()
            experts_of(first, last)
            net.now += 1.0

    attention = attend()
    net.run([gather_a(), gather_b(), load_weights(), sample(attention, 4), compute()])

    net.links, net.now = {}, 0.0
    ended = set()

    def always(d):
        return True

    def row_sum(team):
        at = slots(team)

        def finish(total):
            yb[at, 0] = total.astype(BF16)
            ended.update(team)

        return ring_scatter(
            net, lambda d: yb.at[at, slot_x[d]], cut_b, lambda way, k: rbx.at[way, k, at],
            NX, x_up, x_down, "x", always, finish,
        )

    done_a = set()

    def column_sum(pair):
        at = pl.ds(pair[0], 2)

        def finish(total):
            ya[0, at] = total.astype(BF16)
            done_a.update(pair)

        return ring_scatter(
            net, lambda d: ya.at[slot_z[d], at], cut_a, lambda way, k: ra.at[way, k, at],
            n_z, z_up, z_down, "z", always, finish,
        )

    def end_a(total):
        line[:, 0:wide_a] = total

    def end_b(total):
        line[:, wide_a:wide_a + wide_b] = total

    sum_a = ring_scatter(
        net, lambda d: ya.at[0, slot_x[d]], cut_a, lambda way, k: rax.at[way, k],
        NX, x_up, x_down, "x", lambda d: slot_x[far_x if d == -far_x else d] in done_a, end_a,
    )

    sum_b = ring_scatter(
        net, lambda d: yb.at[slot_z[d], 0], cut_b, lambda way, k: rb.at[way, k],
        n_z, z_up, z_down, "z", lambda d: d in ended, end_b,
    )
    before = list(net.copies)

    def settle():
        yield net.now + 1.0
        each(lambda j: token_copy(j).wait_send())
        each(lambda j: query_copy(j).wait_send())
        for made in before:
            made.wait_send()

    first_rows = [row_sum(team) for team in reversed(teams)]
    columns = [column_sum(pair) for pair in reversed(pairs)]
    net.run(first_rows[:1] + columns + first_rows[1:] + [sum_a, sum_b, sample(attention, 9), settle()])

    for i in range(n_seq):
        begin, turn = share * i // LANE * LANE, share * i % LANE
        span = tokpad.shape[2] + LANE
        value = line[:, begin:begin + span]
        if turn:
            value = pltpu.roll(value, span - turn, 1)
        ebuf[i] = value[:, 0:tokpad.shape[2]].astype(BF16)
    each(lambda j: end_copy(j).start())
    erecv[s] = ebuf[s]
    each(lambda j: end_copy(j).wait_recv())
    for half in range(2):
        total = erecv[half].astype(F32)
        for i in range(1, n_y):
            total = total + erecv[2 * i + half].astype(F32)
        mix_out[half * HALF_TOK:(half + 1) * HALF_TOK, :] = total[:, 0:share].astype(BF16)

    each(lambda j: end_copy(j).wait_send())
    for made in net.copies[len(before):]:
        made.wait_send()


def sample(task, most):
    for _ in range(most):
        try:
            ready = next(task)
        except StopIteration:
            return
        yield ready


def on_device(latent, lengths, queries, fresh_latent, tokens, routes, gates, w_gate, w_up, w_down):
    n_seq, n_ep = lax.axis_size("seq"), lax.axis_size("ep")
    n_z, n_y = n_ep // NX, n_seq // 2
    n_req, heads, width = queries.shape
    share = tokens.shape[1]
    features = share * n_seq
    wide_a = features // 14 * 9
    wide_b = features - wide_a
    padded = -(-share // LANE) * LANE
    rows = n_ep * HALF_TOK
    half_req = n_req // 2
    q_rows = half_req * heads
    far_z, far_x = n_z // 2, NX // 2
    cfg = (n_seq, n_z, wide_a, wide_b, share, heads)
    vmem = pl.BlockSpec(memory_space=pltpu.VMEM)
    hbm = pl.BlockSpec(memory_space=pl.ANY)
    dma = pltpu.SemaphoreType.DMA
    ffn = 2 * rows * features * 6 * LANE
    context, mixed = pl.pallas_call(
        functools.partial(kernel, cfg),
        out_shape=(
            jax.ShapeDtypeStruct((n_req * heads, LAT), BF16),
            jax.ShapeDtypeStruct(tokens.shape, BF16),
        ),
        in_specs=[hbm, hbm, hbm, hbm, hbm, pl.BlockSpec(memory_space=pltpu.SMEM), vmem, vmem, vmem, vmem],
        out_specs=(vmem, vmem),
        scratch_shapes=[
            pltpu.VMEM((2, HALF_TOK, padded), BF16),
            pltpu.VMEM((n_seq, HALF_TOK, padded), BF16),
            pltpu.VMEM((HALF_TOK, features + 2 * LANE), F32),
            pltpu.VMEM((LANE, LANE), F32),
            pltpu.VMEM((n_z, NX, HALF_TOK, wide_a), BF16),
            pltpu.VMEM((n_z, NX, HALF_TOK, wide_b + LANE), BF16),
            pltpu.VMEM((features, 4 * LANE), BF16),
            pltpu.VMEM((2 * LANE, features), BF16),
            pltpu.VMEM((rows, 4 * LANE), F32),
            pltpu.VMEM((rows, 2 * LANE), BF16),
            pltpu.VMEM((n_z, NX, HALF_TOK, wide_a), BF16),
            pltpu.VMEM((n_z, NX, HALF_TOK, wide_b), BF16),
            pltpu.VMEM((2, far_z, NX, HALF_TOK, wide_a), BF16),
            pltpu.VMEM((2, far_x, HALF_TOK, wide_a), BF16),
            pltpu.VMEM((2, far_x, n_z, HALF_TOK, wide_b), BF16),
            pltpu.VMEM((2, far_z, HALF_TOK, wide_b), BF16),
            pltpu.VMEM((n_seq, HALF_TOK, padded), BF16),
            pltpu.VMEM((n_seq, HALF_TOK, padded), BF16),
            pltpu.VMEM((2, half_req, width, LANE), BF16),
            pltpu.VMEM((n_seq, q_rows, width), BF16),
            pltpu.VMEM((n_seq, q_rows, width), F32),
            pltpu.VMEM((n_y, 2 * q_rows, LAT + LANE), BF16),
            pltpu.VMEM((n_y, 2 * q_rows, LAT + LANE), BF16),
            pltpu.VMEM((2, q_rows, LAT), F32),
            pltpu.VMEM((2, q_rows, LAT), BF16),
            pltpu.VMEM((q_rows, LAT), BF16),
            dma((5,)),
            dma((120,)),
            dma((120,)),
            dma((n_seq,)),
            dma((n_seq,)),
            dma((n_seq,)),
            dma((n_seq,)),
            dma((n_seq,)),
            dma((n_seq,)),
        ],
        compiler_params=pltpu.CompilerParams(
            collective_id=0, has_side_effects=True, vmem_limit_bytes=56 * 1024 * 1024
        ),
        cost_estimate=pl.CostEstimate(flops=ffn, bytes_accessed=6 * 2**20, transcendentals=rows * 512),
    )(
        latent.transpose(0, 2, 1),
        queries.reshape(n_req * heads, width),
        w_gate[0],
        w_up[0],
        w_down[0],
        lengths,
        fresh_latent,
        tokens,
        routes.T,
        gates.T,
    )
    return context.reshape(n_req, heads, LAT), mixed


def solution(mesh):
    placed = (
        P("ep", "seq", None),
        P("ep", None),
        P("ep", "seq", None),
        P("ep", None),
        P("ep", "seq"),
        P("ep", None),
        P("ep", None),
        P("ep", None, "seq"),
        P("ep", None, "seq"),
        P("ep", "seq", None),
    )
    return jax.shard_map(
        on_device,
        mesh=mesh,
        in_specs=placed,
        out_specs=(P("ep", "seq", None), P("ep", "seq")),
        check_vma=False,
    )
```

```python
import functools
import heapq

import jax
import jax.numpy as jnp
from jax import lax
from jax.experimental import pallas as pl
from jax.experimental.pallas import tpu as pltpu
from jax.sharding import PartitionSpec as P

MESH = pl.DeviceIdType.MESH
LAT = 512
NX = 4
LANE = 128
HALF_TOK = 16
SCALE = 0.07216878364870322
NEG = -1.0e30
F32 = jnp.float32
BF16 = jnp.bfloat16

LINK_RATE = 45.0e3
HOP = 1.5


def mod(value, n):
    return lax.rem(value + n, n)


class Net:
    def __init__(self, send, recv):
        self.send, self.recv = send, recv
        self.count, self.now = 0, 0.0
        self.links, self.copies = {}, []

    def copy(self, src, dst, device, link):
        at = self.count
        self.count += 1
        made = pltpu.make_async_remote_copy(
            src_ref=src,
            dst_ref=dst,
            send_sem=self.send.at[at],
            recv_sem=self.recv.at[at],
            device_id=device,
            device_id_type=MESH,
        )
        made.start()
        size = 2
        for extent in src.shape:
            size *= extent
        begin = max(self.links.get(link, 0.0), self.now)
        self.links[link] = begin + size / LINK_RATE
        self.copies.append(made)
        return made, self.links[link] + HOP

    def run(self, tasks):
        self.heap, self.order = [], 0
        for task in tasks:
            self.add(self.now, task)
        while self.heap:
            at, _, task = heapq.heappop(self.heap)
            self.now = max(self.now, at)
            try:
                ready = next(task)
            except StopIteration:
                continue
            self.add(ready, task)

    def add(self, at, task):
        self.order += 1
        heapq.heappush(self.heap, (at, self.order, task))


def around(n):
    offsets = [0]
    for k in range(1, n // 2):
        offsets += [k, -k]
    return offsets + [n // 2]


def ring_gather(net, piece, cut, n, up, down, axis, landed):
    far = n // 2

    def pass_on(side, k):
        src, dst = piece((k, -k)[1 - side]), piece(far if k + 1 == far else (k + 1, -k - 1)[1 - side])
        if k + 1 == far:
            src, dst = cut(src, side), cut(dst, side)
        return net.copy(src, dst, (up, down)[side], axis + "+-"[side])

    cu, tu = pass_on(0, 0)
    cd, td = pass_on(1, 0)
    landed(0)
    for k in range(1, far):
        yield tu
        cu.wait_recv()
        cu, tu = pass_on(0, k)
        landed(-k)
        yield td
        cd.wait_recv()
        cd, td = pass_on(1, k)
        landed(k)
    yield max(tu, td)
    cu.wait_recv()
    cd.wait_recv()
    landed(far)


def add_into(ref, other):
    ref[...] = ref[...] + other[...]


def ring_scatter(net, piece, cut, arrived, n, up, down, axis, ready, finish):
    far = n // 2
    while not ready(far):
        yield net.now + 0.01
    cu, tu = net.copy(cut(piece(far), 0), cut(arrived(0, 0), 0), up, axis + "+")
    cd, td = net.copy(cut(piece(far), 1), cut(arrived(1, 0), 1), down, axis + "-")
    for k in range(1, far):
        d = far - k
        while not (ready(d) and ready(-d)):
            yield net.now + 0.01
        yield tu
        cu.wait_recv()
        mine, came = piece(d), arrived(0, k - 1)
        if k == 1:
            mine, came = cut(mine, 0), cut(came, 0)
        add_into(mine, came)
        cu, tu = net.copy(piece(d), arrived(0, k), up, axis + "+")
        yield td
        cd.wait_recv()
        mine, came = piece(-d), arrived(1, k - 1)
        if k == 1:
            mine, came = cut(mine, 1), cut(came, 1)
        add_into(mine, came)
        cd, td = net.copy(piece(-d), arrived(1, k), down, axis + "-")
    while not ready(0):
        yield net.now + 0.01
    yield max(tu, td)
    cu.wait_recv()
    cd.wait_recv()
    if far == 1:
        add_into(cut(piece(0), 0), cut(arrived(0, 0), 0))
        add_into(cut(piece(0), 1), cut(arrived(1, 0), 1))
        finish(piece(0)[...].astype(F32))
    else:
        finish(
            piece(0)[...].astype(F32)
            + arrived(0, far - 1)[...].astype(F32)
            + arrived(1, far - 1)[...].astype(F32)
        )


def kernel(
    cfg,
    latent, queries, wg, wu, wd, lengths, fresh, tokens, routes, gates,
    ctx_out, mix_out,
    tokpad, tokbuf, line, square, xa, xb, wcat, wdcat, acc, hid, ya, yb,
    ra, rax, rbx, rb, ebuf, erecv,
    lbuf, qbuf, qf, obuf, orecv, cf, cb, crecv,
    local_sem, send_sem, recv_sem, t_send, t_recv, q_send, q_recv, e_send, e_recv,
):
    n_seq, n_z, wide_a, wide_b, share, heads = cfg
    n_y = n_seq // 2
    s, e = lax.axis_index("seq"), lax.axis_index("ep")
    y, c = s // 2, lax.rem(s, 2)
    z, x = e // NX, lax.rem(e, NX)
    other = 1 - c
    sibling = (2 * y + other, e)
    experts = n_z * NX
    far_x = NX // 2
    n_req = lengths.shape[1]
    half_req = n_req // 2
    q_rows = half_req * heads
    x_up, x_down = (s, z * NX + mod(x + 1, NX)), (s, z * NX + mod(x - 1, NX))
    z_up, z_down = (s, mod(z + 1, n_z) * NX + x), (s, mod(z - 1, n_z) * NX + x)
    slot_z = {d: i for i, d in enumerate(around(n_z))}
    slot_x = {d: i for i, d in enumerate(around(NX))}

    def local(src, dst, i):
        made = pltpu.make_async_copy(src, dst, local_sem.at[i])
        made.start()
        return made

    for half in range(2):
        tokpad[half] = jnp.zeros_like(tokpad[half])
        tokpad[half, :, 0:share] = tokens[half * HALF_TOK:(half + 1) * HALF_TOK, :]

    barrier = pltpu.get_barrier_semaphore()

    def greet(j, carry):
        pl.semaphore_signal(
            barrier, inc=1, device_id=(lax.rem(s + j, n_seq), e), device_id_type=MESH
        )
        return carry

    lax.fori_loop(1, n_seq, greet, 0)
    for who in (x_up, x_down, z_up, z_down):
        pl.semaphore_signal(barrier, inc=1, device_id=who, device_id_type=MESH)

    mine_q = queries.at[pl.ds(pl.multiple_of(c * q_rows, q_rows), q_rows)]
    loads = [
        local(mine_q, qbuf.at[s], 0),
        local(latent.at[pl.ds(c * half_req, half_req)], lbuf.at[0], 1),
        local(wg, wcat.at[:, pl.ds(0, LANE)], 2),
        local(wu, wcat.at[:, pl.ds(2 * LANE, LANE)], 3),
        local(wd, wdcat.at[pl.ds(0, LANE)], 4),
    ]

    row = lax.broadcasted_iota(jnp.int32, (LANE, routes.shape[1]), 0)
    named = jnp.where(row < experts, row, row - experts)
    weight = jnp.zeros(named.shape, F32)
    for k in range(routes.shape[0]):
        weight = weight + jnp.where(named == routes[k:k + 1, :], gates[k:k + 1, :], 0.0)
    high = weight.astype(BF16).astype(F32)
    weight = jnp.where(row < experts, high, jnp.where(row < 2 * experts, weight - high, 0.0))
    square[...] = jnp.zeros_like(square)
    square[:, 0:routes.shape[1]] = weight
    square[...] = jnp.transpose(square[...])

    pl.semaphore_wait(barrier, n_seq - 1 + 4)

    def token_copy(j):
        to = lax.rem(s + j, n_seq)
        return pltpu.make_async_remote_copy(
            src_ref=tokpad.at[lax.rem(to, 2)],
            dst_ref=tokbuf.at[s],
            send_sem=t_send.at[j],
            recv_sem=t_recv.at[j],
            device_id=(to, e),
            device_id_type=MESH,
        )

    def query_copy(j):
        to = lax.rem(s + j, n_seq)
        begin = pl.multiple_of(lax.rem(to, 2) * q_rows, q_rows)
        return pltpu.make_async_remote_copy(
            src_ref=queries.at[pl.ds(begin, q_rows)],
            dst_ref=qbuf.at[s],
            send_sem=q_send.at[j],
            recv_sem=q_recv.at[j],
            device_id=(to, e),
            device_id_type=MESH,
        )

    def end_copy(j):
        to = lax.rem(s + j, n_seq)
        return pltpu.make_async_remote_copy(
            src_ref=ebuf.at[to],
            dst_ref=erecv.at[s],
            send_sem=e_send.at[j],
            recv_sem=e_recv.at[j],
            device_id=(to, e),
            device_id_type=MESH,
        )

    def each(act):
        def body(j, carry):
            act(j)
            return carry

        lax.fori_loop(1, n_seq, body, 0)

    net = Net(send_sem, recv_sem)
    each(lambda j: token_copy(j).start())
    lat_copy, _ = net.copy(latent.at[pl.ds(other * half_req, half_req)], lbuf.at[1], sibling, "core")
    weights = [
        net.copy(src, dst, sibling, "core")[0]
        for src, dst in (
            (wg, wcat.at[:, pl.ds(LANE, LANE)]),
            (wu, wcat.at[:, pl.ds(3 * LANE, LANE)]),
            (wd, wdcat.at[pl.ds(LANE, LANE)]),
        )
    ]
    each(lambda j: query_copy(j).start())

    tokbuf[s] = tokpad[c]
    line[...] = jnp.zeros_like(line)
    first_row = pl.multiple_of(c * HALF_TOK, HALF_TOK)
    xb[0, 0, :, wide_b:wide_b + LANE] = square[pl.ds(first_row, HALF_TOK), :].astype(BF16)
    each(lambda j: token_copy(j).wait_recv())
    for i in range(n_seq):
        begin, turn = share * i // LANE * LANE, share * i % LANE
        span = tokpad.shape[2] + LANE
        value = jnp.concatenate(
            [tokbuf[i].astype(F32), jnp.zeros((HALF_TOK, LANE), F32)], axis=1
        )
        if turn:
            value = pltpu.roll(value, turn, 1)
        line[:, begin:begin + span] = line[:, begin:begin + span] + value
    xa[0, 0] = line[:, 0:wide_a].astype(BF16)
    xb[0, 0, :, 0:wide_b] = line[:, wide_a:wide_a + wide_b].astype(BF16)

    position = lax.broadcasted_iota(jnp.int32, (n_seq * heads, LANE), 1)

    def one_request(i, carry):
        head_rows = pl.ds(pl.multiple_of(i * heads, heads), heads)
        q = qf[:, head_rows, :].reshape(n_seq * heads, qf.shape[2]).astype(BF16)
        length = lengths[0, c * half_req + i]
        parts = []
        for side, base in ((0, s), (1, 2 * y + other)):
            score = jnp.dot(q, lbuf[side, i], preferred_element_type=F32) * SCALE
            valid = position + base * LANE < length
            parts.append((jnp.where(valid, score, NEG), valid))
        top = jnp.maximum(
            jnp.max(parts[0][0], axis=1, keepdims=True),
            jnp.max(parts[1][0], axis=1, keepdims=True),
        ).astype(BF16).astype(F32)
        total = jnp.zeros((n_seq * heads, 1), F32)
        context = jnp.zeros((n_seq * heads, LAT), F32)
        for side in range(2):
            score, valid = parts[side]
            w = jnp.where(valid, jnp.exp(score - top), 0.0)
            total = total + jnp.sum(w, axis=1, keepdims=True)
            context = context + lax.dot_general(
                w.astype(BF16), lbuf[side, i, 0:LAT, :], (((1,), (1,)), ((), ())),
                preferred_element_type=F32,
            )
        total_high = total.astype(BF16).astype(F32)
        note = jnp.where(
            position == 0,
            top,
            jnp.where(position == 1, total_high, jnp.where(position == 2, total - total_high, 0.0)),
        )
        at = pl.ds(pl.multiple_of(2 * heads * i, 2 * heads), 2 * heads)
        obuf[:, at, 0:LAT] = context.astype(BF16).reshape(n_y, 2 * heads, LAT)
        obuf[:, at, LAT:LAT + LANE] = note.astype(BF16).reshape(n_y, 2 * heads, LANE)
        return carry

    def one_context(i, carry):
        at = pl.ds(pl.multiple_of(2 * heads * i, 2 * heads), 2 * heads)
        head_rows = pl.ds(pl.multiple_of(i * heads, heads), heads)
        line_of = lax.broadcasted_iota(jnp.int32, fresh.shape, 0)
        chosen = jnp.where(line_of == c * half_req + i, fresh[...].astype(F32), 0.0)
        key = jnp.sum(chosen, axis=0, keepdims=True)
        q = qf[pl.ds(2 * y, 2), head_rows, :].reshape(2 * heads, qf.shape[2])
        own = jnp.sum(q * key, axis=1, keepdims=True) * SCALE
        notes = [orecv[j, at, LAT:LAT + LANE].astype(F32) for j in range(n_y)]
        top = own
        for note in notes:
            top = jnp.maximum(top, note[:, 0:1])
        w = jnp.exp(own - top)
        total, context = w, w * key[:, 0:LAT]
        for j, note in enumerate(notes):
            w = jnp.exp(note[:, 0:1] - top)
            total = total + w * (note[:, 1:2] + note[:, 2:3])
            context = context + w * orecv[j, at, 0:LAT].astype(F32)
        context = context / total
        for core in range(2):
            cf[core, head_rows, :] = context[core * heads:(core + 1) * heads]
        return carry

    def attend():
        yield net.now + 8.0
        loads[0].wait()
        loads[1].wait()
        each(lambda j: query_copy(j).wait_recv())
        lat_copy.wait_recv()
        qf[...] = qbuf[...].astype(F32)
        lax.fori_loop(0, half_req // 2, one_request, 0)
        net.now += 2.0
        yield net.now + 0.5
        lax.fori_loop(half_req // 2, half_req, one_request, 0)
        net.now += 2.0
        came = []
        for j in range(1, n_y):
            to = lax.rem(y + j, n_y)
            came.append(net.copy(obuf.at[to], orecv.at[y], (2 * to + c, e), "y"))
        orecv[y] = obuf[y]
        yield net.now + 25.0
        for one, _ in came:
            one.wait_recv()
        lax.fori_loop(0, half_req, one_context, 0)
        net.now += 1.0
        cb[...] = cf[...].astype(BF16)
        back, when = net.copy(cb.at[other], crecv, sibling, "core")
        ctx_out[pl.ds(pl.multiple_of(c * q_rows, q_rows), q_rows), :] = cb[c]
        yield when + 5.0
        back.wait_recv()
        ctx_out[pl.ds(pl.multiple_of(other * q_rows, q_rows), q_rows), :] = crecv[...]

    half_a, half_b = wide_a // 2, wide_b // 2

    def cut_a(ref, side):
        lead = (slice(None),) * (len(ref.shape) - 1)
        return ref.at[lead + (pl.ds(side * half_a, half_a),)]

    def cut_b(ref, side):
        lead = (slice(None),) * (len(ref.shape) - 1)
        size = half_b if side == 0 else ref.shape[-1] - half_b
        return ref.at[lead + (pl.ds(side * half_b, size),)]

    teams = [(0,)] + [(d, -d) for d in range(1, n_z // 2)] + [(n_z // 2,)]

    pairs = [(i, i + 1) for i in range(0, NX, 2)]

    def slots(team):
        return pl.ds(slot_z[team[0]], len(team))

    landed = {d: 0 for d in slot_z}

    def count(team):
        for d in team:
            landed[d] += 1

    def gather_a():
        here = set()

        def start(dx):
            here.add(slot_x[dx])
            for pair in pairs:
                if slot_x[dx] in pair and here.issuperset(pair):
                    net.add(net.now, along_z(pl.ds(pair[0], 2)))

        def along_z(at):
            return ring_gather(
                net, lambda d: xa.at[slot_z[d], at], cut_a, n_z, z_up, z_down, "z",
                lambda d: count((d,)),
            )

        yield from ring_gather(
            net, lambda d: xa.at[0, slot_x[d]], cut_a, NX, x_up, x_down, "x", start
        )

    def gather_b():
        here = set()

        def start(dz):
            here.add(dz)
            team = [team for team in teams if dz in team][0]
            if here.issuperset(team):
                net.add(net.now, ring_gather(
                    net, lambda d: xb.at[slots(team), slot_x[d]], cut_b, NX, x_up, x_down, "x",
                    lambda d: count(team),
                ))

        yield from ring_gather(
            net, lambda d: xb.at[slot_z[d], 0], cut_b, n_z, z_up, z_down, "z", start
        )

    step_a, step_b = wide_a // 3, wide_b // 4
    def experts_of(first, last):
        rows = (last - first) * NX * HALF_TOK

        def up_a(k, carry):
            cols = pl.ds(pl.multiple_of(k * step_a, step_a), step_a)
            value = xa[first:last, :, :, cols].reshape(rows, step_a)
            acc[0:rows, :] += jnp.dot(value, wcat[cols, :], preferred_element_type=F32)
            return carry

        def up_b(k, carry):
            cols = pl.ds(pl.multiple_of(k * step_b, step_b), step_b)
            down = pl.ds(pl.multiple_of(wide_a + k * step_b, LANE), step_b)
            value = xb[first:last, :, :, cols].reshape(rows, step_b)
            acc[0:rows, :] += jnp.dot(value, wcat[down, :], preferred_element_type=F32)
            return carry

        def down_a(k, carry):
            cols = pl.ds(pl.multiple_of(k * step_a, step_a), step_a)
            value = jnp.dot(hid[0:rows, :], wdcat[:, cols], preferred_element_type=F32)
            ya[first:last, :, :, cols] = value.astype(BF16).reshape(last - first, NX, HALF_TOK, step_a)
            return carry

        def down_b(k, carry):
            cols = pl.ds(pl.multiple_of(k * step_b, step_b), step_b)
            down = pl.ds(pl.multiple_of(wide_a + k * step_b, LANE), step_b)
            value = jnp.dot(hid[0:rows, :], wdcat[:, down], preferred_element_type=F32)
            yb[first:last, :, :, cols] = value.astype(BF16).reshape(last - first, NX, HALF_TOK, step_b)
            return carry

        acc[0:rows, :] = jnp.zeros((rows, 4 * LANE), F32)
        lax.fori_loop(0, 3, up_a, 0)
        lax.fori_loop(0, 4, up_b, 0)
        tile = xb[first:last, :, :, wide_b:wide_b + LANE].reshape(rows, LANE).astype(F32)
        lane = lax.broadcasted_iota(jnp.int32, (rows, LANE), 1)
        gate = jnp.sum(
            jnp.where((lane == e) | (lane == e + experts), tile, 0.0), axis=1, keepdims=True
        )
        g = acc[0:rows, 0:2 * LANE]
        value = g / (1.0 + jnp.exp(-g)) * acc[0:rows, 2 * LANE:4 * LANE] * gate
        hid[0:rows, :] = value.astype(BF16)
        lax.fori_loop(0, 4, down_b, 0)
        lax.fori_loop(0, 3, down_a, 0)

    def compute():
        offsets = around(n_z)
        groups = [(0, 3), (3, 5), (5, 7), (7, 8)] if n_z == 8 else [(0, len(offsets))]
        for first, last in groups:
            while any(landed[d] < len(pairs) + NX for d in offsets[first:last]):
                yield net.now + 0.01
            if first == 0:
                for load in loads[2:]:
                    load.wait()
                for made in weights:
                    made.wait_recv()
            experts_of(first, last)
            net.now += 1.0

    attention = attend()
    net.run([gather_a(), gather_b(), sample(attention, 3), compute()])

    net.links, net.now = {}, 0.0
    ended = set()

    def always(d):
        return True

    def row_sum(team):
        at = slots(team)

        def finish(total):
            yb[at, 0] = total.astype(BF16)
            ended.update(team)

        return ring_scatter(
            net, lambda d: yb.at[at, slot_x[d]], cut_b, lambda way, k: rbx.at[way, k, at],
            NX, x_up, x_down, "x", always, finish,
        )

    done_a = set()

    def column_sum(pair):
        at = pl.ds(pair[0], 2)

        def finish(total):
            ya[0, at] = total.astype(BF16)
            done_a.update(pair)

        return ring_scatter(
            net, lambda d: ya.at[slot_z[d], at], cut_a, lambda way, k: ra.at[way, k, at],
            n_z, z_up, z_down, "z", always, finish,
        )

    def end_a(total):
        line[:, 0:wide_a] = total

    def end_b(total):
        line[:, wide_a:wide_a + wide_b] = total

    sum_a = ring_scatter(
        net, lambda d: ya.at[0, slot_x[d]], cut_a, lambda way, k: rax.at[way, k],
        NX, x_up, x_down, "x", lambda d: slot_x[far_x if d == -far_x else d] in done_a, end_a,
    )

    sum_b = ring_scatter(
        net, lambda d: yb.at[slot_z[d], 0], cut_b, lambda way, k: rb.at[way, k],
        n_z, z_up, z_down, "z", lambda d: d in ended, end_b,
    )
    before = list(net.copies)

    def settle():
        yield net.now + 1.0
        each(lambda j: token_copy(j).wait_send())
        each(lambda j: query_copy(j).wait_send())
        for made in before:
            made.wait_send()

    first_rows = [row_sum(team) for team in reversed(teams)]
    columns = [column_sum(pair) for pair in reversed(pairs)]
    net.run(first_rows[:1] + columns + first_rows[1:] + [sum_a, sum_b, sample(attention, 9), settle()])

    for i in range(n_seq):
        begin, turn = share * i // LANE * LANE, share * i % LANE
        span = tokpad.shape[2] + LANE
        value = line[:, begin:begin + span]
        if turn:
            value = pltpu.roll(value, span - turn, 1)
        ebuf[i] = value[:, 0:tokpad.shape[2]].astype(BF16)
    each(lambda j: end_copy(j).start())
    erecv[s] = ebuf[s]
    each(lambda j: end_copy(j).wait_recv())
    for half in range(2):
        total = erecv[half].astype(F32)
        for i in range(1, n_y):
            total = total + erecv[2 * i + half].astype(F32)
        mix_out[half * HALF_TOK:(half + 1) * HALF_TOK, :] = total[:, 0:share].astype(BF16)

    each(lambda j: end_copy(j).wait_send())
    for made in net.copies[len(before):]:
        made.wait_send()


def sample(task, most):
    for _ in range(most):
        try:
            ready = next(task)
        except StopIteration:
            return
        yield ready


def on_device(latent, lengths, queries, fresh_latent, tokens, routes, gates, w_gate, w_up, w_down):
    n_seq, n_ep = lax.axis_size("seq"), lax.axis_size("ep")
    n_z, n_y = n_ep // NX, n_seq // 2
    n_req, heads, width = queries.shape
    share = tokens.shape[1]
    features = share * n_seq
    wide_a = features // 7 * 3
    wide_b = features - wide_a
    padded = -(-share // LANE) * LANE
    rows = n_ep * HALF_TOK
    half_req = n_req // 2
    q_rows = half_req * heads
    far_z, far_x = n_z // 2, NX // 2
    cfg = (n_seq, n_z, wide_a, wide_b, share, heads)
    vmem = pl.BlockSpec(memory_space=pltpu.VMEM)
    hbm = pl.BlockSpec(memory_space=pl.ANY)
    dma = pltpu.SemaphoreType.DMA
    ffn = 2 * rows * features * 6 * LANE
    context, mixed = pl.pallas_call(
        functools.partial(kernel, cfg),
        out_shape=(
            jax.ShapeDtypeStruct((n_req * heads, LAT), BF16),
            jax.ShapeDtypeStruct(tokens.shape, BF16),
        ),
        in_specs=[hbm, hbm, hbm, hbm, hbm, pl.BlockSpec(memory_space=pltpu.SMEM), vmem, vmem, vmem, vmem],
        out_specs=(vmem, vmem),
        scratch_shapes=[
            pltpu.VMEM((2, HALF_TOK, padded), BF16),
            pltpu.VMEM((n_seq, HALF_TOK, padded), BF16),
            pltpu.VMEM((HALF_TOK, features + 2 * LANE), F32),
            pltpu.VMEM((LANE, LANE), F32),
            pltpu.VMEM((n_z, NX, HALF_TOK, wide_a), BF16),
            pltpu.VMEM((n_z, NX, HALF_TOK, wide_b + LANE), BF16),
            pltpu.VMEM((features, 4 * LANE), BF16),
            pltpu.VMEM((2 * LANE, features), BF16),
            pltpu.VMEM((rows, 4 * LANE), F32),
            pltpu.VMEM((rows, 2 * LANE), BF16),
            pltpu.VMEM((n_z, NX, HALF_TOK, wide_a), BF16),
            pltpu.VMEM((n_z, NX, HALF_TOK, wide_b), BF16),
            pltpu.VMEM((2, far_z, NX, HALF_TOK, wide_a), BF16),
            pltpu.VMEM((2, far_x, HALF_TOK, wide_a), BF16),
            pltpu.VMEM((2, far_x, n_z, HALF_TOK, wide_b), BF16),
            pltpu.VMEM((2, far_z, HALF_TOK, wide_b), BF16),
            pltpu.VMEM((n_seq, HALF_TOK, padded), BF16),
            pltpu.VMEM((n_seq, HALF_TOK, padded), BF16),
            pltpu.VMEM((2, half_req, width, LANE), BF16),
            pltpu.VMEM((n_seq, q_rows, width), BF16),
            pltpu.VMEM((n_seq, q_rows, width), F32),
            pltpu.VMEM((n_y, 2 * q_rows, LAT + LANE), BF16),
            pltpu.VMEM((n_y, 2 * q_rows, LAT + LANE), BF16),
            pltpu.VMEM((2, q_rows, LAT), F32),
            pltpu.VMEM((2, q_rows, LAT), BF16),
            pltpu.VMEM((q_rows, LAT), BF16),
            dma((5,)),
            dma((120,)),
            dma((120,)),
            dma((n_seq,)),
            dma((n_seq,)),
            dma((n_seq,)),
            dma((n_seq,)),
            dma((n_seq,)),
            dma((n_seq,)),
        ],
        compiler_params=pltpu.CompilerParams(
            collective_id=0, has_side_effects=True, vmem_limit_bytes=56 * 1024 * 1024
        ),
        cost_estimate=pl.CostEstimate(flops=ffn, bytes_accessed=6 * 2**20, transcendentals=rows * 512),
    )(
        latent.transpose(0, 2, 1),
        queries.reshape(n_req * heads, width),
        w_gate[0],
        w_up[0],
        w_down[0],
        lengths,
        fresh_latent,
        tokens,
        routes.T,
        gates.T,
    )
    return context.reshape(n_req, heads, LAT), mixed


def solution(mesh):
    placed = (
        P("ep", "seq", None),
        P("ep", None),
        P("ep", "seq", None),
        P("ep", None),
        P("ep", "seq"),
        P("ep", None),
        P("ep", None),
        P("ep", None, "seq"),
        P("ep", None, "seq"),
        P("ep", "seq", None),
    )
    return jax.shard_map(
        on_device,
        mesh=mesh,
        in_specs=placed,
        out_specs=(P("ep", "seq", None), P("ep", "seq")),
        check_vma=False,
    )
```

```python
import functools
import heapq

import jax
import jax.numpy as jnp
from jax import lax
from jax.experimental import pallas as pl
from jax.experimental.pallas import tpu as pltpu
from jax.sharding import PartitionSpec as P

MESH = pl.DeviceIdType.MESH
LAT = 512
NX = 4
LANE = 128
HALF_TOK = 16
SCALE = 0.07216878364870322
NEG = -1.0e30
F32 = jnp.float32
BF16 = jnp.bfloat16

LINK_RATE = 45.0e3
HOP = 1.5


def mod(value, n):
    return lax.rem(value + n, n)


class Net:
    def __init__(self, send, recv):
        self.send, self.recv = send, recv
        self.count, self.now = 0, 0.0
        self.links, self.copies = {}, []

    def copy(self, src, dst, device, link, hops=1):
        at = self.count
        self.count += 1
        made = pltpu.make_async_remote_copy(
            src_ref=src,
            dst_ref=dst,
            send_sem=self.send.at[at],
            recv_sem=self.recv.at[at],
            device_id=device,
            device_id_type=MESH,
        )
        made.start()
        size = 2 * hops
        for extent in src.shape:
            size *= extent
        begin = max(self.links.get(link, 0.0), self.now)
        self.links[link] = begin + size / LINK_RATE
        self.copies.append(made)
        return made, self.links[link] + HOP

    def run(self, tasks):
        self.heap, self.order = [], 0
        for task in tasks:
            self.add(self.now, task)
        while self.heap:
            at, _, task = heapq.heappop(self.heap)
            self.now = max(self.now, at)
            try:
                ready = next(task)
            except StopIteration:
                continue
            self.add(ready, task)

    def add(self, at, task):
        self.order += 1
        heapq.heappush(self.heap, (at, self.order, task))


def around(n):
    offsets = [0]
    for k in range(1, n // 2):
        offsets += [k, -k]
    return offsets + [n // 2]


def ring_gather(net, piece, cut, n, up, down, axis, landed):
    far = n // 2

    def pass_on(side, k):
        src, dst = piece((k, -k)[1 - side]), piece(far if k + 1 == far else (k + 1, -k - 1)[1 - side])
        if k + 1 == far:
            src, dst = cut(src, side), cut(dst, side)
        return net.copy(src, dst, (up, down)[side], axis + "+-"[side])

    cu, tu = pass_on(0, 0)
    cd, td = pass_on(1, 0)
    landed(0)
    for k in range(1, far):
        yield tu
        cu.wait_recv()
        cu, tu = pass_on(0, k)
        landed(-k)
        yield td
        cd.wait_recv()
        cd, td = pass_on(1, k)
        landed(k)
    yield max(tu, td)
    cu.wait_recv()
    cd.wait_recv()
    landed(far)


def skip_gather(net, piece, cut, ups, downs, axis, landed):
    def send(src, at, way, hops, side=None):
        dst = piece(at)
        if side is not None:
            src, dst = cut(src, side), cut(dst, side)
        return net.copy(src, dst, way[hops - 1], axis + ("+" if way is ups else "-"), hops)

    c2u, t2u = send(piece(0), -2, ups, 2)
    c2d, t2d = send(piece(0), 2, downs, 2)
    c1u, t1u = send(piece(0), -1, ups, 1)
    c1d, t1d = send(piece(0), 1, downs, 1)
    landed(0)
    yield t2u
    c2u.wait_recv()
    c4u, t4u = send(piece(-2), 4, ups, 2, 0)
    c3u, t3u = send(piece(-2), -3, ups, 1)
    landed(-2)
    yield t2d
    c2d.wait_recv()
    c4d, t4d = send(piece(2), 4, downs, 2, 1)
    c3d, t3d = send(piece(2), 3, downs, 1)
    landed(2)
    yield t1u
    c1u.wait_recv()
    landed(-1)
    yield t1d
    c1d.wait_recv()
    landed(1)
    yield max(t3u, t3d)
    c3u.wait_recv()
    landed(-3)
    c3d.wait_recv()
    landed(3)
    yield max(t4u, t4d)
    c4u.wait_recv()
    c4d.wait_recv()
    landed(4)


def skip_scatter(net, piece, cut, arrived, ups, downs, axis, ready, finish):
    up, down = axis + "+", axis + "-"
    while not (ready(4) and ready(3) and ready(-3)):
        yield net.now + 0.01
    c4u, t4u = net.copy(cut(piece(4), 0), cut(arrived(0, 0), 0), ups[1], up, 2)
    c4d, t4d = net.copy(cut(piece(4), 1), cut(arrived(1, 0), 1), downs[1], down, 2)
    c3u, t3u = net.copy(piece(3), arrived(0, 1), ups[0], up)
    c3d, t3d = net.copy(piece(-3), arrived(1, 1), downs[0], down)
    while not (ready(2) and ready(-2)):
        yield net.now + 0.01
    yield max(t4u, t3u)
    c4u.wait_recv()
    c3u.wait_recv()
    add_into(cut(piece(2), 0), cut(arrived(0, 0), 0))
    add_into(piece(2), arrived(0, 1))
    c2u, t2u = net.copy(piece(2), arrived(0, 2), ups[1], up, 2)
    yield max(t4d, t3d)
    c4d.wait_recv()
    c3d.wait_recv()
    add_into(cut(piece(-2), 1), cut(arrived(1, 0), 1))
    add_into(piece(-2), arrived(1, 1))
    c2d, t2d = net.copy(piece(-2), arrived(1, 2), downs[1], down, 2)
    while not (ready(1) and ready(-1)):
        yield net.now + 0.01
    c1u, t1u = net.copy(piece(1), arrived(0, 3), ups[0], up)
    c1d, t1d = net.copy(piece(-1), arrived(1, 3), downs[0], down)
    while not ready(0):
        yield net.now + 0.01
    yield max(t2u, t2d, t1u, t1d)
    total = piece(0)[...].astype(F32)
    for k, (one, two) in ((3, (c1u, c1d)), (2, (c2u, c2d))):
        one.wait_recv()
        two.wait_recv()
        total = total + arrived(0, k)[...].astype(F32) + arrived(1, k)[...].astype(F32)
    finish(total)


def add_into(ref, other):
    ref[...] = ref[...] + other[...]


def ring_scatter(net, piece, cut, arrived, n, up, down, axis, ready, finish):
    far = n // 2
    while not ready(far):
        yield net.now + 0.01
    cu, tu = net.copy(cut(piece(far), 0), cut(arrived(0, 0), 0), up, axis + "+")
    cd, td = net.copy(cut(piece(far), 1), cut(arrived(1, 0), 1), down, axis + "-")
    for k in range(1, far):
        d = far - k
        while not (ready(d) and ready(-d)):
            yield net.now + 0.01
        yield tu
        cu.wait_recv()
        mine, came = piece(d), arrived(0, k - 1)
        if k == 1:
            mine, came = cut(mine, 0), cut(came, 0)
        add_into(mine, came)
        cu, tu = net.copy(piece(d), arrived(0, k), up, axis + "+")
        yield td
        cd.wait_recv()
        mine, came = piece(-d), arrived(1, k - 1)
        if k == 1:
            mine, came = cut(mine, 1), cut(came, 1)
        add_into(mine, came)
        cd, td = net.copy(piece(-d), arrived(1, k), down, axis + "-")
    while not ready(0):
        yield net.now + 0.01
    yield max(tu, td)
    cu.wait_recv()
    cd.wait_recv()
    if far == 1:
        add_into(cut(piece(0), 0), cut(arrived(0, 0), 0))
        add_into(cut(piece(0), 1), cut(arrived(1, 0), 1))
        finish(piece(0)[...].astype(F32))
    else:
        finish(
            piece(0)[...].astype(F32)
            + arrived(0, far - 1)[...].astype(F32)
            + arrived(1, far - 1)[...].astype(F32)
        )


def kernel(
    cfg,
    latent, queries, wg, wu, wd, lengths, fresh, tokens, routes, gates,
    ctx_out, mix_out,
    tokpad, tokbuf, line, square, xa, xb, wcat, wdcat, acc, hid, ya, yb,
    ra, rax, rbx, rb, ebuf, erecv,
    lbuf, qbuf, qf, obuf, orecv, cf, cb, crecv,
    local_sem, send_sem, recv_sem, t_send, t_recv, q_send, q_recv, e_send, e_recv,
):
    n_seq, n_z, wide_a, wide_b, share, heads = cfg
    n_y = n_seq // 2
    s, e = lax.axis_index("seq"), lax.axis_index("ep")
    y, c = s // 2, lax.rem(s, 2)
    z, x = e // NX, lax.rem(e, NX)
    other = 1 - c
    sibling = (2 * y + other, e)
    experts = n_z * NX
    far_x = NX // 2
    n_req = lengths.shape[1]
    half_req = n_req // 2
    q_rows = half_req * heads
    x_up, x_down = (s, z * NX + mod(x + 1, NX)), (s, z * NX + mod(x - 1, NX))
    z_up, z_down = (s, mod(z + 1, n_z) * NX + x), (s, mod(z - 1, n_z) * NX + x)
    z_ups = (z_up, (s, mod(z + 2, n_z) * NX + x))
    z_downs = (z_down, (s, mod(z - 2, n_z) * NX + x))
    slot_z = {d: i for i, d in enumerate(around(n_z))}
    slot_x = {d: i for i, d in enumerate(around(NX))}

    def local(src, dst, i):
        made = pltpu.make_async_copy(src, dst, local_sem.at[i])
        made.start()
        return made

    for half in range(2):
        tokpad[half] = jnp.zeros_like(tokpad[half])
        tokpad[half, :, 0:share] = tokens[half * HALF_TOK:(half + 1) * HALF_TOK, :]

    barrier = pltpu.get_barrier_semaphore()

    def greet(j, carry):
        pl.semaphore_signal(
            barrier, inc=1, device_id=(lax.rem(s + j, n_seq), e), device_id_type=MESH
        )
        return carry

    lax.fori_loop(1, n_seq, greet, 0)
    for who in (x_up, x_down) + z_ups + z_downs:
        pl.semaphore_signal(barrier, inc=1, device_id=who, device_id_type=MESH)

    mine_q = queries.at[pl.ds(pl.multiple_of(c * q_rows, q_rows), q_rows)]
    loads = [
        local(mine_q, qbuf.at[s], 0),
        local(latent.at[pl.ds(c * half_req, half_req)], lbuf.at[0], 1),
        local(wg, wcat.at[:, pl.ds(0, LANE)], 2),
        local(wu, wcat.at[:, pl.ds(2 * LANE, LANE)], 3),
        local(wd, wdcat.at[pl.ds(0, LANE)], 4),
    ]

    row = lax.broadcasted_iota(jnp.int32, (LANE, routes.shape[1]), 0)
    named = jnp.where(row < experts, row, row - experts)
    weight = jnp.zeros(named.shape, F32)
    for k in range(routes.shape[0]):
        weight = weight + jnp.where(named == routes[k:k + 1, :], gates[k:k + 1, :], 0.0)
    high = weight.astype(BF16).astype(F32)
    weight = jnp.where(row < experts, high, jnp.where(row < 2 * experts, weight - high, 0.0))
    square[...] = jnp.zeros_like(square)
    square[:, 0:routes.shape[1]] = weight
    square[...] = jnp.transpose(square[...])

    pl.semaphore_wait(barrier, n_seq - 1 + 6)

    def token_copy(j):
        to = lax.rem(s + j, n_seq)
        return pltpu.make_async_remote_copy(
            src_ref=tokpad.at[lax.rem(to, 2)],
            dst_ref=tokbuf.at[s],
            send_sem=t_send.at[j],
            recv_sem=t_recv.at[j],
            device_id=(to, e),
            device_id_type=MESH,
        )

    def query_copy(j):
        to = lax.rem(s + j, n_seq)
        begin = pl.multiple_of(lax.rem(to, 2) * q_rows, q_rows)
        return pltpu.make_async_remote_copy(
            src_ref=queries.at[pl.ds(begin, q_rows)],
            dst_ref=qbuf.at[s],
            send_sem=q_send.at[j],
            recv_sem=q_recv.at[j],
            device_id=(to, e),
            device_id_type=MESH,
        )

    def end_copy(j):
        to = lax.rem(s + j, n_seq)
        return pltpu.make_async_remote_copy(
            src_ref=ebuf.at[to],
            dst_ref=erecv.at[s],
            send_sem=e_send.at[j],
            recv_sem=e_recv.at[j],
            device_id=(to, e),
            device_id_type=MESH,
        )

    def each(act):
        def body(j, carry):
            act(j)
            return carry

        lax.fori_loop(1, n_seq, body, 0)

    net = Net(send_sem, recv_sem)
    each(lambda j: token_copy(j).start())
    lat_copy, _ = net.copy(latent.at[pl.ds(other * half_req, half_req)], lbuf.at[1], sibling, "core")
    weights = [
        net.copy(src, dst, sibling, "core")[0]
        for src, dst in (
            (wg, wcat.at[:, pl.ds(LANE, LANE)]),
            (wu, wcat.at[:, pl.ds(3 * LANE, LANE)]),
            (wd, wdcat.at[pl.ds(LANE, LANE)]),
        )
    ]
    each(lambda j: query_copy(j).start())

    tokbuf[s] = tokpad[c]
    line[...] = jnp.zeros_like(line)
    first_row = pl.multiple_of(c * HALF_TOK, HALF_TOK)
    xb[0, 0, :, wide_b:wide_b + LANE] = square[pl.ds(first_row, HALF_TOK), :].astype(BF16)
    each(lambda j: token_copy(j).wait_recv())
    for i in range(n_seq):
        begin, turn = share * i // LANE * LANE, share * i % LANE
        span = tokpad.shape[2] + LANE
        value = jnp.concatenate(
            [tokbuf[i].astype(F32), jnp.zeros((HALF_TOK, LANE), F32)], axis=1
        )
        if turn:
            value = pltpu.roll(value, turn, 1)
        line[:, begin:begin + span] = line[:, begin:begin + span] + value
    xa[0, 0] = line[:, 0:wide_a].astype(BF16)
    xb[0, 0, :, 0:wide_b] = line[:, wide_a:wide_a + wide_b].astype(BF16)

    position = lax.broadcasted_iota(jnp.int32, (n_seq * heads, LANE), 1)

    def one_request(i, carry):
        head_rows = pl.ds(pl.multiple_of(i * heads, heads), heads)
        q = qf[:, head_rows, :].reshape(n_seq * heads, qf.shape[2]).astype(BF16)
        length = lengths[0, c * half_req + i]
        parts = []
        for side, base in ((0, s), (1, 2 * y + other)):
            score = jnp.dot(q, lbuf[side, i], preferred_element_type=F32) * SCALE
            valid = position + base * LANE < length
            parts.append((jnp.where(valid, score, NEG), valid))
        top = jnp.maximum(
            jnp.max(parts[0][0], axis=1, keepdims=True),
            jnp.max(parts[1][0], axis=1, keepdims=True),
        ).astype(BF16).astype(F32)
        total = jnp.zeros((n_seq * heads, 1), F32)
        context = jnp.zeros((n_seq * heads, LAT), F32)
        for side in range(2):
            score, valid = parts[side]
            w = jnp.where(valid, jnp.exp(score - top), 0.0)
            total = total + jnp.sum(w, axis=1, keepdims=True)
            context = context + lax.dot_general(
                w.astype(BF16), lbuf[side, i, 0:LAT, :], (((1,), (1,)), ((), ())),
                preferred_element_type=F32,
            )
        total_high = total.astype(BF16).astype(F32)
        note = jnp.where(
            position == 0,
            top,
            jnp.where(position == 1, total_high, jnp.where(position == 2, total - total_high, 0.0)),
        )
        at = pl.ds(pl.multiple_of(2 * heads * i, 2 * heads), 2 * heads)
        obuf[:, at, 0:LAT] = context.astype(BF16).reshape(n_y, 2 * heads, LAT)
        obuf[:, at, LAT:LAT + LANE] = note.astype(BF16).reshape(n_y, 2 * heads, LANE)
        return carry

    def one_context(i, carry):
        at = pl.ds(pl.multiple_of(2 * heads * i, 2 * heads), 2 * heads)
        head_rows = pl.ds(pl.multiple_of(i * heads, heads), heads)
        line_of = lax.broadcasted_iota(jnp.int32, fresh.shape, 0)
        chosen = jnp.where(line_of == c * half_req + i, fresh[...].astype(F32), 0.0)
        key = jnp.sum(chosen, axis=0, keepdims=True)
        q = qf[pl.ds(2 * y, 2), head_rows, :].reshape(2 * heads, qf.shape[2])
        own = jnp.sum(q * key, axis=1, keepdims=True) * SCALE
        notes = [orecv[j, at, LAT:LAT + LANE].astype(F32) for j in range(n_y)]
        top = own
        for note in notes:
            top = jnp.maximum(top, note[:, 0:1])
        w = jnp.exp(own - top)
        total, context = w, w * key[:, 0:LAT]
        for j, note in enumerate(notes):
            w = jnp.exp(note[:, 0:1] - top)
            total = total + w * (note[:, 1:2] + note[:, 2:3])
            context = context + w * orecv[j, at, 0:LAT].astype(F32)
        context = context / total
        for core in range(2):
            cf[core, head_rows, :] = context[core * heads:(core + 1) * heads]
        return carry

    def attend():
        yield net.now + 8.0
        loads[0].wait()
        loads[1].wait()
        each(lambda j: query_copy(j).wait_recv())
        lat_copy.wait_recv()
        qf[...] = qbuf[...].astype(F32)
        lax.fori_loop(0, half_req // 2, one_request, 0)
        net.now += 2.0
        yield net.now + 0.5
        lax.fori_loop(half_req // 2, half_req, one_request, 0)
        net.now += 2.0
        came = []
        for j in range(1, n_y):
            to = lax.rem(y + j, n_y)
            came.append(net.copy(obuf.at[to], orecv.at[y], (2 * to + c, e), "y"))
        orecv[y] = obuf[y]
        yield net.now + 25.0
        for one, _ in came:
            one.wait_recv()
        lax.fori_loop(0, half_req, one_context, 0)
        net.now += 1.0
        cb[...] = cf[...].astype(BF16)
        back, when = net.copy(cb.at[other], crecv, sibling, "core")
        ctx_out[pl.ds(pl.multiple_of(c * q_rows, q_rows), q_rows), :] = cb[c]
        yield when + 5.0
        back.wait_recv()
        ctx_out[pl.ds(pl.multiple_of(other * q_rows, q_rows), q_rows), :] = crecv[...]

    half_a, half_b = wide_a // 2, wide_b // 2

    def cut_a(ref, side):
        lead = (slice(None),) * (len(ref.shape) - 1)
        return ref.at[lead + (pl.ds(side * half_a, half_a),)]

    def cut_b(ref, side):
        lead = (slice(None),) * (len(ref.shape) - 1)
        size = half_b if side == 0 else ref.shape[-1] - half_b
        return ref.at[lead + (pl.ds(side * half_b, size),)]

    teams = [(0,)] + [(d, -d) for d in range(1, n_z // 2)] + [(n_z // 2,)]

    pairs = [(i, i + 1) for i in range(0, NX, 2)]

    def slots(team):
        return pl.ds(slot_z[team[0]], len(team))

    def gather_z(piece, cut, done):
        if n_z == 8:
            return skip_gather(net, piece, cut, z_ups, z_downs, "z", done)
        return ring_gather(net, piece, cut, n_z, z_up, z_down, "z", done)

    def scatter_z(piece, cut, arrived, ready, finish):
        if n_z == 8:
            return skip_scatter(net, piece, cut, arrived, z_ups, z_downs, "z", ready, finish)
        return ring_scatter(net, piece, cut, arrived, n_z, z_up, z_down, "z", ready, finish)

    landed = {d: 0 for d in slot_z}

    def count(team):
        for d in team:
            landed[d] += 1

    def gather_a():
        here = set()

        def start(dx):
            here.add(slot_x[dx])
            for pair in pairs:
                if slot_x[dx] in pair and here.issuperset(pair):
                    net.add(net.now, along_z(pl.ds(pair[0], 2)))

        def along_z(at):
            return gather_z(lambda d: xa.at[slot_z[d], at], cut_a, lambda d: count((d,)))

        yield from ring_gather(
            net, lambda d: xa.at[0, slot_x[d]], cut_a, NX, x_up, x_down, "x", start
        )

    def gather_b():
        here = set()

        def start(dz):
            here.add(dz)
            team = [team for team in teams if dz in team][0]
            if here.issuperset(team):
                net.add(net.now, ring_gather(
                    net, lambda d: xb.at[slots(team), slot_x[d]], cut_b, NX, x_up, x_down, "x",
                    lambda d: count(team),
                ))

        yield from gather_z(lambda d: xb.at[slot_z[d], 0], cut_b, start)

    step_a, step_b = wide_a // 2, wide_b // 5
    def experts_of(first, last):
        rows = (last - first) * NX * HALF_TOK

        def up_a(k, carry):
            cols = pl.ds(pl.multiple_of(k * step_a, step_a), step_a)
            value = xa[first:last, :, :, cols].reshape(rows, step_a)
            acc[0:rows, :] += jnp.dot(value, wcat[cols, :], preferred_element_type=F32)
            return carry

        def up_b(k, carry):
            cols = pl.ds(pl.multiple_of(k * step_b, step_b), step_b)
            down = pl.ds(pl.multiple_of(wide_a + k * step_b, LANE), step_b)
            value = xb[first:last, :, :, cols].reshape(rows, step_b)
            acc[0:rows, :] += jnp.dot(value, wcat[down, :], preferred_element_type=F32)
            return carry

        def down_a(k, carry):
            cols = pl.ds(pl.multiple_of(k * step_a, step_a), step_a)
            value = jnp.dot(hid[0:rows, :], wdcat[:, cols], preferred_element_type=F32)
            ya[first:last, :, :, cols] = value.astype(BF16).reshape(last - first, NX, HALF_TOK, step_a)
            return carry

        def down_b(k, carry):
            cols = pl.ds(pl.multiple_of(k * step_b, step_b), step_b)
            down = pl.ds(pl.multiple_of(wide_a + k * step_b, LANE), step_b)
            value = jnp.dot(hid[0:rows, :], wdcat[:, down], preferred_element_type=F32)
            yb[first:last, :, :, cols] = value.astype(BF16).reshape(last - first, NX, HALF_TOK, step_b)
            return carry

        acc[0:rows, :] = jnp.zeros((rows, 4 * LANE), F32)
        lax.fori_loop(0, 2, up_a, 0)
        lax.fori_loop(0, 5, up_b, 0)
        tile = xb[first:last, :, :, wide_b:wide_b + LANE].reshape(rows, LANE).astype(F32)
        lane = lax.broadcasted_iota(jnp.int32, (rows, LANE), 1)
        gate = jnp.sum(
            jnp.where((lane == e) | (lane == e + experts), tile, 0.0), axis=1, keepdims=True
        )
        g = acc[0:rows, 0:2 * LANE]
        value = g / (1.0 + jnp.exp(-g)) * acc[0:rows, 2 * LANE:4 * LANE] * gate
        hid[0:rows, :] = value.astype(BF16)
        lax.fori_loop(0, 5, down_b, 0)
        lax.fori_loop(0, 2, down_a, 0)

    def compute():
        offsets = around(n_z)
        groups = [(0, 5), (5, 8)] if n_z == 8 else [(0, len(offsets))]
        for first, last in groups:
            while any(landed[d] < len(pairs) + NX for d in offsets[first:last]):
                yield net.now + 0.01
            if first == 0:
                for load in loads[2:]:
                    load.wait()
                for made in weights:
                    made.wait_recv()
            experts_of(first, last)
            net.now += 1.0

    attention = attend()
    net.run([gather_a(), gather_b(), sample(attention, 3), compute()])

    net.links, net.now = {}, 0.0
    ended = set()

    def always(d):
        return True

    def row_sum(team):
        at = slots(team)

        def finish(total):
            yb[at, 0] = total.astype(BF16)
            ended.update(team)

        return ring_scatter(
            net, lambda d: yb.at[at, slot_x[d]], cut_b, lambda way, k: rbx.at[way, k, at],
            NX, x_up, x_down, "x", always, finish,
        )

    done_a = set()

    def column_sum(pair):
        at = pl.ds(pair[0], 2)

        def finish(total):
            ya[0, at] = total.astype(BF16)
            done_a.update(pair)

        return scatter_z(
            lambda d: ya.at[slot_z[d], at], cut_a, lambda way, k: ra.at[way, k, at], always, finish
        )

    def end_a(total):
        line[:, 0:wide_a] = total

    def end_b(total):
        line[:, wide_a:wide_a + wide_b] = total

    sum_a = ring_scatter(
        net, lambda d: ya.at[0, slot_x[d]], cut_a, lambda way, k: rax.at[way, k],
        NX, x_up, x_down, "x", lambda d: slot_x[far_x if d == -far_x else d] in done_a, end_a,
    )

    sum_b = scatter_z(
        lambda d: yb.at[slot_z[d], 0], cut_b, lambda way, k: rb.at[way, k],
        lambda d: d in ended, end_b,
    )
    before = list(net.copies)

    def settle():
        yield net.now + 1.0
        each(lambda j: token_copy(j).wait_send())
        each(lambda j: query_copy(j).wait_send())
        for made in before:
            made.wait_send()

    first_rows = [row_sum(team) for team in reversed(teams)]
    columns = [column_sum(pair) for pair in reversed(pairs)]
    net.run(first_rows[:1] + columns + first_rows[1:] + [sum_a, sum_b, sample(attention, 9), settle()])

    for i in range(n_seq):
        begin, turn = share * i // LANE * LANE, share * i % LANE
        span = tokpad.shape[2] + LANE
        value = line[:, begin:begin + span]
        if turn:
            value = pltpu.roll(value, span - turn, 1)
        ebuf[i] = value[:, 0:tokpad.shape[2]].astype(BF16)
    each(lambda j: end_copy(j).start())
    erecv[s] = ebuf[s]
    each(lambda j: end_copy(j).wait_recv())
    for half in range(2):
        total = erecv[half].astype(F32)
        for i in range(1, n_y):
            total = total + erecv[2 * i + half].astype(F32)
        mix_out[half * HALF_TOK:(half + 1) * HALF_TOK, :] = total[:, 0:share].astype(BF16)

    each(lambda j: end_copy(j).wait_send())
    for made in net.copies[len(before):]:
        made.wait_send()


def sample(task, most):
    for _ in range(most):
        try:
            ready = next(task)
        except StopIteration:
            return
        yield ready


def on_device(latent, lengths, queries, fresh_latent, tokens, routes, gates, w_gate, w_up, w_down):
    n_seq, n_ep = lax.axis_size("seq"), lax.axis_size("ep")
    n_z, n_y = n_ep // NX, n_seq // 2
    n_req, heads, width = queries.shape
    share = tokens.shape[1]
    features = share * n_seq
    wide_a = features // 7 * 2
    wide_b = features - wide_a
    padded = -(-share // LANE) * LANE
    rows = n_ep * HALF_TOK
    half_req = n_req // 2
    q_rows = half_req * heads
    far_z, far_x = n_z // 2, NX // 2
    cfg = (n_seq, n_z, wide_a, wide_b, share, heads)
    vmem = pl.BlockSpec(memory_space=pltpu.VMEM)
    hbm = pl.BlockSpec(memory_space=pl.ANY)
    dma = pltpu.SemaphoreType.DMA
    ffn = 2 * rows * features * 6 * LANE
    context, mixed = pl.pallas_call(
        functools.partial(kernel, cfg),
        out_shape=(
            jax.ShapeDtypeStruct((n_req * heads, LAT), BF16),
            jax.ShapeDtypeStruct(tokens.shape, BF16),
        ),
        in_specs=[hbm, hbm, hbm, hbm, hbm, pl.BlockSpec(memory_space=pltpu.SMEM), vmem, vmem, vmem, vmem],
        out_specs=(vmem, vmem),
        scratch_shapes=[
            pltpu.VMEM((2, HALF_TOK, padded), BF16),
            pltpu.VMEM((n_seq, HALF_TOK, padded), BF16),
            pltpu.VMEM((HALF_TOK, features + 2 * LANE), F32),
            pltpu.VMEM((LANE, LANE), F32),
            pltpu.VMEM((n_z, NX, HALF_TOK, wide_a), BF16),
            pltpu.VMEM((n_z, NX, HALF_TOK, wide_b + LANE), BF16),
            pltpu.VMEM((features, 4 * LANE), BF16),
            pltpu.VMEM((2 * LANE, features), BF16),
            pltpu.VMEM((rows, 4 * LANE), F32),
            pltpu.VMEM((rows, 2 * LANE), BF16),
            pltpu.VMEM((n_z, NX, HALF_TOK, wide_a), BF16),
            pltpu.VMEM((n_z, NX, HALF_TOK, wide_b), BF16),
            pltpu.VMEM((2, far_z, NX, HALF_TOK, wide_a), BF16),
            pltpu.VMEM((2, far_x, HALF_TOK, wide_a), BF16),
            pltpu.VMEM((2, far_x, n_z, HALF_TOK, wide_b), BF16),
            pltpu.VMEM((2, far_z, HALF_TOK, wide_b), BF16),
            pltpu.VMEM((n_seq, HALF_TOK, padded), BF16),
            pltpu.VMEM((n_seq, HALF_TOK, padded), BF16),
            pltpu.VMEM((2, half_req, width, LANE), BF16),
            pltpu.VMEM((n_seq, q_rows, width), BF16),
            pltpu.VMEM((n_seq, q_rows, width), F32),
            pltpu.VMEM((n_y, 2 * q_rows, LAT + LANE), BF16),
            pltpu.VMEM((n_y, 2 * q_rows, LAT + LANE), BF16),
            pltpu.VMEM((2, q_rows, LAT), F32),
            pltpu.VMEM((2, q_rows, LAT), BF16),
            pltpu.VMEM((q_rows, LAT), BF16),
            dma((5,)),
            dma((120,)),
            dma((120,)),
            dma((n_seq,)),
            dma((n_seq,)),
            dma((n_seq,)),
            dma((n_seq,)),
            dma((n_seq,)),
            dma((n_seq,)),
        ],
        compiler_params=pltpu.CompilerParams(
            collective_id=0, has_side_effects=True, vmem_limit_bytes=56 * 1024 * 1024
        ),
        cost_estimate=pl.CostEstimate(flops=ffn, bytes_accessed=6 * 2**20, transcendentals=rows * 512),
    )(
        latent.transpose(0, 2, 1),
        queries.reshape(n_req * heads, width),
        w_gate[0],
        w_up[0],
        w_down[0],
        lengths,
        fresh_latent,
        tokens,
        routes.T,
        gates.T,
    )
    return context.reshape(n_req, heads, LAT), mixed


def solution(mesh):
    placed = (
        P("ep", "seq", None),
        P("ep", None),
        P("ep", "seq", None),
        P("ep", None),
        P("ep", "seq"),
        P("ep", None),
        P("ep", None),
        P("ep", None, "seq"),
        P("ep", None, "seq"),
        P("ep", "seq", None),
    )
    return jax.shard_map(
        on_device,
        mesh=mesh,
        in_specs=placed,
        out_specs=(P("ep", "seq", None), P("ep", "seq")),
        check_vma=False,
    )
```

```python
import functools
import heapq

import jax
import jax.numpy as jnp
from jax import lax
from jax.experimental import pallas as pl
from jax.experimental.pallas import tpu as pltpu
from jax.sharding import PartitionSpec as P

MESH = pl.DeviceIdType.MESH
LAT = 512
NX = 4
LANE = 128
HALF_TOK = 16
SCALE = 0.07216878364870322
NEG = -1.0e30
F32 = jnp.float32
BF16 = jnp.bfloat16

LINK_RATE = 45.0e3
HOP = 1.5


def mod(value, n):
    return lax.rem(value + n, n)


class Net:
    def __init__(self, send, recv):
        self.send, self.recv = send, recv
        self.count, self.now = 0, 0.0
        self.links, self.copies = {}, []

    def copy(self, src, dst, device, link, hops=1):
        at = self.count
        self.count += 1
        made = pltpu.make_async_remote_copy(
            src_ref=src,
            dst_ref=dst,
            send_sem=self.send.at[at],
            recv_sem=self.recv.at[at],
            device_id=device,
            device_id_type=MESH,
        )
        made.start()
        size = 2 * hops
        for extent in src.shape:
            size *= extent
        begin = max(self.links.get(link, 0.0), self.now)
        self.links[link] = begin + size / LINK_RATE
        self.copies.append(made)
        return made, self.links[link] + HOP

    def run(self, tasks):
        self.heap, self.order = [], 0
        for task in tasks:
            self.add(self.now, task)
        while self.heap:
            at, _, task = heapq.heappop(self.heap)
            self.now = max(self.now, at)
            try:
                ready = next(task)
            except StopIteration:
                continue
            self.add(ready, task)

    def add(self, at, task):
        self.order += 1
        heapq.heappush(self.heap, (at, self.order, task))


def around(n):
    offsets = [0]
    for k in range(1, n // 2):
        offsets += [k, -k]
    return offsets + [n // 2]


def ring_gather(net, piece, cut, n, up, down, axis, landed):
    far = n // 2

    def pass_on(side, k):
        src, dst = piece((k, -k)[1 - side]), piece(far if k + 1 == far else (k + 1, -k - 1)[1 - side])
        if k + 1 == far:
            src, dst = cut(src, side), cut(dst, side)
        return net.copy(src, dst, (up, down)[side], axis + "+-"[side])

    cu, tu = pass_on(0, 0)
    cd, td = pass_on(1, 0)
    landed(0)
    for k in range(1, far):
        yield tu
        cu.wait_recv()
        cu, tu = pass_on(0, k)
        landed(-k)
        yield td
        cd.wait_recv()
        cd, td = pass_on(1, k)
        landed(k)
    yield max(tu, td)
    cu.wait_recv()
    cd.wait_recv()
    landed(far)


def skip_gather(net, piece, cut, ups, downs, axis, landed):
    def send(src, at, way, hops, side=None):
        dst = piece(at)
        if side is not None:
            src, dst = cut(src, side), cut(dst, side)
        return net.copy(src, dst, way[hops - 1], axis + ("+" if way is ups else "-"), hops)

    c2u, t2u = send(piece(0), -2, ups, 2)
    c2d, t2d = send(piece(0), 2, downs, 2)
    c1u, t1u = send(piece(0), -1, ups, 1)
    c1d, t1d = send(piece(0), 1, downs, 1)
    landed(0)
    yield t2u
    c2u.wait_recv()
    c4u, t4u = send(piece(-2), 4, ups, 2, 0)
    c3u, t3u = send(piece(-2), -3, ups, 1)
    landed(-2)
    yield t2d
    c2d.wait_recv()
    c4d, t4d = send(piece(2), 4, downs, 2, 1)
    c3d, t3d = send(piece(2), 3, downs, 1)
    landed(2)
    yield t1u
    c1u.wait_recv()
    landed(-1)
    yield t1d
    c1d.wait_recv()
    landed(1)
    yield max(t3u, t3d)
    c3u.wait_recv()
    landed(-3)
    c3d.wait_recv()
    landed(3)
    yield max(t4u, t4d)
    c4u.wait_recv()
    c4d.wait_recv()
    landed(4)


def skip_scatter(net, piece, cut, arrived, ups, downs, axis, ready, finish):
    up, down = axis + "+", axis + "-"
    while not (ready(4) and ready(3) and ready(-3)):
        yield net.now + 0.01
    c4u, t4u = net.copy(cut(piece(4), 0), cut(arrived(0, 0), 0), ups[1], up, 2)
    c4d, t4d = net.copy(cut(piece(4), 1), cut(arrived(1, 0), 1), downs[1], down, 2)
    c3u, t3u = net.copy(piece(3), arrived(0, 1), ups[0], up)
    c3d, t3d = net.copy(piece(-3), arrived(1, 1), downs[0], down)
    while not (ready(2) and ready(-2)):
        yield net.now + 0.01
    yield max(t4u, t3u)
    c4u.wait_recv()
    c3u.wait_recv()
    add_into(cut(piece(2), 0), cut(arrived(0, 0), 0))
    add_into(piece(2), arrived(0, 1))
    c2u, t2u = net.copy(piece(2), arrived(0, 2), ups[1], up, 2)
    yield max(t4d, t3d)
    c4d.wait_recv()
    c3d.wait_recv()
    add_into(cut(piece(-2), 1), cut(arrived(1, 0), 1))
    add_into(piece(-2), arrived(1, 1))
    c2d, t2d = net.copy(piece(-2), arrived(1, 2), downs[1], down, 2)
    while not (ready(1) and ready(-1)):
        yield net.now + 0.01
    c1u, t1u = net.copy(piece(1), arrived(0, 3), ups[0], up)
    c1d, t1d = net.copy(piece(-1), arrived(1, 3), downs[0], down)
    while not ready(0):
        yield net.now + 0.01
    yield max(t2u, t2d, t1u, t1d)
    total = piece(0)[...].astype(F32)
    for k, (one, two) in ((3, (c1u, c1d)), (2, (c2u, c2d))):
        one.wait_recv()
        two.wait_recv()
        total = total + arrived(0, k)[...].astype(F32) + arrived(1, k)[...].astype(F32)
    finish(total)


def add_into(ref, other):
    ref[...] = ref[...] + other[...]


def ring_scatter(net, piece, cut, arrived, n, up, down, axis, ready, finish):
    far = n // 2
    while not ready(far):
        yield net.now + 0.01
    cu, tu = net.copy(cut(piece(far), 0), cut(arrived(0, 0), 0), up, axis + "+")
    cd, td = net.copy(cut(piece(far), 1), cut(arrived(1, 0), 1), down, axis + "-")
    for k in range(1, far):
        d = far - k
        while not (ready(d) and ready(-d)):
            yield net.now + 0.01
        yield tu
        cu.wait_recv()
        mine, came = piece(d), arrived(0, k - 1)
        if k == 1:
            mine, came = cut(mine, 0), cut(came, 0)
        add_into(mine, came)
        cu, tu = net.copy(piece(d), arrived(0, k), up, axis + "+")
        yield td
        cd.wait_recv()
        mine, came = piece(-d), arrived(1, k - 1)
        if k == 1:
            mine, came = cut(mine, 1), cut(came, 1)
        add_into(mine, came)
        cd, td = net.copy(piece(-d), arrived(1, k), down, axis + "-")
    while not ready(0):
        yield net.now + 0.01
    yield max(tu, td)
    cu.wait_recv()
    cd.wait_recv()
    if far == 1:
        add_into(cut(piece(0), 0), cut(arrived(0, 0), 0))
        add_into(cut(piece(0), 1), cut(arrived(1, 0), 1))
        finish(piece(0)[...].astype(F32))
    else:
        finish(
            piece(0)[...].astype(F32)
            + arrived(0, far - 1)[...].astype(F32)
            + arrived(1, far - 1)[...].astype(F32)
        )


def kernel(
    cfg,
    latent, queries, wg, wu, wd, lengths, fresh, tokens, routes, gates,
    ctx_out, mix_out,
    tokpad, tokbuf, line, square, xa, xb, wcat, wdcat, acc, hid, ya, yb,
    ra, rax, rbx, rb, ebuf, erecv,
    lbuf, qpad, qbuf, qf, obuf, orecv, cf, cb, crecv,
    local_sem, send_sem, recv_sem, t_send, t_recv, q_send, q_recv, e_send, e_recv,
):
    n_seq, n_z, wide_a, wide_b, share, heads = cfg
    n_y = n_seq // 2
    s, e = lax.axis_index("seq"), lax.axis_index("ep")
    y, c = s // 2, lax.rem(s, 2)
    z, x = e // NX, lax.rem(e, NX)
    other = 1 - c
    sibling = (2 * y + other, e)
    experts = n_z * NX
    far_x = NX // 2
    n_req = lengths.shape[1]
    half_req = n_req // 2
    q_rows = half_req * heads
    x_up, x_down = (s, z * NX + mod(x + 1, NX)), (s, z * NX + mod(x - 1, NX))
    z_up, z_down = (s, mod(z + 1, n_z) * NX + x), (s, mod(z - 1, n_z) * NX + x)
    z_ups = (z_up, (s, mod(z + 2, n_z) * NX + x))
    z_downs = (z_down, (s, mod(z - 2, n_z) * NX + x))
    slot_z = {d: i for i, d in enumerate(around(n_z))}
    slot_x = {d: i for i, d in enumerate(around(NX))}

    def local(src, dst, i):
        made = pltpu.make_async_copy(src, dst, local_sem.at[i])
        made.start()
        return made

    for half in range(2):
        tokpad[half] = jnp.zeros_like(tokpad[half])
        tokpad[half, :, 0:share] = tokens[half * HALF_TOK:(half + 1) * HALF_TOK, :]

    width = queries.shape[1]
    for half in range(2):
        qpad[half] = jnp.zeros_like(qpad[half])
        qpad[half, :, 0:width] = queries[half * q_rows:(half + 1) * q_rows, :]

    barrier = pltpu.get_barrier_semaphore()

    def greet(j, carry):
        pl.semaphore_signal(
            barrier, inc=1, device_id=(lax.rem(s + j, n_seq), e), device_id_type=MESH
        )
        return carry

    lax.fori_loop(1, n_seq, greet, 0)
    for who in (x_up, x_down) + z_ups + z_downs:
        pl.semaphore_signal(barrier, inc=1, device_id=who, device_id_type=MESH)

    loads = [
        local(latent.at[pl.ds(c * half_req, half_req)], lbuf.at[0], 0),
        local(wg, wcat.at[0], 1),
        local(wu, wcat.at[2], 2),
        local(wd, wdcat.at[pl.ds(0, LANE)], 3),
    ]

    row = lax.broadcasted_iota(jnp.int32, (LANE, routes.shape[1]), 0)
    named = jnp.where(row < experts, row, row - experts)
    weight = jnp.zeros(named.shape, F32)
    for k in range(routes.shape[0]):
        weight = weight + jnp.where(named == routes[k:k + 1, :], gates[k:k + 1, :], 0.0)
    high = weight.astype(BF16).astype(F32)
    weight = jnp.where(row < experts, high, jnp.where(row < 2 * experts, weight - high, 0.0))
    square[...] = jnp.zeros_like(square)
    square[:, 0:routes.shape[1]] = weight
    square[...] = jnp.transpose(square[...])

    pl.semaphore_wait(barrier, n_seq - 1 + 6)

    def token_copy(j):
        to = lax.rem(s + j, n_seq)
        return pltpu.make_async_remote_copy(
            src_ref=tokpad.at[lax.rem(to, 2)],
            dst_ref=tokbuf.at[s],
            send_sem=t_send.at[j],
            recv_sem=t_recv.at[j],
            device_id=(to, e),
            device_id_type=MESH,
        )

    def query_copy(j):
        to = lax.rem(s + j, n_seq)
        return pltpu.make_async_remote_copy(
            src_ref=qpad.at[lax.rem(to, 2)],
            dst_ref=qbuf.at[s],
            send_sem=q_send.at[j],
            recv_sem=q_recv.at[j],
            device_id=(to, e),
            device_id_type=MESH,
        )

    def end_copy(j):
        to = lax.rem(s + j, n_seq)
        return pltpu.make_async_remote_copy(
            src_ref=ebuf.at[to],
            dst_ref=erecv.at[s],
            send_sem=e_send.at[j],
            recv_sem=e_recv.at[j],
            device_id=(to, e),
            device_id_type=MESH,
        )

    def each(act):
        def body(j, carry):
            act(j)
            return carry

        lax.fori_loop(1, n_seq, body, 0)

    net = Net(send_sem, recv_sem)
    each(lambda j: token_copy(j).start())
    lat_copy, _ = net.copy(latent.at[pl.ds(other * half_req, half_req)], lbuf.at[1], sibling, "core")
    weights = [
        net.copy(src, dst, sibling, "core")[0]
        for src, dst in (
            (wg, wcat.at[1]),
            (wu, wcat.at[3]),
            (wd, wdcat.at[pl.ds(LANE, LANE)]),
        )
    ]
    each(lambda j: query_copy(j).start())

    tokbuf[s] = tokpad[c]
    qbuf[s] = qpad[c]
    line[...] = jnp.zeros_like(line)
    first_row = pl.multiple_of(c * HALF_TOK, HALF_TOK)
    xb[0, 0, :, wide_b:wide_b + LANE] = square[pl.ds(first_row, HALF_TOK), :].astype(BF16)
    each(lambda j: token_copy(j).wait_recv())
    for i in range(n_seq):
        begin, turn = share * i // LANE * LANE, share * i % LANE
        span = tokpad.shape[2] + LANE
        value = jnp.concatenate(
            [tokbuf[i].astype(F32), jnp.zeros((HALF_TOK, LANE), F32)], axis=1
        )
        if turn:
            value = pltpu.roll(value, turn, 1)
        line[:, begin:begin + span] = line[:, begin:begin + span] + value
    xa[0, 0] = line[:, 0:wide_a].astype(BF16)
    xb[0, 0, :, 0:wide_b] = line[:, wide_a:wide_a + wide_b].astype(BF16)

    position = lax.broadcasted_iota(jnp.int32, (n_seq * heads, LANE), 1)

    def one_request(i, carry):
        head_rows = pl.ds(pl.multiple_of(i * heads, heads), heads)
        q = qf[:, head_rows, :].reshape(n_seq * heads, qf.shape[2]).astype(BF16)
        length = lengths[0, c * half_req + i]
        parts = []
        for side, base in ((0, s), (1, 2 * y + other)):
            score = jnp.dot(q, lbuf[side, i], preferred_element_type=F32) * SCALE
            valid = position + base * LANE < length
            parts.append((jnp.where(valid, score, NEG), valid))
        top = jnp.maximum(
            jnp.max(parts[0][0], axis=1, keepdims=True),
            jnp.max(parts[1][0], axis=1, keepdims=True),
        ).astype(BF16).astype(F32)
        total = jnp.zeros((n_seq * heads, 1), F32)
        context = jnp.zeros((n_seq * heads, LAT), F32)
        for side in range(2):
            score, valid = parts[side]
            w = jnp.where(valid, jnp.exp(score - top), 0.0)
            total = total + jnp.sum(w, axis=1, keepdims=True)
            context = context + lax.dot_general(
                w.astype(BF16), lbuf[side, i, 0:LAT, :], (((1,), (1,)), ((), ())),
                preferred_element_type=F32,
            )
        total_high = total.astype(BF16).astype(F32)
        note = jnp.where(
            position == 0,
            top,
            jnp.where(position == 1, total_high, jnp.where(position == 2, total - total_high, 0.0)),
        )
        at = pl.ds(pl.multiple_of(2 * heads * i, 2 * heads), 2 * heads)
        obuf[:, at, 0:LAT] = context.astype(BF16).reshape(n_y, 2 * heads, LAT)
        obuf[:, at, LAT:LAT + LANE] = note.astype(BF16).reshape(n_y, 2 * heads, LANE)
        return carry

    def one_context(i, carry):
        at = pl.ds(pl.multiple_of(2 * heads * i, 2 * heads), 2 * heads)
        head_rows = pl.ds(pl.multiple_of(i * heads, heads), heads)
        line_of = lax.broadcasted_iota(jnp.int32, fresh.shape, 0)
        chosen = jnp.where(line_of == c * half_req + i, fresh[...].astype(F32), 0.0)
        key = jnp.sum(chosen, axis=0, keepdims=True)
        q = qf[pl.ds(2 * y, 2), head_rows, :].reshape(2 * heads, qf.shape[2])
        own = jnp.sum(q * key, axis=1, keepdims=True) * SCALE
        notes = [orecv[j, at, LAT:LAT + LANE].astype(F32) for j in range(n_y)]
        top = own
        for note in notes:
            top = jnp.maximum(top, note[:, 0:1])
        w = jnp.exp(own - top)
        total, context = w, w * key[:, 0:LAT]
        for j, note in enumerate(notes):
            w = jnp.exp(note[:, 0:1] - top)
            total = total + w * (note[:, 1:2] + note[:, 2:3])
            context = context + w * orecv[j, at, 0:LAT].astype(F32)
        context = context / total
        for core in range(2):
            cf[core, head_rows, :] = context[core * heads:(core + 1) * heads]
        return carry

    def attend():
        yield net.now + 8.0
        loads[0].wait()
        each(lambda j: query_copy(j).wait_recv())
        lat_copy.wait_recv()
        qf[...] = qbuf[:, :, 0:width].astype(F32)
        lax.fori_loop(0, half_req // 2, one_request, 0)
        net.now += 2.0
        yield net.now + 0.5
        lax.fori_loop(half_req // 2, half_req, one_request, 0)
        net.now += 2.0
        came = []
        for j in range(1, n_y):
            to = lax.rem(y + j, n_y)
            came.append(net.copy(obuf.at[to], orecv.at[y], (2 * to + c, e), "y"))
        orecv[y] = obuf[y]
        yield net.now + 25.0
        for one, _ in came:
            one.wait_recv()
        lax.fori_loop(0, half_req, one_context, 0)
        net.now += 1.0
        cb[...] = cf[...].astype(BF16)
        back, when = net.copy(cb.at[other], crecv, sibling, "core")
        ctx_out[pl.ds(pl.multiple_of(c * q_rows, q_rows), q_rows), :] = cb[c]
        yield when + 5.0
        back.wait_recv()
        ctx_out[pl.ds(pl.multiple_of(other * q_rows, q_rows), q_rows), :] = crecv[...]

    half_a, half_b = wide_a // 2, wide_b // 2

    def cut_a(ref, side):
        lead = (slice(None),) * (len(ref.shape) - 1)
        return ref.at[lead + (pl.ds(side * half_a, half_a),)]

    def cut_b(ref, side):
        lead = (slice(None),) * (len(ref.shape) - 1)
        size = half_b if side == 0 else ref.shape[-1] - half_b
        return ref.at[lead + (pl.ds(side * half_b, size),)]

    teams = [(0,)] + [(d, -d) for d in range(1, n_z // 2)] + [(n_z // 2,)]

    pairs = [(i, i + 1) for i in range(0, NX, 2)]

    def slots(team):
        return pl.ds(slot_z[team[0]], len(team))

    def gather_z(piece, cut, done):
        if n_z == 8:
            return skip_gather(net, piece, cut, z_ups, z_downs, "z", done)
        return ring_gather(net, piece, cut, n_z, z_up, z_down, "z", done)

    def scatter_z(piece, cut, arrived, ready, finish):
        if n_z == 8:
            return skip_scatter(net, piece, cut, arrived, z_ups, z_downs, "z", ready, finish)
        return ring_scatter(net, piece, cut, arrived, n_z, z_up, z_down, "z", ready, finish)

    landed = {d: 0 for d in slot_z}

    def count(team):
        for d in team:
            landed[d] += 1

    def gather_a():
        here = set()

        def start(dx):
            here.add(slot_x[dx])
            for pair in pairs:
                if slot_x[dx] in pair and here.issuperset(pair):
                    net.add(net.now, along_z(pl.ds(pair[0], 2)))

        def along_z(at):
            return gather_z(lambda d: xa.at[slot_z[d], at], cut_a, lambda d: count((d,)))

        yield from ring_gather(
            net, lambda d: xa.at[0, slot_x[d]], cut_a, NX, x_up, x_down, "x", start
        )

    def gather_b():
        here = set()

        def start(dz):
            here.add(dz)
            team = [team for team in teams if dz in team][0]
            if here.issuperset(team):
                net.add(net.now, ring_gather(
                    net, lambda d: xb.at[slots(team), slot_x[d]], cut_b, NX, x_up, x_down, "x",
                    lambda d: count(team),
                ))

        yield from gather_z(lambda d: xb.at[slot_z[d], 0], cut_b, start)

    step_a, step_b = wide_a // 2, wide_b // 5
    def experts_of(first, last):
        rows = (last - first) * NX * HALF_TOK

        def beside(some):
            return jnp.concatenate([wcat[i, some, :] for i in range(4)], axis=1)

        def up_a(k, carry):
            cols = pl.ds(pl.multiple_of(k * step_a, step_a), step_a)
            value = xa[first:last, :, :, cols].reshape(rows, step_a)
            acc[0:rows, :] += jnp.dot(value, beside(cols), preferred_element_type=F32)
            return carry

        def up_b(k, carry):
            cols = pl.ds(pl.multiple_of(k * step_b, step_b), step_b)
            down = pl.ds(pl.multiple_of(wide_a + k * step_b, LANE), step_b)
            value = xb[first:last, :, :, cols].reshape(rows, step_b)
            acc[0:rows, :] += jnp.dot(value, beside(down), preferred_element_type=F32)
            return carry

        def down_a(k, carry):
            cols = pl.ds(pl.multiple_of(k * step_a, step_a), step_a)
            value = jnp.dot(hid[0:rows, :], wdcat[:, cols], preferred_element_type=F32)
            ya[first:last, :, :, cols] = value.astype(BF16).reshape(last - first, NX, HALF_TOK, step_a)
            return carry

        def down_b(k, carry):
            cols = pl.ds(pl.multiple_of(k * step_b, step_b), step_b)
            down = pl.ds(pl.multiple_of(wide_a + k * step_b, LANE), step_b)
            value = jnp.dot(hid[0:rows, :], wdcat[:, down], preferred_element_type=F32)
            yb[first:last, :, :, cols] = value.astype(BF16).reshape(last - first, NX, HALF_TOK, step_b)
            return carry

        acc[0:rows, :] = jnp.zeros((rows, 4 * LANE), F32)
        lax.fori_loop(0, 2, up_a, 0)
        lax.fori_loop(0, 5, up_b, 0)
        tile = xb[first:last, :, :, wide_b:wide_b + LANE].reshape(rows, LANE).astype(F32)
        lane = lax.broadcasted_iota(jnp.int32, (rows, LANE), 1)
        gate = jnp.sum(
            jnp.where((lane == e) | (lane == e + experts), tile, 0.0), axis=1, keepdims=True
        )
        g = acc[0:rows, 0:2 * LANE]
        value = g / (1.0 + jnp.exp(-g)) * acc[0:rows, 2 * LANE:4 * LANE] * gate
        hid[0:rows, :] = value.astype(BF16)
        lax.fori_loop(0, 5, down_b, 0)
        lax.fori_loop(0, 2, down_a, 0)

    def compute():
        offsets = around(n_z)
        groups = [(0, 5), (5, 8)] if n_z == 8 else [(0, len(offsets))]
        for first, last in groups:
            while any(landed[d] < len(pairs) + NX for d in offsets[first:last]):
                yield net.now + 0.01
            if first == 0:
                for load in loads[1:]:
                    load.wait()
                for made in weights:
                    made.wait_recv()
            experts_of(first, last)
            net.now += 1.0

    attention = attend()
    net.run([gather_a(), gather_b(), sample(attention, 3), compute()])

    net.links, net.now = {}, 0.0
    ended = set()

    def always(d):
        return True

    def row_sum(team):
        at = slots(team)

        def finish(total):
            yb[at, 0] = total.astype(BF16)
            ended.update(team)

        return ring_scatter(
            net, lambda d: yb.at[at, slot_x[d]], cut_b, lambda way, k: rbx.at[way, k, at],
            NX, x_up, x_down, "x", always, finish,
        )

    done_a = set()

    def column_sum(pair):
        at = pl.ds(pair[0], 2)

        def finish(total):
            ya[0, at] = total.astype(BF16)
            done_a.update(pair)

        return scatter_z(
            lambda d: ya.at[slot_z[d], at], cut_a, lambda way, k: ra.at[way, k, at], always, finish
        )

    def end_a(total):
        line[:, 0:wide_a] = total

    def end_b(total):
        line[:, wide_a:wide_a + wide_b] = total

    sum_a = ring_scatter(
        net, lambda d: ya.at[0, slot_x[d]], cut_a, lambda way, k: rax.at[way, k],
        NX, x_up, x_down, "x", lambda d: slot_x[far_x if d == -far_x else d] in done_a, end_a,
    )

    sum_b = scatter_z(
        lambda d: yb.at[slot_z[d], 0], cut_b, lambda way, k: rb.at[way, k],
        lambda d: d in ended, end_b,
    )
    before = list(net.copies)

    def settle():
        yield net.now + 1.0
        each(lambda j: token_copy(j).wait_send())
        each(lambda j: query_copy(j).wait_send())
        for made in before:
            made.wait_send()

    first_rows = [row_sum(team) for team in reversed(teams)]
    columns = [column_sum(pair) for pair in reversed(pairs)]
    net.run(first_rows[:1] + columns + first_rows[1:] + [sum_a, sum_b, sample(attention, 9), settle()])

    for i in range(n_seq):
        begin, turn = share * i // LANE * LANE, share * i % LANE
        span = tokpad.shape[2] + LANE
        value = line[:, begin:begin + span]
        if turn:
            value = pltpu.roll(value, span - turn, 1)
        ebuf[i] = value[:, 0:tokpad.shape[2]].astype(BF16)
    each(lambda j: end_copy(j).start())
    erecv[s] = ebuf[s]
    each(lambda j: end_copy(j).wait_recv())
    for half in range(2):
        total = erecv[half].astype(F32)
        for i in range(1, n_y):
            total = total + erecv[2 * i + half].astype(F32)
        mix_out[half * HALF_TOK:(half + 1) * HALF_TOK, :] = total[:, 0:share].astype(BF16)

    each(lambda j: end_copy(j).wait_send())
    for made in net.copies[len(before):]:
        made.wait_send()


def sample(task, most):
    for _ in range(most):
        try:
            ready = next(task)
        except StopIteration:
            return
        yield ready


def on_device(latent, lengths, queries, fresh_latent, tokens, routes, gates, w_gate, w_up, w_down):
    n_seq, n_ep = lax.axis_size("seq"), lax.axis_size("ep")
    n_z, n_y = n_ep // NX, n_seq // 2
    n_req, heads, width = queries.shape
    share = tokens.shape[1]
    features = share * n_seq
    wide_a = features // 7 * 2
    wide_b = features - wide_a
    padded = -(-share // LANE) * LANE
    wide_q = -(-width // LANE) * LANE
    rows = n_ep * HALF_TOK
    half_req = n_req // 2
    q_rows = half_req * heads
    far_z, far_x = n_z // 2, NX // 2
    cfg = (n_seq, n_z, wide_a, wide_b, share, heads)
    vmem = pl.BlockSpec(memory_space=pltpu.VMEM)
    hbm = pl.BlockSpec(memory_space=pl.ANY)
    dma = pltpu.SemaphoreType.DMA
    ffn = 2 * rows * features * 6 * LANE
    context, mixed = pl.pallas_call(
        functools.partial(kernel, cfg),
        out_shape=(
            jax.ShapeDtypeStruct((n_req * heads, LAT), BF16),
            jax.ShapeDtypeStruct(tokens.shape, BF16),
        ),
        in_specs=[hbm, vmem, hbm, hbm, hbm, pl.BlockSpec(memory_space=pltpu.SMEM), vmem, vmem, vmem, vmem],
        out_specs=(vmem, vmem),
        scratch_shapes=[
            pltpu.VMEM((2, HALF_TOK, padded), BF16),
            pltpu.VMEM((n_seq, HALF_TOK, padded), BF16),
            pltpu.VMEM((HALF_TOK, features + 2 * LANE), F32),
            pltpu.VMEM((LANE, LANE), F32),
            pltpu.VMEM((n_z, NX, HALF_TOK, wide_a), BF16),
            pltpu.VMEM((n_z, NX, HALF_TOK, wide_b + LANE), BF16),
            pltpu.VMEM((4, features, LANE), BF16),
            pltpu.VMEM((2 * LANE, features), BF16),
            pltpu.VMEM((rows, 4 * LANE), F32),
            pltpu.VMEM((rows, 2 * LANE), BF16),
            pltpu.VMEM((n_z, NX, HALF_TOK, wide_a), BF16),
            pltpu.VMEM((n_z, NX, HALF_TOK, wide_b), BF16),
            pltpu.VMEM((2, far_z, NX, HALF_TOK, wide_a), BF16),
            pltpu.VMEM((2, far_x, HALF_TOK, wide_a), BF16),
            pltpu.VMEM((2, far_x, n_z, HALF_TOK, wide_b), BF16),
            pltpu.VMEM((2, far_z, HALF_TOK, wide_b), BF16),
            pltpu.VMEM((n_seq, HALF_TOK, padded), BF16),
            pltpu.VMEM((n_seq, HALF_TOK, padded), BF16),
            pltpu.VMEM((2, half_req, width, LANE), BF16),
            pltpu.VMEM((2, q_rows, wide_q), BF16),
            pltpu.VMEM((n_seq, q_rows, wide_q), BF16),
            pltpu.VMEM((n_seq, q_rows, width), F32),
            pltpu.VMEM((n_y, 2 * q_rows, LAT + LANE), BF16),
            pltpu.VMEM((n_y, 2 * q_rows, LAT + LANE), BF16),
            pltpu.VMEM((2, q_rows, LAT), F32),
            pltpu.VMEM((2, q_rows, LAT), BF16),
            pltpu.VMEM((q_rows, LAT), BF16),
            dma((4,)),
            dma((120,)),
            dma((120,)),
            dma((n_seq,)),
            dma((n_seq,)),
            dma((n_seq,)),
            dma((n_seq,)),
            dma((n_seq,)),
            dma((n_seq,)),
        ],
        compiler_params=pltpu.CompilerParams(
            collective_id=0, has_side_effects=True, vmem_limit_bytes=56 * 1024 * 1024
        ),
        cost_estimate=pl.CostEstimate(flops=ffn, bytes_accessed=6 * 2**20, transcendentals=rows * 512),
    )(
        latent.transpose(0, 2, 1),
        queries.reshape(n_req * heads, width),
        w_gate[0],
        w_up[0],
        w_down[0],
        lengths,
        fresh_latent,
        tokens,
        routes.T,
        gates.T,
    )
    return context.reshape(n_req, heads, LAT), mixed


def solution(mesh):
    placed = (
        P("ep", "seq", None),
        P("ep", None),
        P("ep", "seq", None),
        P("ep", None),
        P("ep", "seq"),
        P("ep", None),
        P("ep", None),
        P("ep", None, "seq"),
        P("ep", None, "seq"),
        P("ep", "seq", None),
    )
    return jax.shard_map(
        on_device,
        mesh=mesh,
        in_specs=placed,
        out_specs=(P("ep", "seq", None), P("ep", "seq")),
        check_vma=False,
    )
```

```python
import functools
import heapq

import jax
import jax.numpy as jnp
from jax import lax
from jax.experimental import pallas as pl
from jax.experimental.pallas import tpu as pltpu
from jax.sharding import PartitionSpec as P

MESH = pl.DeviceIdType.MESH
LAT = 512
NX = 4
LANE = 128
HALF_TOK = 16
SCALE = 0.07216878364870322
NEG = -1.0e30
F32 = jnp.float32
BF16 = jnp.bfloat16

LINK_RATE = 45.0e3
HOP = 1.5


def mod(value, n):
    return lax.rem(value + n, n)


class Net:
    def __init__(self, send, recv):
        self.send, self.recv = send, recv
        self.count, self.now = 0, 0.0
        self.links, self.copies = {}, []

    def copy(self, src, dst, device, link, hops=1):
        at = self.count
        self.count += 1
        made = pltpu.make_async_remote_copy(
            src_ref=src,
            dst_ref=dst,
            send_sem=self.send.at[at],
            recv_sem=self.recv.at[at],
            device_id=device,
            device_id_type=MESH,
        )
        made.start()
        size = 2 * hops
        for extent in src.shape:
            size *= extent
        begin = max(self.links.get(link, 0.0), self.now)
        self.links[link] = begin + size / LINK_RATE
        self.copies.append(made)
        return made, self.links[link] + HOP

    def run(self, tasks):
        self.heap, self.order = [], 0
        for task in tasks:
            self.add(self.now, task)
        while self.heap:
            at, _, task = heapq.heappop(self.heap)
            self.now = max(self.now, at)
            try:
                ready = next(task)
            except StopIteration:
                continue
            self.add(ready, task)

    def add(self, at, task):
        self.order += 1
        heapq.heappush(self.heap, (at, self.order, task))


def around(n):
    offsets = [0]
    for k in range(1, n // 2):
        offsets += [k, -k]
    return offsets + [n // 2]


def ring_gather(net, piece, cut, n, up, down, axis, landed):
    far = n // 2

    def pass_on(side, k):
        src, dst = piece((k, -k)[1 - side]), piece(far if k + 1 == far else (k + 1, -k - 1)[1 - side])
        if k + 1 == far:
            src, dst = cut(src, side), cut(dst, side)
        return net.copy(src, dst, (up, down)[side], axis + "+-"[side])

    cu, tu = pass_on(0, 0)
    cd, td = pass_on(1, 0)
    landed(0)
    for k in range(1, far):
        yield tu
        cu.wait_recv()
        cu, tu = pass_on(0, k)
        landed(-k)
        yield td
        cd.wait_recv()
        cd, td = pass_on(1, k)
        landed(k)
    yield max(tu, td)
    cu.wait_recv()
    cd.wait_recv()
    landed(far)


def skip_gather(net, piece, cut, ups, downs, axis, landed):
    def send(src, at, way, hops, side=None):
        dst = piece(at)
        if side is not None:
            src, dst = cut(src, side), cut(dst, side)
        return net.copy(src, dst, way[hops - 1], axis + ("+" if way is ups else "-"), hops)

    c2u, t2u = send(piece(0), -2, ups, 2)
    c2d, t2d = send(piece(0), 2, downs, 2)
    c1u, t1u = send(piece(0), -1, ups, 1)
    c1d, t1d = send(piece(0), 1, downs, 1)
    landed(0)
    yield t2u
    c2u.wait_recv()
    c4u, t4u = send(piece(-2), 4, ups, 2, 0)
    c3u, t3u = send(piece(-2), -3, ups, 1)
    landed(-2)
    yield t2d
    c2d.wait_recv()
    c4d, t4d = send(piece(2), 4, downs, 2, 1)
    c3d, t3d = send(piece(2), 3, downs, 1)
    landed(2)
    yield t1u
    c1u.wait_recv()
    landed(-1)
    yield t1d
    c1d.wait_recv()
    landed(1)
    yield max(t3u, t3d)
    c3u.wait_recv()
    landed(-3)
    c3d.wait_recv()
    landed(3)
    yield max(t4u, t4d)
    c4u.wait_recv()
    c4d.wait_recv()
    landed(4)


def skip_scatter(net, piece, cut, arrived, ups, downs, axis, ready, finish):
    up, down = axis + "+", axis + "-"
    while not (ready(4) and ready(3) and ready(-3)):
        yield net.now + 0.01
    c4u, t4u = net.copy(cut(piece(4), 0), cut(arrived(0, 0), 0), ups[1], up, 2)
    c4d, t4d = net.copy(cut(piece(4), 1), cut(arrived(1, 0), 1), downs[1], down, 2)
    c3u, t3u = net.copy(piece(3), arrived(0, 1), ups[0], up)
    c3d, t3d = net.copy(piece(-3), arrived(1, 1), downs[0], down)
    while not (ready(2) and ready(-2)):
        yield net.now + 0.01
    yield max(t4u, t3u)
    c4u.wait_recv()
    c3u.wait_recv()
    add_into(cut(piece(2), 0), cut(arrived(0, 0), 0))
    add_into(piece(2), arrived(0, 1))
    c2u, t2u = net.copy(piece(2), arrived(0, 2), ups[1], up, 2)
    yield max(t4d, t3d)
    c4d.wait_recv()
    c3d.wait_recv()
    add_into(cut(piece(-2), 1), cut(arrived(1, 0), 1))
    add_into(piece(-2), arrived(1, 1))
    c2d, t2d = net.copy(piece(-2), arrived(1, 2), downs[1], down, 2)
    while not (ready(1) and ready(-1)):
        yield net.now + 0.01
    c1u, t1u = net.copy(piece(1), arrived(0, 3), ups[0], up)
    c1d, t1d = net.copy(piece(-1), arrived(1, 3), downs[0], down)
    while not ready(0):
        yield net.now + 0.01
    yield max(t2u, t2d, t1u, t1d)
    total = piece(0)[...].astype(F32)
    for k, (one, two) in ((3, (c1u, c1d)), (2, (c2u, c2d))):
        one.wait_recv()
        two.wait_recv()
        total = total + arrived(0, k)[...].astype(F32) + arrived(1, k)[...].astype(F32)
    finish(total)


def add_into(ref, other):
    ref[...] = ref[...] + other[...]


def ring_scatter(net, piece, cut, arrived, n, up, down, axis, ready, finish):
    far = n // 2
    while not ready(far):
        yield net.now + 0.01
    cu, tu = net.copy(cut(piece(far), 0), cut(arrived(0, 0), 0), up, axis + "+")
    cd, td = net.copy(cut(piece(far), 1), cut(arrived(1, 0), 1), down, axis + "-")
    for k in range(1, far):
        d = far - k
        while not (ready(d) and ready(-d)):
            yield net.now + 0.01
        yield tu
        cu.wait_recv()
        mine, came = piece(d), arrived(0, k - 1)
        if k == 1:
            mine, came = cut(mine, 0), cut(came, 0)
        add_into(mine, came)
        cu, tu = net.copy(piece(d), arrived(0, k), up, axis + "+")
        yield td
        cd.wait_recv()
        mine, came = piece(-d), arrived(1, k - 1)
        if k == 1:
            mine, came = cut(mine, 1), cut(came, 1)
        add_into(mine, came)
        cd, td = net.copy(piece(-d), arrived(1, k), down, axis + "-")
    while not ready(0):
        yield net.now + 0.01
    yield max(tu, td)
    cu.wait_recv()
    cd.wait_recv()
    if far == 1:
        add_into(cut(piece(0), 0), cut(arrived(0, 0), 0))
        add_into(cut(piece(0), 1), cut(arrived(1, 0), 1))
        finish(piece(0)[...].astype(F32))
    else:
        finish(
            piece(0)[...].astype(F32)
            + arrived(0, far - 1)[...].astype(F32)
            + arrived(1, far - 1)[...].astype(F32)
        )


def kernel(
    cfg,
    latent, queries, wg, wu, wd, lengths, fresh, tokens, routes, gates,
    ctx_out, mix_out,
    tokpad, tokbuf, line, square, xa, xb, wcat, wdcat, acc, hid, ya, yb,
    ra, rax, rbx, rb, ebuf, erecv,
    lbuf, qpad, qbuf, qf, obuf, orecv, cf, cb, crecv,
    local_sem, send_sem, recv_sem, t_send, t_recv, q_send, q_recv, e_send, e_recv,
):
    n_seq, n_z, wide_a, wide_b, share, heads = cfg
    n_y = n_seq // 2
    s, e = lax.axis_index("seq"), lax.axis_index("ep")
    y, c = s // 2, lax.rem(s, 2)
    z, x = e // NX, lax.rem(e, NX)
    other = 1 - c
    sibling = (2 * y + other, e)
    experts = n_z * NX
    far_x = NX // 2
    n_req = lengths.shape[1]
    half_req = n_req // 2
    q_rows = half_req * heads
    x_up, x_down = (s, z * NX + mod(x + 1, NX)), (s, z * NX + mod(x - 1, NX))
    z_up, z_down = (s, mod(z + 1, n_z) * NX + x), (s, mod(z - 1, n_z) * NX + x)
    z_ups = (z_up, (s, mod(z + 2, n_z) * NX + x))
    z_downs = (z_down, (s, mod(z - 2, n_z) * NX + x))
    slot_z = {d: i for i, d in enumerate(around(n_z))}
    slot_x = {d: i for i, d in enumerate(around(NX))}

    def local(src, dst, i):
        made = pltpu.make_async_copy(src, dst, local_sem.at[i])
        made.start()
        return made

    for half in range(2):
        tokpad[half] = jnp.zeros_like(tokpad[half])
        tokpad[half, :, 0:share] = tokens[half * HALF_TOK:(half + 1) * HALF_TOK, :]

    width = queries.shape[1]
    for half in range(2):
        qpad[half] = jnp.zeros_like(qpad[half])
        qpad[half, :, 0:width] = queries[half * q_rows:(half + 1) * q_rows, :]

    barrier = pltpu.get_barrier_semaphore()

    def greet(j, carry):
        pl.semaphore_signal(
            barrier, inc=1, device_id=(lax.rem(s + j, n_seq), e), device_id_type=MESH
        )
        return carry

    lax.fori_loop(1, n_seq, greet, 0)
    for who in (x_up, x_down) + z_ups + z_downs:
        pl.semaphore_signal(barrier, inc=1, device_id=who, device_id_type=MESH)

    loads = [
        local(latent.at[pl.ds(c * half_req, half_req)], lbuf.at[0], 0),
        local(wg, wcat.at[0], 1),
        local(wu, wcat.at[2], 2),
        local(wd, wdcat.at[pl.ds(0, LANE)], 3),
    ]

    row = lax.broadcasted_iota(jnp.int32, (LANE, routes.shape[1]), 0)
    named = jnp.where(row < experts, row, row - experts)
    weight = jnp.zeros(named.shape, F32)
    for k in range(routes.shape[0]):
        weight = weight + jnp.where(named == routes[k:k + 1, :], gates[k:k + 1, :], 0.0)
    high = weight.astype(BF16).astype(F32)
    weight = jnp.where(row < experts, high, jnp.where(row < 2 * experts, weight - high, 0.0))
    square[...] = jnp.zeros_like(square)
    square[:, 0:routes.shape[1]] = weight
    square[...] = jnp.transpose(square[...])

    pl.semaphore_wait(barrier, n_seq - 1 + 6)

    def token_copy(j):
        to = lax.rem(s + j, n_seq)
        return pltpu.make_async_remote_copy(
            src_ref=tokpad.at[lax.rem(to, 2)],
            dst_ref=tokbuf.at[s],
            send_sem=t_send.at[j],
            recv_sem=t_recv.at[j],
            device_id=(to, e),
            device_id_type=MESH,
        )

    def query_copy(j):
        to = lax.rem(s + j, n_seq)
        return pltpu.make_async_remote_copy(
            src_ref=qpad.at[lax.rem(to, 2)],
            dst_ref=qbuf.at[s],
            send_sem=q_send.at[j],
            recv_sem=q_recv.at[j],
            device_id=(to, e),
            device_id_type=MESH,
        )

    def end_copy(j):
        to = lax.rem(s + j, n_seq)
        return pltpu.make_async_remote_copy(
            src_ref=ebuf.at[to],
            dst_ref=erecv.at[s],
            send_sem=e_send.at[j],
            recv_sem=e_recv.at[j],
            device_id=(to, e),
            device_id_type=MESH,
        )

    def each(act):
        def body(j, carry):
            act(j)
            return carry

        lax.fori_loop(1, n_seq, body, 0)

    net = Net(send_sem, recv_sem)
    each(lambda j: token_copy(j).start())
    lat_copy, _ = net.copy(latent.at[pl.ds(other * half_req, half_req)], lbuf.at[1], sibling, "core")
    weights = [
        net.copy(src, dst, sibling, "core")[0]
        for src, dst in (
            (wg, wcat.at[1]),
            (wu, wcat.at[3]),
            (wd, wdcat.at[pl.ds(LANE, LANE)]),
        )
    ]
    each(lambda j: query_copy(j).start())

    tokbuf[s] = tokpad[c]
    qbuf[s] = qpad[c]
    line[...] = jnp.zeros_like(line)
    first_row = pl.multiple_of(c * HALF_TOK, HALF_TOK)
    xb[0, 0, :, wide_b:wide_b + LANE] = square[pl.ds(first_row, HALF_TOK), :].astype(BF16)
    each(lambda j: token_copy(j).wait_recv())
    for i in range(n_seq):
        begin, turn = share * i // LANE * LANE, share * i % LANE
        span = tokpad.shape[2] + LANE
        value = jnp.concatenate(
            [tokbuf[i].astype(F32), jnp.zeros((HALF_TOK, LANE), F32)], axis=1
        )
        if turn:
            value = pltpu.roll(value, turn, 1)
        line[:, begin:begin + span] = line[:, begin:begin + span] + value
    xa[0, 0] = line[:, 0:wide_a].astype(BF16)
    xb[0, 0, :, 0:wide_b] = line[:, wide_a:wide_a + wide_b].astype(BF16)

    position = lax.broadcasted_iota(jnp.int32, (n_seq * heads, LANE), 1)

    def one_request(i, carry):
        head_rows = pl.ds(pl.multiple_of(i * heads, heads), heads)
        q = qf[:, head_rows, :].reshape(n_seq * heads, qf.shape[2]).astype(BF16)
        length = lengths[0, c * half_req + i]
        parts = []
        for side, base in ((0, s), (1, 2 * y + other)):
            score = jnp.dot(q, lbuf[side, i], preferred_element_type=F32) * SCALE
            valid = position + base * LANE < length
            parts.append((jnp.where(valid, score, NEG), valid))
        top = jnp.maximum(
            jnp.max(parts[0][0], axis=1, keepdims=True),
            jnp.max(parts[1][0], axis=1, keepdims=True),
        ).astype(BF16).astype(F32)
        total = jnp.zeros((n_seq * heads, 1), F32)
        context = jnp.zeros((n_seq * heads, LAT), F32)
        for side in range(2):
            score, valid = parts[side]
            w = jnp.where(valid, jnp.exp(score - top), 0.0)
            total = total + jnp.sum(w, axis=1, keepdims=True)
            context = context + lax.dot_general(
                w.astype(BF16), lbuf[side, i, 0:LAT, :], (((1,), (1,)), ((), ())),
                preferred_element_type=F32,
            )
        total_high = total.astype(BF16).astype(F32)
        note = jnp.where(
            position == 0,
            top,
            jnp.where(position == 1, total_high, jnp.where(position == 2, total - total_high, 0.0)),
        )
        at = pl.ds(pl.multiple_of(2 * heads * i, 2 * heads), 2 * heads)
        obuf[:, at, 0:LAT] = context.astype(BF16).reshape(n_y, 2 * heads, LAT)
        obuf[:, at, LAT:LAT + LANE] = note.astype(BF16).reshape(n_y, 2 * heads, LANE)
        return carry

    def one_context(i, carry):
        at = pl.ds(pl.multiple_of(2 * heads * i, 2 * heads), 2 * heads)
        head_rows = pl.ds(pl.multiple_of(i * heads, heads), heads)
        line_of = lax.broadcasted_iota(jnp.int32, fresh.shape, 0)
        chosen = jnp.where(line_of == c * half_req + i, fresh[...].astype(F32), 0.0)
        key = jnp.sum(chosen, axis=0, keepdims=True)
        q = qf[pl.ds(2 * y, 2), head_rows, :].reshape(2 * heads, qf.shape[2])
        own = jnp.sum(q * key, axis=1, keepdims=True) * SCALE
        notes = [orecv[j, at, LAT:LAT + LANE].astype(F32) for j in range(n_y)]
        top = own
        for note in notes:
            top = jnp.maximum(top, note[:, 0:1])
        w = jnp.exp(own - top)
        total, context = w, w * key[:, 0:LAT]
        for j, note in enumerate(notes):
            w = jnp.exp(note[:, 0:1] - top)
            total = total + w * (note[:, 1:2] + note[:, 2:3])
            context = context + w * orecv[j, at, 0:LAT].astype(F32)
        context = context / total
        for core in range(2):
            cf[core, head_rows, :] = context[core * heads:(core + 1) * heads]
        return carry

    def attend():
        yield net.now + 0.3
        loads[0].wait()
        each(lambda j: query_copy(j).wait_recv())
        lat_copy.wait_recv()
        qf[...] = qbuf[:, :, 0:width].astype(F32)
        lax.fori_loop(0, half_req // 2, one_request, 0)
        net.now += 2.0
        yield net.now + 0.5
        lax.fori_loop(half_req // 2, half_req, one_request, 0)
        net.now += 2.0
        came = []
        for j in range(1, n_y):
            to = lax.rem(y + j, n_y)
            came.append(net.copy(obuf.at[to], orecv.at[y], (2 * to + c, e), "y"))
        orecv[y] = obuf[y]
        yield net.now + 22.0
        for one, _ in came:
            one.wait_recv()
        lax.fori_loop(0, half_req, one_context, 0)
        net.now += 1.0
        cb[...] = cf[...].astype(BF16)
        back, when = net.copy(cb.at[other], crecv, sibling, "core")
        ctx_out[pl.ds(pl.multiple_of(c * q_rows, q_rows), q_rows), :] = cb[c]
        yield when + 5.0
        back.wait_recv()
        ctx_out[pl.ds(pl.multiple_of(other * q_rows, q_rows), q_rows), :] = crecv[...]

    half_a, half_b = wide_a // 2, wide_b // 2

    def cut_a(ref, side):
        lead = (slice(None),) * (len(ref.shape) - 1)
        return ref.at[lead + (pl.ds(side * half_a, half_a),)]

    def cut_b(ref, side):
        lead = (slice(None),) * (len(ref.shape) - 1)
        size = half_b if side == 0 else ref.shape[-1] - half_b
        return ref.at[lead + (pl.ds(side * half_b, size),)]

    teams = [(0,)] + [(d, -d) for d in range(1, n_z // 2)] + [(n_z // 2,)]

    pairs = [(i, i + 1) for i in range(0, NX, 2)]

    def slots(team):
        return pl.ds(slot_z[team[0]], len(team))

    def gather_z(piece, cut, done):
        if n_z == 8:
            return skip_gather(net, piece, cut, z_ups, z_downs, "z", done)
        return ring_gather(net, piece, cut, n_z, z_up, z_down, "z", done)

    def scatter_z(piece, cut, arrived, ready, finish):
        if n_z == 8:
            return skip_scatter(net, piece, cut, arrived, z_ups, z_downs, "z", ready, finish)
        return ring_scatter(net, piece, cut, arrived, n_z, z_up, z_down, "z", ready, finish)

    landed = {d: 0 for d in slot_z}

    def count(team):
        for d in team:
            landed[d] += 1

    def gather_a():
        here = set()

        def start(dx):
            here.add(slot_x[dx])
            for pair in pairs:
                if slot_x[dx] in pair and here.issuperset(pair):
                    net.add(net.now, along_z(pl.ds(pair[0], 2)))

        def along_z(at):
            return gather_z(lambda d: xa.at[slot_z[d], at], cut_a, lambda d: count((d,)))

        yield from ring_gather(
            net, lambda d: xa.at[0, slot_x[d]], cut_a, NX, x_up, x_down, "x", start
        )

    def gather_b():
        here = set()

        def start(dz):
            here.add(dz)
            team = [team for team in teams if dz in team][0]
            if here.issuperset(team):
                net.add(net.now, ring_gather(
                    net, lambda d: xb.at[slots(team), slot_x[d]], cut_b, NX, x_up, x_down, "x",
                    lambda d: count(team),
                ))

        yield from gather_z(lambda d: xb.at[slot_z[d], 0], cut_b, start)

    step_a, step_b = wide_a // 2, wide_b // 5
    def experts_of(first, last):
        rows = (last - first) * NX * HALF_TOK

        def beside(some):
            return jnp.concatenate([wcat[i, some, :] for i in range(4)], axis=1)

        def up_a(k, carry):
            cols = pl.ds(pl.multiple_of(k * step_a, step_a), step_a)
            value = xa[first:last, :, :, cols].reshape(rows, step_a)
            acc[0:rows, :] += jnp.dot(value, beside(cols), preferred_element_type=F32)
            return carry

        def up_b(k, carry):
            cols = pl.ds(pl.multiple_of(k * step_b, step_b), step_b)
            down = pl.ds(pl.multiple_of(wide_a + k * step_b, LANE), step_b)
            value = xb[first:last, :, :, cols].reshape(rows, step_b)
            acc[0:rows, :] += jnp.dot(value, beside(down), preferred_element_type=F32)
            return carry

        def down_a(k, carry):
            cols = pl.ds(pl.multiple_of(k * step_a, step_a), step_a)
            value = jnp.dot(hid[0:rows, :], wdcat[:, cols], preferred_element_type=F32)
            ya[first:last, :, :, cols] = value.astype(BF16).reshape(last - first, NX, HALF_TOK, step_a)
            return carry

        def down_b(k, carry):
            cols = pl.ds(pl.multiple_of(k * step_b, step_b), step_b)
            down = pl.ds(pl.multiple_of(wide_a + k * step_b, LANE), step_b)
            value = jnp.dot(hid[0:rows, :], wdcat[:, down], preferred_element_type=F32)
            yb[first:last, :, :, cols] = value.astype(BF16).reshape(last - first, NX, HALF_TOK, step_b)
            return carry

        acc[0:rows, :] = jnp.zeros((rows, 4 * LANE), F32)
        lax.fori_loop(0, 2, up_a, 0)
        lax.fori_loop(0, 5, up_b, 0)
        tile = xb[first:last, :, :, wide_b:wide_b + LANE].reshape(rows, LANE).astype(F32)
        lane = lax.broadcasted_iota(jnp.int32, (rows, LANE), 1)
        gate = jnp.sum(
            jnp.where((lane == e) | (lane == e + experts), tile, 0.0), axis=1, keepdims=True
        )
        g = acc[0:rows, 0:2 * LANE]
        value = g / (1.0 + jnp.exp(-g)) * acc[0:rows, 2 * LANE:4 * LANE] * gate
        hid[0:rows, :] = value.astype(BF16)
        lax.fori_loop(0, 5, down_b, 0)
        lax.fori_loop(0, 2, down_a, 0)

    def compute():
        offsets = around(n_z)
        groups = [(0, 5), (5, 8)] if n_z == 8 else [(0, len(offsets))]
        for first, last in groups:
            while any(landed[d] < len(pairs) + NX for d in offsets[first:last]):
                yield net.now + 0.01
            if first == 0:
                for load in loads[1:]:
                    load.wait()
                for made in weights:
                    made.wait_recv()
            experts_of(first, last)
            net.now += 1.0

    net.run([gather_a(), gather_b(), compute()])

    net.links, net.now = {}, 0.0
    ended = set()

    def always(d):
        return True

    def row_sum(team):
        at = slots(team)

        def finish(total):
            yb[at, 0] = total.astype(BF16)
            ended.update(team)

        return ring_scatter(
            net, lambda d: yb.at[at, slot_x[d]], cut_b, lambda way, k: rbx.at[way, k, at],
            NX, x_up, x_down, "x", always, finish,
        )

    done_a = set()

    def column_sum(pair):
        at = pl.ds(pair[0], 2)

        def finish(total):
            ya[0, at] = total.astype(BF16)
            done_a.update(pair)

        return scatter_z(
            lambda d: ya.at[slot_z[d], at], cut_a, lambda way, k: ra.at[way, k, at], always, finish
        )

    def end_a(total):
        line[:, 0:wide_a] = total

    def end_b(total):
        line[:, wide_a:wide_a + wide_b] = total

    sum_a = ring_scatter(
        net, lambda d: ya.at[0, slot_x[d]], cut_a, lambda way, k: rax.at[way, k],
        NX, x_up, x_down, "x", lambda d: slot_x[far_x if d == -far_x else d] in done_a, end_a,
    )

    sum_b = scatter_z(
        lambda d: yb.at[slot_z[d], 0], cut_b, lambda way, k: rb.at[way, k],
        lambda d: d in ended, end_b,
    )
    before = list(net.copies)

    def settle():
        yield net.now + 1.0
        each(lambda j: token_copy(j).wait_send())
        each(lambda j: query_copy(j).wait_send())
        for made in before:
            made.wait_send()

    first_rows = [row_sum(team) for team in reversed(teams)]
    columns = [column_sum(pair) for pair in reversed(pairs)]
    net.run(first_rows[:1] + columns + first_rows[1:] + [sum_a, sum_b, attend(), settle()])

    for i in range(n_seq):
        begin, turn = share * i // LANE * LANE, share * i % LANE
        span = tokpad.shape[2] + LANE
        value = line[:, begin:begin + span]
        if turn:
            value = pltpu.roll(value, span - turn, 1)
        ebuf[i] = value[:, 0:tokpad.shape[2]].astype(BF16)
    each(lambda j: end_copy(j).start())
    erecv[s] = ebuf[s]
    each(lambda j: end_copy(j).wait_recv())
    for half in range(2):
        total = erecv[half].astype(F32)
        for i in range(1, n_y):
            total = total + erecv[2 * i + half].astype(F32)
        mix_out[half * HALF_TOK:(half + 1) * HALF_TOK, :] = total[:, 0:share].astype(BF16)

    each(lambda j: end_copy(j).wait_send())
    for made in net.copies[len(before):]:
        made.wait_send()


def on_device(latent, lengths, queries, fresh_latent, tokens, routes, gates, w_gate, w_up, w_down):
    n_seq, n_ep = lax.axis_size("seq"), lax.axis_size("ep")
    n_z, n_y = n_ep // NX, n_seq // 2
    n_req, heads, width = queries.shape
    share = tokens.shape[1]
    features = share * n_seq
    wide_a = features // 7 * 2
    wide_b = features - wide_a
    padded = -(-share // LANE) * LANE
    wide_q = -(-width // LANE) * LANE
    rows = n_ep * HALF_TOK
    half_req = n_req // 2
    q_rows = half_req * heads
    far_z, far_x = n_z // 2, NX // 2
    cfg = (n_seq, n_z, wide_a, wide_b, share, heads)
    vmem = pl.BlockSpec(memory_space=pltpu.VMEM)
    hbm = pl.BlockSpec(memory_space=pl.ANY)
    dma = pltpu.SemaphoreType.DMA
    ffn = 2 * rows * features * 6 * LANE
    context, mixed = pl.pallas_call(
        functools.partial(kernel, cfg),
        out_shape=(
            jax.ShapeDtypeStruct((n_req * heads, LAT), BF16),
            jax.ShapeDtypeStruct(tokens.shape, BF16),
        ),
        in_specs=[hbm, vmem, hbm, hbm, hbm, pl.BlockSpec(memory_space=pltpu.SMEM), vmem, vmem, vmem, vmem],
        out_specs=(vmem, vmem),
        scratch_shapes=[
            pltpu.VMEM((2, HALF_TOK, padded), BF16),
            pltpu.VMEM((n_seq, HALF_TOK, padded), BF16),
            pltpu.VMEM((HALF_TOK, features + 2 * LANE), F32),
            pltpu.VMEM((LANE, LANE), F32),
            pltpu.VMEM((n_z, NX, HALF_TOK, wide_a), BF16),
            pltpu.VMEM((n_z, NX, HALF_TOK, wide_b + LANE), BF16),
            pltpu.VMEM((4, features, LANE), BF16),
            pltpu.VMEM((2 * LANE, features), BF16),
            pltpu.VMEM((rows, 4 * LANE), F32),
            pltpu.VMEM((rows, 2 * LANE), BF16),
            pltpu.VMEM((n_z, NX, HALF_TOK, wide_a), BF16),
            pltpu.VMEM((n_z, NX, HALF_TOK, wide_b), BF16),
            pltpu.VMEM((2, far_z, NX, HALF_TOK, wide_a), BF16),
            pltpu.VMEM((2, far_x, HALF_TOK, wide_a), BF16),
            pltpu.VMEM((2, far_x, n_z, HALF_TOK, wide_b), BF16),
            pltpu.VMEM((2, far_z, HALF_TOK, wide_b), BF16),
            pltpu.VMEM((n_seq, HALF_TOK, padded), BF16),
            pltpu.VMEM((n_seq, HALF_TOK, padded), BF16),
            pltpu.VMEM((2, half_req, width, LANE), BF16),
            pltpu.VMEM((2, q_rows, wide_q), BF16),
            pltpu.VMEM((n_seq, q_rows, wide_q), BF16),
            pltpu.VMEM((n_seq, q_rows, width), F32),
            pltpu.VMEM((n_y, 2 * q_rows, LAT + LANE), BF16),
            pltpu.VMEM((n_y, 2 * q_rows, LAT + LANE), BF16),
            pltpu.VMEM((2, q_rows, LAT), F32),
            pltpu.VMEM((2, q_rows, LAT), BF16),
            pltpu.VMEM((q_rows, LAT), BF16),
            dma((4,)),
            dma((120,)),
            dma((120,)),
            dma((n_seq,)),
            dma((n_seq,)),
            dma((n_seq,)),
            dma((n_seq,)),
            dma((n_seq,)),
            dma((n_seq,)),
        ],
        compiler_params=pltpu.CompilerParams(
            collective_id=0, has_side_effects=True, vmem_limit_bytes=56 * 1024 * 1024
        ),
        cost_estimate=pl.CostEstimate(flops=ffn, bytes_accessed=6 * 2**20, transcendentals=rows * 512),
    )(
        latent.transpose(0, 2, 1),
        queries.reshape(n_req * heads, width),
        w_gate[0],
        w_up[0],
        w_down[0],
        lengths,
        fresh_latent,
        tokens,
        routes.T,
        gates.T,
    )
    return context.reshape(n_req, heads, LAT), mixed


def solution(mesh):
    placed = (
        P("ep", "seq", None),
        P("ep", None),
        P("ep", "seq", None),
        P("ep", None),
        P("ep", "seq"),
        P("ep", None),
        P("ep", None),
        P("ep", None, "seq"),
        P("ep", None, "seq"),
        P("ep", "seq", None),
    )
    return jax.shard_map(
        on_device,
        mesh=mesh,
        in_specs=placed,
        out_specs=(P("ep", "seq", None), P("ep", "seq")),
        check_vma=False,
    )
```

```python
import functools
import heapq

import jax
import jax.numpy as jnp
from jax import lax
from jax.experimental import pallas as pl
from jax.experimental.pallas import tpu as pltpu
from jax.sharding import PartitionSpec as P

MESH = pl.DeviceIdType.MESH
LAT = 512
NX = 4
LANE = 128
HALF_TOK = 16
SCALE = 0.07216878364870322
NEG = -1.0e30
F32 = jnp.float32
BF16 = jnp.bfloat16

LINK_RATE = 45.0e3
HOP = 1.5


def mod(value, n):
    return lax.rem(value + n, n)


class Net:
    def __init__(self, send, recv):
        self.send, self.recv = send, recv
        self.count, self.now = 0, 0.0
        self.links, self.copies = {}, []

    def copy(self, src, dst, device, link):
        at = self.count
        self.count += 1
        made = pltpu.make_async_remote_copy(
            src_ref=src,
            dst_ref=dst,
            send_sem=self.send.at[at],
            recv_sem=self.recv.at[at],
            device_id=device,
            device_id_type=MESH,
        )
        made.start()
        size = 2
        for extent in src.shape:
            size *= extent
        begin = max(self.links.get(link, 0.0), self.now)
        self.links[link] = begin + size / LINK_RATE
        self.copies.append(made)
        return made, self.links[link] + HOP

    def run(self, tasks):
        self.heap, self.order = [], 0
        for task in tasks:
            self.add(self.now, task)
        while self.heap:
            at, _, task = heapq.heappop(self.heap)
            self.now = max(self.now, at)
            try:
                ready = next(task)
            except StopIteration:
                continue
            self.add(ready, task)

    def add(self, at, task):
        self.order += 1
        heapq.heappush(self.heap, (at, self.order, task))


def around(n):
    offsets = [0]
    for k in range(1, n // 2):
        offsets += [k, -k]
    return offsets + [n // 2]


def ring_gather(net, piece, cut, n, up, down, axis, landed):
    far = n // 2

    def pass_on(side, k):
        src, dst = piece((k, -k)[1 - side]), piece(far if k + 1 == far else (k + 1, -k - 1)[1 - side])
        if k + 1 == far:
            src, dst = cut(src, side), cut(dst, side)
        return net.copy(src, dst, (up, down)[side], axis + "+-"[side])

    cu, tu = pass_on(0, 0)
    cd, td = pass_on(1, 0)
    landed(0)
    for k in range(1, far):
        yield tu
        cu.wait_recv()
        cu, tu = pass_on(0, k)
        landed(-k)
        yield td
        cd.wait_recv()
        cd, td = pass_on(1, k)
        landed(k)
    yield max(tu, td)
    cu.wait_recv()
    cd.wait_recv()
    landed(far)


def add_into(ref, other):
    ref[...] = ref[...] + other[...]


def ring_scatter(net, piece, cut, arrived, n, up, down, axis, ready, finish):
    far = n // 2
    while not ready(far):
        yield net.now + 0.01
    cu, tu = net.copy(cut(piece(far), 0), cut(arrived(0, 0), 0), up, axis + "+")
    cd, td = net.copy(cut(piece(far), 1), cut(arrived(1, 0), 1), down, axis + "-")
    for k in range(1, far):
        d = far - k
        while not (ready(d) and ready(-d)):
            yield net.now + 0.01
        yield tu
        cu.wait_recv()
        mine, came = piece(d), arrived(0, k - 1)
        if k == 1:
            mine, came = cut(mine, 0), cut(came, 0)
        add_into(mine, came)
        cu, tu = net.copy(piece(d), arrived(0, k), up, axis + "+")
        yield td
        cd.wait_recv()
        mine, came = piece(-d), arrived(1, k - 1)
        if k == 1:
            mine, came = cut(mine, 1), cut(came, 1)
        add_into(mine, came)
        cd, td = net.copy(piece(-d), arrived(1, k), down, axis + "-")
    while not ready(0):
        yield net.now + 0.01
    yield max(tu, td)
    cu.wait_recv()
    cd.wait_recv()
    if far == 1:
        add_into(cut(piece(0), 0), cut(arrived(0, 0), 0))
        add_into(cut(piece(0), 1), cut(arrived(1, 0), 1))
        finish(piece(0)[...].astype(F32))
    else:
        finish(
            piece(0)[...].astype(F32)
            + arrived(0, far - 1)[...].astype(F32)
            + arrived(1, far - 1)[...].astype(F32)
        )


def kernel(
    cfg,
    latent, queries, wg, wu, wd, lengths, fresh, tokens, routes, gates,
    ctx_out, mix_out,
    tokpad, tokbuf, line, square, xa, xb, wcat, wdcat, acc, hid, ya, yb,
    ra, rax, rbx, rb, ebuf, erecv,
    lbuf, qbuf, qf, obuf, orecv, cf, cb, crecv,
    local_sem, send_sem, recv_sem, t_send, t_recv, q_send, q_recv, e_send, e_recv,
):
    n_seq, n_z, wide_a, wide_b, share, heads = cfg
    n_y = n_seq // 2
    s, e = lax.axis_index("seq"), lax.axis_index("ep")
    y, c = s // 2, lax.rem(s, 2)
    z, x = e // NX, lax.rem(e, NX)
    other = 1 - c
    sibling = (2 * y + other, e)
    experts = n_z * NX
    n_req = lengths.shape[1]
    half_req = n_req // 2
    q_rows = half_req * heads
    turn = 1 - 2 * c
    x_up, x_down = (s, z * NX + mod(x + turn, NX)), (s, z * NX + mod(x - turn, NX))
    z_up, z_down = (s, mod(z + turn, n_z) * NX + x), (s, mod(z - turn, n_z) * NX + x)
    slot_z = {d: i for i, d in enumerate(around(n_z))}
    slot_x = {d: i for i, d in enumerate(around(NX))}

    def local(src, dst, i):
        made = pltpu.make_async_copy(src, dst, local_sem.at[i])
        made.start()
        return made

    for half in range(2):
        tokpad[half] = jnp.zeros_like(tokpad[half])
        tokpad[half, :, 0:share] = tokens[half * HALF_TOK:(half + 1) * HALF_TOK, :]

    barrier = pltpu.get_barrier_semaphore()

    def greet(j, carry):
        pl.semaphore_signal(
            barrier, inc=1, device_id=(lax.rem(s + j, n_seq), e), device_id_type=MESH
        )
        return carry

    lax.fori_loop(1, n_seq, greet, 0)
    for who in (x_up, x_down, z_up, z_down):
        pl.semaphore_signal(barrier, inc=1, device_id=who, device_id_type=MESH)

    mine_q = queries.at[pl.ds(pl.multiple_of(c * q_rows, q_rows), q_rows)]
    loads = [
        local(mine_q, qbuf.at[s], 0),
        local(latent.at[pl.ds(c * half_req, half_req)], lbuf.at[0], 1),
        local(wg, wcat.at[:, pl.ds(0, LANE)], 2),
        local(wu, wcat.at[:, pl.ds(2 * LANE, LANE)], 3),
        local(wd, wdcat.at[pl.ds(0, LANE)], 4),
    ]

    row = lax.broadcasted_iota(jnp.int32, (LANE, routes.shape[1]), 0)
    named = jnp.where(row < experts, row, row - experts)
    weight = jnp.zeros(named.shape, F32)
    for k in range(routes.shape[0]):
        weight = weight + jnp.where(named == routes[k:k + 1, :], gates[k:k + 1, :], 0.0)
    high = weight.astype(BF16).astype(F32)
    weight = jnp.where(row < experts, high, jnp.where(row < 2 * experts, weight - high, 0.0))
    square[...] = jnp.zeros_like(square)
    square[:, 0:routes.shape[1]] = weight
    square[...] = jnp.transpose(square[...])

    pl.semaphore_wait(barrier, n_seq - 1 + 4)

    def token_copy(j):
        to = lax.rem(s + j, n_seq)
        return pltpu.make_async_remote_copy(
            src_ref=tokpad.at[lax.rem(to, 2)],
            dst_ref=tokbuf.at[s],
            send_sem=t_send.at[j],
            recv_sem=t_recv.at[j],
            device_id=(to, e),
            device_id_type=MESH,
        )

    def query_copy(j):
        to = lax.rem(s + j, n_seq)
        begin = pl.multiple_of(lax.rem(to, 2) * q_rows, q_rows)
        return pltpu.make_async_remote_copy(
            src_ref=queries.at[pl.ds(begin, q_rows)],
            dst_ref=qbuf.at[s],
            send_sem=q_send.at[j],
            recv_sem=q_recv.at[j],
            device_id=(to, e),
            device_id_type=MESH,
        )

    def end_copy(j):
        to = lax.rem(s + j, n_seq)
        return pltpu.make_async_remote_copy(
            src_ref=ebuf.at[to],
            dst_ref=erecv.at[s],
            send_sem=e_send.at[j],
            recv_sem=e_recv.at[j],
            device_id=(to, e),
            device_id_type=MESH,
        )

    def each(act):
        def body(j, carry):
            act(j)
            return carry

        lax.fori_loop(1, n_seq, body, 0)

    net = Net(send_sem, recv_sem)
    each(lambda j: token_copy(j).start())
    each(lambda j: query_copy(j).start())
    lat_copy, _ = net.copy(latent.at[pl.ds(other * half_req, half_req)], lbuf.at[1], sibling, "core")

    tokbuf[s] = tokpad[c]
    line[...] = jnp.zeros_like(line)
    first_row = pl.multiple_of(c * HALF_TOK, HALF_TOK)
    xb[0, 0, :, wide_b:wide_b + LANE] = square[pl.ds(first_row, HALF_TOK), :].astype(BF16)
    each(lambda j: token_copy(j).wait_recv())
    for i in range(n_seq):
        begin, turn = share * i // LANE * LANE, share * i % LANE
        span = tokpad.shape[2] + LANE
        value = jnp.concatenate(
            [tokbuf[i].astype(F32), jnp.zeros((HALF_TOK, LANE), F32)], axis=1
        )
        if turn:
            value = pltpu.roll(value, turn, 1)
        line[:, begin:begin + span] = line[:, begin:begin + span] + value
    xa[0, 0] = line[:, 0:wide_a].astype(BF16)
    xb[0, 0, :, 0:wide_b] = line[:, wide_a:wide_a + wide_b].astype(BF16)

    position = lax.broadcasted_iota(jnp.int32, (n_seq * heads, LANE), 1)

    def one_request(i, carry):
        head_rows = pl.ds(pl.multiple_of(i * heads, heads), heads)
        q = qf[:, head_rows, :].reshape(n_seq * heads, qf.shape[2]).astype(BF16)
        length = lengths[0, c * half_req + i]
        parts = []
        for side, base in ((0, s), (1, 2 * y + other)):
            score = jnp.dot(q, lbuf[side, i], preferred_element_type=F32) * SCALE
            valid = position + base * LANE < length
            parts.append((jnp.where(valid, score, NEG), valid))
        top = jnp.maximum(
            jnp.max(parts[0][0], axis=1, keepdims=True),
            jnp.max(parts[1][0], axis=1, keepdims=True),
        ).astype(BF16).astype(F32)
        total = jnp.zeros((n_seq * heads, 1), F32)
        context = jnp.zeros((n_seq * heads, LAT), F32)
        for side in range(2):
            score, valid = parts[side]
            w = jnp.where(valid, jnp.exp(score - top), 0.0)
            total = total + jnp.sum(w, axis=1, keepdims=True)
            context = context + lax.dot_general(
                w.astype(BF16), lbuf[side, i, 0:LAT, :], (((1,), (1,)), ((), ())),
                preferred_element_type=F32,
            )
        total_high = total.astype(BF16).astype(F32)
        note = jnp.where(
            position == 0,
            top,
            jnp.where(position == 1, total_high, jnp.where(position == 2, total - total_high, 0.0)),
        )
        at = pl.ds(pl.multiple_of(2 * heads * i, 2 * heads), 2 * heads)
        obuf[:, at, 0:LAT] = context.astype(BF16).reshape(n_y, 2 * heads, LAT)
        obuf[:, at, LAT:LAT + LANE] = note.astype(BF16).reshape(n_y, 2 * heads, LANE)
        return carry

    def one_context(i, carry):
        at = pl.ds(pl.multiple_of(2 * heads * i, 2 * heads), 2 * heads)
        head_rows = pl.ds(pl.multiple_of(i * heads, heads), heads)
        line_of = lax.broadcasted_iota(jnp.int32, fresh.shape, 0)
        chosen = jnp.where(line_of == c * half_req + i, fresh[...].astype(F32), 0.0)
        key = jnp.sum(chosen, axis=0, keepdims=True)
        q = qf[pl.ds(2 * y, 2), head_rows, :].reshape(2 * heads, qf.shape[2])
        own = jnp.sum(q * key, axis=1, keepdims=True) * SCALE
        notes = [orecv[j, at, LAT:LAT + LANE].astype(F32) for j in range(n_y)]
        top = own
        for note in notes:
            top = jnp.maximum(top, note[:, 0:1])
        w = jnp.exp(own - top)
        total, context = w, w * key[:, 0:LAT]
        for j, note in enumerate(notes):
            w = jnp.exp(note[:, 0:1] - top)
            total = total + w * (note[:, 1:2] + note[:, 2:3])
            context = context + w * orecv[j, at, 0:LAT].astype(F32)
        context = context / total
        for core in range(2):
            cf[core, head_rows, :] = context[core * heads:(core + 1) * heads]
        return carry

    def attend():
        yield net.now + 8.0
        loads[0].wait()
        loads[1].wait()
        each(lambda j: query_copy(j).wait_recv())
        lat_copy.wait_recv()
        qf[...] = qbuf[...].astype(F32)
        lax.fori_loop(0, half_req // 2, one_request, 0)
        net.now += 2.0
        yield net.now + 0.5
        lax.fori_loop(half_req // 2, half_req, one_request, 0)
        net.now += 2.0
        came = []
        for j in range(1, n_y):
            to = lax.rem(y + j, n_y)
            came.append(net.copy(obuf.at[to], orecv.at[y], (2 * to + c, e), "y"))
        orecv[y] = obuf[y]
        yield net.now + 25.0
        for one, _ in came:
            one.wait_recv()
        lax.fori_loop(0, half_req, one_context, 0)
        net.now += 1.0
        cb[...] = cf[...].astype(BF16)
        back, when = net.copy(cb.at[other], crecv, sibling, "core")
        ctx_out[pl.ds(pl.multiple_of(c * q_rows, q_rows), q_rows), :] = cb[c]
        yield when + 5.0
        back.wait_recv()
        ctx_out[pl.ds(pl.multiple_of(other * q_rows, q_rows), q_rows), :] = crecv[...]

    half_a, half_b = wide_a // 2, wide_b // 2

    def cut_a(ref, side):
        lead = (slice(None),) * (len(ref.shape) - 1)
        return ref.at[lead + (pl.ds(side * half_a, half_a),)]

    def cut_b(ref, side):
        lead = (slice(None),) * (len(ref.shape) - 1)
        size = half_b if side == 0 else ref.shape[-1] - half_b
        return ref.at[lead + (pl.ds(side * half_b, size),)]

    teams = [(0,)] + [(d, -d) for d in range(1, n_z // 2)] + [(n_z // 2,)]

    def slots(team):
        return pl.ds(slot_z[team[0]], len(team))

    landed = {d: 0 for d in slot_z}

    def count(team):
        for d in team:
            landed[d] += 1

    def gather_a():
        yield from ring_gather(
            net, lambda d: xa.at[0, slot_x[d]], cut_a, NX, x_up, x_down, "x", lambda d: None
        )
        yield from ring_gather(
            net, lambda d: xa.at[slot_z[d]], cut_a, n_z, z_up, z_down, "z", lambda d: count((d,))
        )

    def gather_b():
        here = set()

        def start(dz):
            here.add(dz)
            team = [team for team in teams if dz in team][0]
            if here.issuperset(team):
                net.add(net.now, ring_gather(
                    net, lambda d: xb.at[slots(team), slot_x[d]], cut_b, NX, x_up, x_down, "x",
                    lambda d: count(team),
                ))

        yield from ring_gather(
            net, lambda d: xb.at[slot_z[d], 0], cut_b, n_z, z_up, z_down, "z", start
        )

    step_a, step_b = wide_a // 3, wide_b // 4
    weights = []

    def load_weights():
        yield net.now + 0.5
        for src, dst in (
            (wg, wcat.at[:, pl.ds(LANE, LANE)]),
            (wu, wcat.at[:, pl.ds(3 * LANE, LANE)]),
            (wd, wdcat.at[pl.ds(LANE, LANE)]),
        ):
            weights.append(net.copy(src, dst, sibling, "core")[0])

    def experts_of(first, last):
        rows = (last - first) * NX * HALF_TOK

        def up_a(k, carry):
            cols = pl.ds(pl.multiple_of(k * step_a, step_a), step_a)
            value = xa[first:last, :, :, cols].reshape(rows, step_a)
            acc[0:rows, :] += jnp.dot(value, wcat[cols, :], preferred_element_type=F32)
            return carry

        def up_b(k, carry):
            cols = pl.ds(pl.multiple_of(k * step_b, step_b), step_b)
            down = pl.ds(pl.multiple_of(wide_a + k * step_b, step_b), step_b)
            value = xb[first:last, :, :, cols].reshape(rows, step_b)
            acc[0:rows, :] += jnp.dot(value, wcat[down, :], preferred_element_type=F32)
            return carry

        def down_a(k, carry):
            cols = pl.ds(pl.multiple_of(k * step_a, step_a), step_a)
            value = jnp.dot(hid[0:rows, :], wdcat[:, cols], preferred_element_type=F32)
            ya[first:last, :, :, cols] = value.astype(BF16).reshape(last - first, NX, HALF_TOK, step_a)
            return carry

        def down_b(k, carry):
            cols = pl.ds(pl.multiple_of(k * step_b, step_b), step_b)
            down = pl.ds(pl.multiple_of(wide_a + k * step_b, step_b), step_b)
            value = jnp.dot(hid[0:rows, :], wdcat[:, down], preferred_element_type=F32)
            yb[first:last, :, :, cols] = value.astype(BF16).reshape(last - first, NX, HALF_TOK, step_b)
            return carry

        acc[0:rows, :] = jnp.zeros((rows, 4 * LANE), F32)
        lax.fori_loop(0, 3, up_a, 0)
        lax.fori_loop(0, 4, up_b, 0)
        tile = xb[first:last, :, :, wide_b:wide_b + LANE].reshape(rows, LANE).astype(F32)
        lane = lax.broadcasted_iota(jnp.int32, (rows, LANE), 1)
        gate = jnp.sum(
            jnp.where((lane == e) | (lane == e + experts), tile, 0.0), axis=1, keepdims=True
        )
        g = acc[0:rows, 0:2 * LANE]
        value = g / (1.0 + jnp.exp(-g)) * acc[0:rows, 2 * LANE:4 * LANE] * gate
        hid[0:rows, :] = value.astype(BF16)
        lax.fori_loop(0, 4, down_b, 0)
        lax.fori_loop(0, 3, down_a, 0)

    def compute():
        offsets = around(n_z)
        groups = [(0, 3), (3, 5), (5, 7), (7, 8)] if n_z == 8 else [(0, len(offsets))]
        for first, last in groups:
            while any(landed[d] < 1 + NX for d in offsets[first:last]):
                yield net.now + 0.01
            if first == 0:
                for load in loads[2:]:
                    load.wait()
                for made in weights:
                    made.wait_recv()
            experts_of(first, last)
            net.now += 1.0

    attention = attend()
    net.run([gather_a(), gather_b(), load_weights(), sample(attention, 3), compute()])

    net.links, net.now = {}, 0.0
    ended = set()

    def always(d):
        return True

    def row_sum(team):
        at = slots(team)

        def finish(total):
            yb[at, 0] = total.astype(BF16)
            ended.update(team)

        return ring_scatter(
            net, lambda d: yb.at[at, slot_x[d]], cut_b, lambda way, k: rbx.at[way, k, at],
            NX, x_up, x_down, "x", always, finish,
        )

    def keep_a(total):
        ya[0] = total.astype(BF16)

    def end_a(total):
        line[:, 0:wide_a] = total

    def end_b(total):
        line[:, wide_a:wide_a + wide_b] = total

    def sum_a():
        yield from ring_scatter(
            net, lambda d: ya.at[slot_z[d]], cut_a, lambda way, k: ra.at[way, k],
            n_z, z_up, z_down, "z", always, keep_a,
        )
        yield from ring_scatter(
            net, lambda d: ya.at[0, slot_x[d]], cut_a, lambda way, k: rax.at[way, k],
            NX, x_up, x_down, "x", always, end_a,
        )

    sum_b = ring_scatter(
        net, lambda d: yb.at[slot_z[d], 0], cut_b, lambda way, k: rb.at[way, k],
        n_z, z_up, z_down, "z", lambda d: d in ended, end_b,
    )
    before = list(net.copies)

    def settle():
        yield net.now + 1.0
        each(lambda j: token_copy(j).wait_send())
        each(lambda j: query_copy(j).wait_send())
        for made in before:
            made.wait_send()

    first_rows = [row_sum(team) for team in reversed(teams)]
    net.run(first_rows[:1] + [sum_a()] + first_rows[1:] + [sum_b, sample(attention, 9), settle()])

    for i in range(n_seq):
        begin, turn = share * i // LANE * LANE, share * i % LANE
        span = tokpad.shape[2] + LANE
        value = line[:, begin:begin + span]
        if turn:
            value = pltpu.roll(value, span - turn, 1)
        ebuf[i] = value[:, 0:tokpad.shape[2]].astype(BF16)
    each(lambda j: end_copy(j).start())
    erecv[s] = ebuf[s]
    each(lambda j: end_copy(j).wait_recv())
    for half in range(2):
        total = erecv[half].astype(F32)
        for i in range(1, n_y):
            total = total + erecv[2 * i + half].astype(F32)
        mix_out[half * HALF_TOK:(half + 1) * HALF_TOK, :] = total[:, 0:share].astype(BF16)

    each(lambda j: end_copy(j).wait_send())
    for made in net.copies[len(before):]:
        made.wait_send()


def sample(task, most):
    for _ in range(most):
        try:
            ready = next(task)
        except StopIteration:
            return
        yield ready


def on_device(latent, lengths, queries, fresh_latent, tokens, routes, gates, w_gate, w_up, w_down):
    n_seq, n_ep = lax.axis_size("seq"), lax.axis_size("ep")
    n_z, n_y = n_ep // NX, n_seq // 2
    n_req, heads, width = queries.shape
    share = tokens.shape[1]
    features = share * n_seq
    wide_a = features // 7 * 3
    wide_b = features - wide_a
    padded = -(-share // LANE) * LANE
    rows = n_ep * HALF_TOK
    half_req = n_req // 2
    q_rows = half_req * heads
    far_z, far_x = n_z // 2, NX // 2
    cfg = (n_seq, n_z, wide_a, wide_b, share, heads)
    vmem = pl.BlockSpec(memory_space=pltpu.VMEM)
    hbm = pl.BlockSpec(memory_space=pl.ANY)
    dma = pltpu.SemaphoreType.DMA
    ffn = 2 * rows * features * 6 * LANE
    context, mixed = pl.pallas_call(
        functools.partial(kernel, cfg),
        out_shape=(
            jax.ShapeDtypeStruct((n_req * heads, LAT), BF16),
            jax.ShapeDtypeStruct(tokens.shape, BF16),
        ),
        in_specs=[hbm, hbm, hbm, hbm, hbm, pl.BlockSpec(memory_space=pltpu.SMEM), vmem, vmem, vmem, vmem],
        out_specs=(vmem, vmem),
        scratch_shapes=[
            pltpu.VMEM((2, HALF_TOK, padded), BF16),
            pltpu.VMEM((n_seq, HALF_TOK, padded), BF16),
            pltpu.VMEM((HALF_TOK, features + 2 * LANE), F32),
            pltpu.VMEM((LANE, LANE), F32),
            pltpu.VMEM((n_z, NX, HALF_TOK, wide_a), BF16),
            pltpu.VMEM((n_z, NX, HALF_TOK, wide_b + LANE), BF16),
            pltpu.VMEM((features, 4 * LANE), BF16),
            pltpu.VMEM((2 * LANE, features), BF16),
            pltpu.VMEM((rows, 4 * LANE), F32),
            pltpu.VMEM((rows, 2 * LANE), BF16),
            pltpu.VMEM((n_z, NX, HALF_TOK, wide_a), BF16),
            pltpu.VMEM((n_z, NX, HALF_TOK, wide_b), BF16),
            pltpu.VMEM((2, far_z, NX, HALF_TOK, wide_a), BF16),
            pltpu.VMEM((2, far_x, HALF_TOK, wide_a), BF16),
            pltpu.VMEM((2, far_x, n_z, HALF_TOK, wide_b), BF16),
            pltpu.VMEM((2, far_z, HALF_TOK, wide_b), BF16),
            pltpu.VMEM((n_seq, HALF_TOK, padded), BF16),
            pltpu.VMEM((n_seq, HALF_TOK, padded), BF16),
            pltpu.VMEM((2, half_req, width, LANE), BF16),
            pltpu.VMEM((n_seq, q_rows, width), BF16),
            pltpu.VMEM((n_seq, q_rows, width), F32),
            pltpu.VMEM((n_y, 2 * q_rows, LAT + LANE), BF16),
            pltpu.VMEM((n_y, 2 * q_rows, LAT + LANE), BF16),
            pltpu.VMEM((2, q_rows, LAT), F32),
            pltpu.VMEM((2, q_rows, LAT), BF16),
            pltpu.VMEM((q_rows, LAT), BF16),
            dma((5,)),
            dma((120,)),
            dma((120,)),
            dma((n_seq,)),
            dma((n_seq,)),
            dma((n_seq,)),
            dma((n_seq,)),
            dma((n_seq,)),
            dma((n_seq,)),
        ],
        compiler_params=pltpu.CompilerParams(
            collective_id=0, has_side_effects=True, vmem_limit_bytes=56 * 1024 * 1024
        ),
        cost_estimate=pl.CostEstimate(flops=ffn, bytes_accessed=6 * 2**20, transcendentals=rows * 512),
    )(
        latent.transpose(0, 2, 1),
        queries.reshape(n_req * heads, width),
        w_gate[0],
        w_up[0],
        w_down[0],
        lengths,
        fresh_latent,
        tokens,
        routes.T,
        gates.T,
    )
    return context.reshape(n_req, heads, LAT), mixed


def solution(mesh):
    placed = (
        P("ep", "seq", None),
        P("ep", None),
        P("ep", "seq", None),
        P("ep", None),
        P("ep", "seq"),
        P("ep", None),
        P("ep", None),
        P("ep", None, "seq"),
        P("ep", None, "seq"),
        P("ep", "seq", None),
    )
    return jax.shard_map(
        on_device,
        mesh=mesh,
        in_specs=placed,
        out_specs=(P("ep", "seq", None), P("ep", "seq")),
        check_vma=False,
    )
```

```python
import functools
import heapq

import jax
import jax.numpy as jnp
from jax import lax
from jax.experimental import pallas as pl
from jax.experimental.pallas import tpu as pltpu
from jax.sharding import PartitionSpec as P

MESH = pl.DeviceIdType.MESH
LAT = 512
NX = 4
LANE = 128
HALF_TOK = 16
SCALE = 0.07216878364870322
NEG = -1.0e30
F32 = jnp.float32
BF16 = jnp.bfloat16

LINK_RATE = 45.0e3
HOP = 1.5


def mod(value, n):
    return lax.rem(value + n, n)


class Net:
    def __init__(self, send, recv):
        self.send, self.recv = send, recv
        self.count, self.now = 0, 0.0
        self.links, self.copies = {}, []

    def copy(self, src, dst, device, link, hops=1):
        at = self.count
        self.count += 1
        made = pltpu.make_async_remote_copy(
            src_ref=src,
            dst_ref=dst,
            send_sem=self.send.at[at],
            recv_sem=self.recv.at[at],
            device_id=device,
            device_id_type=MESH,
        )
        made.start()
        size = 2 * hops
        for extent in src.shape:
            size *= extent
        begin = max(self.links.get(link, 0.0), self.now)
        self.links[link] = begin + size / LINK_RATE
        self.copies.append(made)
        return made, self.links[link] + HOP

    def run(self, tasks):
        self.heap, self.order = [], 0
        for task in tasks:
            self.add(self.now, task)
        while self.heap:
            at, _, task = heapq.heappop(self.heap)
            self.now = max(self.now, at)
            try:
                ready = next(task)
            except StopIteration:
                continue
            self.add(ready, task)

    def add(self, at, task):
        self.order += 1
        heapq.heappush(self.heap, (at, self.order, task))


def around(n):
    offsets = [0]
    for k in range(1, n // 2):
        offsets += [k, -k]
    return offsets + [n // 2]


def ring_gather(net, piece, cut, n, up, down, axis, landed):
    far = n // 2

    def pass_on(side, k):
        src, dst = piece((k, -k)[1 - side]), piece(far if k + 1 == far else (k + 1, -k - 1)[1 - side])
        if k + 1 == far:
            src, dst = cut(src, side), cut(dst, side)
        return net.copy(src, dst, (up, down)[side], axis + "+-"[side])

    cu, tu = pass_on(0, 0)
    cd, td = pass_on(1, 0)
    landed(0)
    for k in range(1, far):
        yield tu
        cu.wait_recv()
        cu, tu = pass_on(0, k)
        landed(-k)
        yield td
        cd.wait_recv()
        cd, td = pass_on(1, k)
        landed(k)
    yield max(tu, td)
    cu.wait_recv()
    cd.wait_recv()
    landed(far)


def skip_gather(net, piece, cut, ups, downs, axis, landed):
    def send(src, at, way, hops, side=None):
        dst = piece(at)
        if side is not None:
            src, dst = cut(src, side), cut(dst, side)
        return net.copy(src, dst, way[hops - 1], axis + ("+" if way is ups else "-"), hops)

    c2u, t2u = send(piece(0), -2, ups, 2)
    c2d, t2d = send(piece(0), 2, downs, 2)
    c1u, t1u = send(piece(0), -1, ups, 1)
    c1d, t1d = send(piece(0), 1, downs, 1)
    landed(0)
    yield t2u
    c2u.wait_recv()
    c4u, t4u = send(piece(-2), 4, ups, 2, 0)
    c3u, t3u = send(piece(-2), -3, ups, 1)
    landed(-2)
    yield t2d
    c2d.wait_recv()
    c4d, t4d = send(piece(2), 4, downs, 2, 1)
    c3d, t3d = send(piece(2), 3, downs, 1)
    landed(2)
    yield t1u
    c1u.wait_recv()
    landed(-1)
    yield t1d
    c1d.wait_recv()
    landed(1)
    yield max(t3u, t3d)
    c3u.wait_recv()
    landed(-3)
    c3d.wait_recv()
    landed(3)
    yield max(t4u, t4d)
    c4u.wait_recv()
    c4d.wait_recv()
    landed(4)


def skip_scatter(net, piece, cut, arrived, ups, downs, axis, ready, finish):
    up, down = axis + "+", axis + "-"
    while not (ready(4) and ready(3) and ready(-3)):
        yield net.now + 0.01
    c4u, t4u = net.copy(cut(piece(4), 0), cut(arrived(0, 0), 0), ups[1], up, 2)
    c4d, t4d = net.copy(cut(piece(4), 1), cut(arrived(1, 0), 1), downs[1], down, 2)
    c3u, t3u = net.copy(piece(3), arrived(0, 1), ups[0], up)
    c3d, t3d = net.copy(piece(-3), arrived(1, 1), downs[0], down)
    while not (ready(2) and ready(-2)):
        yield net.now + 0.01
    yield max(t4u, t3u)
    c4u.wait_recv()
    c3u.wait_recv()
    add_into(cut(piece(2), 0), cut(arrived(0, 0), 0))
    add_into(piece(2), arrived(0, 1))
    c2u, t2u = net.copy(piece(2), arrived(0, 2), ups[1], up, 2)
    yield max(t4d, t3d)
    c4d.wait_recv()
    c3d.wait_recv()
    add_into(cut(piece(-2), 1), cut(arrived(1, 0), 1))
    add_into(piece(-2), arrived(1, 1))
    c2d, t2d = net.copy(piece(-2), arrived(1, 2), downs[1], down, 2)
    while not (ready(1) and ready(-1)):
        yield net.now + 0.01
    c1u, t1u = net.copy(piece(1), arrived(0, 3), ups[0], up)
    c1d, t1d = net.copy(piece(-1), arrived(1, 3), downs[0], down)
    while not ready(0):
        yield net.now + 0.01
    yield max(t2u, t2d, t1u, t1d)
    total = piece(0)[...].astype(F32)
    for k, (one, two) in ((3, (c1u, c1d)), (2, (c2u, c2d))):
        one.wait_recv()
        two.wait_recv()
        total = total + arrived(0, k)[...].astype(F32) + arrived(1, k)[...].astype(F32)
    finish(total)


def add_into(ref, other):
    ref[...] = ref[...] + other[...]


def ring_scatter(net, piece, cut, arrived, n, up, down, axis, ready, finish):
    far = n // 2
    while not ready(far):
        yield net.now + 0.01
    cu, tu = net.copy(cut(piece(far), 0), cut(arrived(0, 0), 0), up, axis + "+")
    cd, td = net.copy(cut(piece(far), 1), cut(arrived(1, 0), 1), down, axis + "-")
    for k in range(1, far):
        d = far - k
        while not (ready(d) and ready(-d)):
            yield net.now + 0.01
        yield tu
        cu.wait_recv()
        mine, came = piece(d), arrived(0, k - 1)
        if k == 1:
            mine, came = cut(mine, 0), cut(came, 0)
        add_into(mine, came)
        cu, tu = net.copy(piece(d), arrived(0, k), up, axis + "+")
        yield td
        cd.wait_recv()
        mine, came = piece(-d), arrived(1, k - 1)
        if k == 1:
            mine, came = cut(mine, 1), cut(came, 1)
        add_into(mine, came)
        cd, td = net.copy(piece(-d), arrived(1, k), down, axis + "-")
    while not ready(0):
        yield net.now + 0.01
    yield max(tu, td)
    cu.wait_recv()
    cd.wait_recv()
    if far == 1:
        add_into(cut(piece(0), 0), cut(arrived(0, 0), 0))
        add_into(cut(piece(0), 1), cut(arrived(1, 0), 1))
        finish(piece(0)[...].astype(F32))
    else:
        finish(
            piece(0)[...].astype(F32)
            + arrived(0, far - 1)[...].astype(F32)
            + arrived(1, far - 1)[...].astype(F32)
        )


def kernel(
    cfg,
    latent, queries, wg, wu, wd, lengths, fresh, tokens, routes, gates,
    ctx_out, mix_out,
    tokpad, tokbuf, line, square, xa, xb, wcat, wdcat, acc, hid, ya, yb,
    ra, rax, rbx, rb, ebuf, erecv,
    lbuf, qpad, qbuf, qf, obuf, orecv, cf, cb, crecv,
    local_sem, send_sem, recv_sem, t_send, t_recv, q_send, q_recv, e_send, e_recv,
):
    n_seq, n_z, wide_a, wide_b, share, heads = cfg
    n_y = n_seq // 2
    s, e = lax.axis_index("seq"), lax.axis_index("ep")
    y, c = s // 2, lax.rem(s, 2)
    z, x = e // NX, lax.rem(e, NX)
    other = 1 - c
    sibling = (2 * y + other, e)
    experts = n_z * NX
    far_x = NX // 2
    n_req = lengths.shape[1]
    half_req = n_req // 2
    q_rows = half_req * heads
    x_up, x_down = (s, z * NX + mod(x + 1, NX)), (s, z * NX + mod(x - 1, NX))
    z_up, z_down = (s, mod(z + 1, n_z) * NX + x), (s, mod(z - 1, n_z) * NX + x)
    z_ups = (z_up, (s, mod(z + 2, n_z) * NX + x))
    z_downs = (z_down, (s, mod(z - 2, n_z) * NX + x))
    slot_z = {d: i for i, d in enumerate(around(n_z))}
    slot_x = {d: i for i, d in enumerate(around(NX))}

    def local(src, dst, i):
        made = pltpu.make_async_copy(src, dst, local_sem.at[i])
        made.start()
        return made

    for half in range(2):
        tokpad[half] = jnp.zeros_like(tokpad[half])
        tokpad[half, :, 0:share] = tokens[half * HALF_TOK:(half + 1) * HALF_TOK, :]

    width = queries.shape[1]
    for half in range(2):
        qpad[half] = jnp.zeros_like(qpad[half])
        qpad[half, :, 0:width] = queries[half * q_rows:(half + 1) * q_rows, :]

    barrier = pltpu.get_barrier_semaphore()

    def greet(j, carry):
        pl.semaphore_signal(
            barrier, inc=1, device_id=(lax.rem(s + j, n_seq), e), device_id_type=MESH
        )
        return carry

    lax.fori_loop(1, n_seq, greet, 0)
    for who in (x_up, x_down) + z_ups + z_downs:
        pl.semaphore_signal(barrier, inc=1, device_id=who, device_id_type=MESH)

    loads = [
        local(latent.at[pl.ds(c * half_req, half_req)], lbuf.at[0], 0),
        local(wg, wcat.at[0], 1),
        local(wu, wcat.at[2], 2),
        local(wd, wdcat.at[pl.ds(0, LANE)], 3),
    ]

    row = lax.broadcasted_iota(jnp.int32, (LANE, routes.shape[1]), 0)
    named = jnp.where(row < experts, row, row - experts)
    weight = jnp.zeros(named.shape, F32)
    for k in range(routes.shape[0]):
        weight = weight + jnp.where(named == routes[k:k + 1, :], gates[k:k + 1, :], 0.0)
    high = weight.astype(BF16).astype(F32)
    weight = jnp.where(row < experts, high, jnp.where(row < 2 * experts, weight - high, 0.0))
    square[...] = jnp.zeros_like(square)
    square[:, 0:routes.shape[1]] = weight
    square[...] = jnp.transpose(square[...])

    pl.semaphore_wait(barrier, n_seq - 1 + 6)

    def token_copy(j):
        to = lax.rem(s + j, n_seq)
        return pltpu.make_async_remote_copy(
            src_ref=tokpad.at[lax.rem(to, 2)],
            dst_ref=tokbuf.at[s],
            send_sem=t_send.at[j],
            recv_sem=t_recv.at[j],
            device_id=(to, e),
            device_id_type=MESH,
        )

    def query_copy(j):
        to = lax.rem(s + j, n_seq)
        return pltpu.make_async_remote_copy(
            src_ref=qpad.at[lax.rem(to, 2)],
            dst_ref=qbuf.at[s],
            send_sem=q_send.at[j],
            recv_sem=q_recv.at[j],
            device_id=(to, e),
            device_id_type=MESH,
        )

    def end_copy(j):
        to = lax.rem(s + j, n_seq)
        return pltpu.make_async_remote_copy(
            src_ref=ebuf.at[to],
            dst_ref=erecv.at[s],
            send_sem=e_send.at[j],
            recv_sem=e_recv.at[j],
            device_id=(to, e),
            device_id_type=MESH,
        )

    def each(act):
        def body(j, carry):
            act(j)
            return carry

        lax.fori_loop(1, n_seq, body, 0)

    net = Net(send_sem, recv_sem)
    each(lambda j: token_copy(j).start())
    lat_copy, _ = net.copy(latent.at[pl.ds(other * half_req, half_req)], lbuf.at[1], sibling, "core")
    for load in loads[1:]:
        load.wait()
    weights = []
    count_w = 7
    tall, flat = wcat.shape[1] // count_w, LANE // 8
    for k in range(8):
        if k < count_w:
            some = pl.ds(k * tall, tall)
            weights.append(net.copy(wcat.at[0, some], wcat.at[1, some], sibling, "core")[0])
            weights.append(net.copy(wcat.at[2, some], wcat.at[3, some], sibling, "core")[0])
        weights.append(net.copy(
            wdcat.at[pl.ds(k * flat, flat)], wdcat.at[pl.ds(LANE + k * flat, flat)], sibling, "core"
        )[0])
    each(lambda j: query_copy(j).start())

    tokbuf[s] = tokpad[c]
    qbuf[s] = qpad[c]
    line[...] = jnp.zeros_like(line)
    first_row = pl.multiple_of(c * HALF_TOK, HALF_TOK)
    xb[0, 0, :, wide_b:wide_b + LANE] = square[pl.ds(first_row, HALF_TOK), :].astype(BF16)
    each(lambda j: token_copy(j).wait_recv())
    for i in range(n_seq):
        begin, turn = share * i // LANE * LANE, share * i % LANE
        span = tokpad.shape[2] + LANE
        value = jnp.concatenate(
            [tokbuf[i].astype(F32), jnp.zeros((HALF_TOK, LANE), F32)], axis=1
        )
        if turn:
            value = pltpu.roll(value, turn, 1)
        line[:, begin:begin + span] = line[:, begin:begin + span] + value
    xa[0, 0] = line[:, 0:wide_a].astype(BF16)
    xb[0, 0, :, 0:wide_b] = line[:, wide_a:wide_a + wide_b].astype(BF16)

    position = lax.broadcasted_iota(jnp.int32, (n_seq * heads, LANE), 1)

    def one_request(i, carry):
        head_rows = pl.ds(pl.multiple_of(i * heads, heads), heads)
        q = qf[:, head_rows, :].reshape(n_seq * heads, qf.shape[2]).astype(BF16)
        length = lengths[0, c * half_req + i]
        parts = []
        for side, base in ((0, s), (1, 2 * y + other)):
            score = jnp.dot(q, lbuf[side, i], preferred_element_type=F32) * SCALE
            valid = position + base * LANE < length
            parts.append((jnp.where(valid, score, NEG), valid))
        top = jnp.maximum(
            jnp.max(parts[0][0], axis=1, keepdims=True),
            jnp.max(parts[1][0], axis=1, keepdims=True),
        ).astype(BF16).astype(F32)
        total = jnp.zeros((n_seq * heads, 1), F32)
        context = jnp.zeros((n_seq * heads, LAT), F32)
        for side in range(2):
            score, valid = parts[side]
            w = jnp.where(valid, jnp.exp(score - top), 0.0)
            total = total + jnp.sum(w, axis=1, keepdims=True)
            context = context + lax.dot_general(
                w.astype(BF16), lbuf[side, i, 0:LAT, :], (((1,), (1,)), ((), ())),
                preferred_element_type=F32,
            )
        total_high = total.astype(BF16).astype(F32)
        note = jnp.where(
            position == 0,
            top,
            jnp.where(position == 1, total_high, jnp.where(position == 2, total - total_high, 0.0)),
        )
        at = pl.ds(pl.multiple_of(2 * heads * i, 2 * heads), 2 * heads)
        obuf[:, at, 0:LAT] = context.astype(BF16).reshape(n_y, 2 * heads, LAT)
        obuf[:, at, LAT:LAT + LANE] = note.astype(BF16).reshape(n_y, 2 * heads, LANE)
        return carry

    def one_context(i, carry):
        at = pl.ds(pl.multiple_of(2 * heads * i, 2 * heads), 2 * heads)
        head_rows = pl.ds(pl.multiple_of(i * heads, heads), heads)
        line_of = lax.broadcasted_iota(jnp.int32, fresh.shape, 0)
        chosen = jnp.where(line_of == c * half_req + i, fresh[...].astype(F32), 0.0)
        key = jnp.sum(chosen, axis=0, keepdims=True)
        q = qf[pl.ds(2 * y, 2), head_rows, :].reshape(2 * heads, qf.shape[2])
        own = jnp.sum(q * key, axis=1, keepdims=True) * SCALE
        notes = [orecv[j, at, LAT:LAT + LANE].astype(F32) for j in range(n_y)]
        top = own
        for note in notes:
            top = jnp.maximum(top, note[:, 0:1])
        w = jnp.exp(own - top)
        total, context = w, w * key[:, 0:LAT]
        for j, note in enumerate(notes):
            w = jnp.exp(note[:, 0:1] - top)
            total = total + w * (note[:, 1:2] + note[:, 2:3])
            context = context + w * orecv[j, at, 0:LAT].astype(F32)
        context = context / total
        for core in range(2):
            cf[core, head_rows, :] = context[core * heads:(core + 1) * heads]
        return carry

    def attend():
        yield net.now + 8.0
        loads[0].wait()
        each(lambda j: query_copy(j).wait_recv())
        lat_copy.wait_recv()
        qf[...] = qbuf[:, :, 0:width].astype(F32)
        lax.fori_loop(0, half_req // 2, one_request, 0)
        net.now += 2.0
        yield net.now + 0.5
        lax.fori_loop(half_req // 2, half_req, one_request, 0)
        net.now += 2.0
        came = []
        for j in range(1, n_y):
            to = lax.rem(y + j, n_y)
            came.append(net.copy(obuf.at[to], orecv.at[y], (2 * to + c, e), "y"))
        orecv[y] = obuf[y]
        yield net.now + 25.0
        for one, _ in came:
            one.wait_recv()
        lax.fori_loop(0, half_req, one_context, 0)
        net.now += 1.0
        cb[...] = cf[...].astype(BF16)
        back, when = net.copy(cb.at[other], crecv, sibling, "core")
        ctx_out[pl.ds(pl.multiple_of(c * q_rows, q_rows), q_rows), :] = cb[c]
        yield when + 5.0
        back.wait_recv()
        ctx_out[pl.ds(pl.multiple_of(other * q_rows, q_rows), q_rows), :] = crecv[...]

    half_a, half_b = wide_a // 2, wide_b // 2

    def cut_a(ref, side):
        lead = (slice(None),) * (len(ref.shape) - 1)
        return ref.at[lead + (pl.ds(side * half_a, half_a),)]

    def cut_b(ref, side):
        lead = (slice(None),) * (len(ref.shape) - 1)
        size = half_b if side == 0 else ref.shape[-1] - half_b
        return ref.at[lead + (pl.ds(side * half_b, size),)]

    teams = [(0,)] + [(d, -d) for d in range(1, n_z // 2)] + [(n_z // 2,)]

    pairs = [(i, i + 1) for i in range(0, NX, 2)]

    def slots(team):
        return pl.ds(slot_z[team[0]], len(team))

    def gather_z(piece, cut, done):
        if n_z == 8:
            return skip_gather(net, piece, cut, z_ups, z_downs, "z", done)
        return ring_gather(net, piece, cut, n_z, z_up, z_down, "z", done)

    def scatter_z(piece, cut, arrived, ready, finish):
        if n_z == 8:
            return skip_scatter(net, piece, cut, arrived, z_ups, z_downs, "z", ready, finish)
        return ring_scatter(net, piece, cut, arrived, n_z, z_up, z_down, "z", ready, finish)

    landed = {d: 0 for d in slot_z}

    def count(team):
        for d in team:
            landed[d] += 1

    def gather_a():
        here = set()

        def start(dx):
            here.add(slot_x[dx])
            for pair in pairs:
                if slot_x[dx] in pair and here.issuperset(pair):
                    net.add(net.now, along_z(pl.ds(pair[0], 2)))

        def along_z(at):
            return gather_z(lambda d: xa.at[slot_z[d], at], cut_a, lambda d: count((d,)))

        yield from ring_gather(
            net, lambda d: xa.at[0, slot_x[d]], cut_a, NX, x_up, x_down, "x", start
        )

    def gather_b():
        here = set()

        def start(dz):
            here.add(dz)
            team = [team for team in teams if dz in team][0]
            if here.issuperset(team):
                net.add(net.now, ring_gather(
                    net, lambda d: xb.at[slots(team), slot_x[d]], cut_b, NX, x_up, x_down, "x",
                    lambda d: count(team),
                ))

        yield from gather_z(lambda d: xb.at[slot_z[d], 0], cut_b, start)

    step_a, step_b = wide_a // 2, wide_b // 5
    def experts_of(first, last):
        rows = (last - first) * NX * HALF_TOK

        def beside(some):
            return jnp.concatenate([wcat[i, some, :] for i in range(4)], axis=1)

        def up_a(k, carry):
            cols = pl.ds(pl.multiple_of(k * step_a, step_a), step_a)
            value = xa[first:last, :, :, cols].reshape(rows, step_a)
            acc[0:rows, :] += jnp.dot(value, beside(cols), preferred_element_type=F32)
            return carry

        def up_b(k, carry):
            cols = pl.ds(pl.multiple_of(k * step_b, step_b), step_b)
            down = pl.ds(pl.multiple_of(wide_a + k * step_b, LANE), step_b)
            value = xb[first:last, :, :, cols].reshape(rows, step_b)
            acc[0:rows, :] += jnp.dot(value, beside(down), preferred_element_type=F32)
            return carry

        def down_a(k, carry):
            cols = pl.ds(pl.multiple_of(k * step_a, step_a), step_a)
            value = jnp.dot(hid[0:rows, :], wdcat[:, cols], preferred_element_type=F32)
            ya[first:last, :, :, cols] = value.astype(BF16).reshape(last - first, NX, HALF_TOK, step_a)
            return carry

        def down_b(k, carry):
            cols = pl.ds(pl.multiple_of(k * step_b, step_b), step_b)
            down = pl.ds(pl.multiple_of(wide_a + k * step_b, LANE), step_b)
            value = jnp.dot(hid[0:rows, :], wdcat[:, down], preferred_element_type=F32)
            yb[first:last, :, :, cols] = value.astype(BF16).reshape(last - first, NX, HALF_TOK, step_b)
            return carry

        acc[0:rows, :] = jnp.zeros((rows, 4 * LANE), F32)
        lax.fori_loop(0, 2, up_a, 0)
        lax.fori_loop(0, 5, up_b, 0)
        tile = xb[first:last, :, :, wide_b:wide_b + LANE].reshape(rows, LANE).astype(F32)
        lane = lax.broadcasted_iota(jnp.int32, (rows, LANE), 1)
        gate = jnp.sum(
            jnp.where((lane == e) | (lane == e + experts), tile, 0.0), axis=1, keepdims=True
        )
        g = acc[0:rows, 0:2 * LANE]
        value = g / (1.0 + jnp.exp(-g)) * acc[0:rows, 2 * LANE:4 * LANE] * gate
        hid[0:rows, :] = value.astype(BF16)
        lax.fori_loop(0, 5, down_b, 0)
        lax.fori_loop(0, 2, down_a, 0)

    def compute():
        offsets = around(n_z)
        groups = [(0, 5), (5, 8)] if n_z == 8 else [(0, len(offsets))]
        for first, last in groups:
            while any(landed[d] < len(pairs) + NX for d in offsets[first:last]):
                yield net.now + 0.01
            if first == 0:
                for made in weights:
                    made.wait_recv()
            experts_of(first, last)
            net.now += 1.0

    attention = attend()
    net.run([gather_a(), gather_b(), sample(attention, 3), compute()])

    net.links, net.now = {}, 0.0
    ended = set()

    def always(d):
        return True

    def row_sum(team):
        at = slots(team)

        def finish(total):
            yb[at, 0] = total.astype(BF16)
            ended.update(team)

        return ring_scatter(
            net, lambda d: yb.at[at, slot_x[d]], cut_b, lambda way, k: rbx.at[way, k, at],
            NX, x_up, x_down, "x", always, finish,
        )

    done_a = set()

    def column_sum(pair):
        at = pl.ds(pair[0], 2)

        def finish(total):
            ya[0, at] = total.astype(BF16)
            done_a.update(pair)

        return scatter_z(
            lambda d: ya.at[slot_z[d], at], cut_a, lambda way, k: ra.at[way, k, at], always, finish
        )

    def end_a(total):
        line[:, 0:wide_a] = total

    def end_b(total):
        line[:, wide_a:wide_a + wide_b] = total

    sum_a = ring_scatter(
        net, lambda d: ya.at[0, slot_x[d]], cut_a, lambda way, k: rax.at[way, k],
        NX, x_up, x_down, "x", lambda d: slot_x[far_x if d == -far_x else d] in done_a, end_a,
    )

    sum_b = scatter_z(
        lambda d: yb.at[slot_z[d], 0], cut_b, lambda way, k: rb.at[way, k],
        lambda d: d in ended, end_b,
    )
    before = list(net.copies)

    def settle():
        yield net.now + 1.0
        each(lambda j: token_copy(j).wait_send())
        each(lambda j: query_copy(j).wait_send())
        for made in before:
            made.wait_send()

    first_rows = [row_sum(team) for team in reversed(teams)]
    columns = [column_sum(pair) for pair in reversed(pairs)]
    net.run(first_rows[:1] + columns + first_rows[1:] + [sum_a, sum_b, sample(attention, 9), settle()])

    for i in range(n_seq):
        begin, turn = share * i // LANE * LANE, share * i % LANE
        span = tokpad.shape[2] + LANE
        value = line[:, begin:begin + span]
        if turn:
            value = pltpu.roll(value, span - turn, 1)
        ebuf[i] = value[:, 0:tokpad.shape[2]].astype(BF16)
    each(lambda j: end_copy(j).start())
    erecv[s] = ebuf[s]
    each(lambda j: end_copy(j).wait_recv())
    for half in range(2):
        total = erecv[half].astype(F32)
        for i in range(1, n_y):
            total = total + erecv[2 * i + half].astype(F32)
        mix_out[half * HALF_TOK:(half + 1) * HALF_TOK, :] = total[:, 0:share].astype(BF16)

    each(lambda j: end_copy(j).wait_send())
    for made in net.copies[len(before):]:
        made.wait_send()


def sample(task, most):
    for _ in range(most):
        try:
            ready = next(task)
        except StopIteration:
            return
        yield ready


def on_device(latent, lengths, queries, fresh_latent, tokens, routes, gates, w_gate, w_up, w_down):
    n_seq, n_ep = lax.axis_size("seq"), lax.axis_size("ep")
    n_z, n_y = n_ep // NX, n_seq // 2
    n_req, heads, width = queries.shape
    share = tokens.shape[1]
    features = share * n_seq
    wide_a = features // 7 * 2
    wide_b = features - wide_a
    padded = -(-share // LANE) * LANE
    wide_q = -(-width // LANE) * LANE
    rows = n_ep * HALF_TOK
    half_req = n_req // 2
    q_rows = half_req * heads
    far_z, far_x = n_z // 2, NX // 2
    cfg = (n_seq, n_z, wide_a, wide_b, share, heads)
    vmem = pl.BlockSpec(memory_space=pltpu.VMEM)
    hbm = pl.BlockSpec(memory_space=pl.ANY)
    dma = pltpu.SemaphoreType.DMA
    ffn = 2 * rows * features * 6 * LANE
    context, mixed = pl.pallas_call(
        functools.partial(kernel, cfg),
        out_shape=(
            jax.ShapeDtypeStruct((n_req * heads, LAT), BF16),
            jax.ShapeDtypeStruct(tokens.shape, BF16),
        ),
        in_specs=[hbm, vmem, hbm, hbm, hbm, pl.BlockSpec(memory_space=pltpu.SMEM), vmem, vmem, vmem, vmem],
        out_specs=(vmem, vmem),
        scratch_shapes=[
            pltpu.VMEM((2, HALF_TOK, padded), BF16),
            pltpu.VMEM((n_seq, HALF_TOK, padded), BF16),
            pltpu.VMEM((HALF_TOK, features + 2 * LANE), F32),
            pltpu.VMEM((LANE, LANE), F32),
            pltpu.VMEM((n_z, NX, HALF_TOK, wide_a), BF16),
            pltpu.VMEM((n_z, NX, HALF_TOK, wide_b + LANE), BF16),
            pltpu.VMEM((4, features, LANE), BF16),
            pltpu.VMEM((2 * LANE, features), BF16),
            pltpu.VMEM((rows, 4 * LANE), F32),
            pltpu.VMEM((rows, 2 * LANE), BF16),
            pltpu.VMEM((n_z, NX, HALF_TOK, wide_a), BF16),
            pltpu.VMEM((n_z, NX, HALF_TOK, wide_b), BF16),
            pltpu.VMEM((2, far_z, NX, HALF_TOK, wide_a), BF16),
            pltpu.VMEM((2, far_x, HALF_TOK, wide_a), BF16),
            pltpu.VMEM((2, far_x, n_z, HALF_TOK, wide_b), BF16),
            pltpu.VMEM((2, far_z, HALF_TOK, wide_b), BF16),
            pltpu.VMEM((n_seq, HALF_TOK, padded), BF16),
            pltpu.VMEM((n_seq, HALF_TOK, padded), BF16),
            pltpu.VMEM((2, half_req, width, LANE), BF16),
            pltpu.VMEM((2, q_rows, wide_q), BF16),
            pltpu.VMEM((n_seq, q_rows, wide_q), BF16),
            pltpu.VMEM((n_seq, q_rows, width), F32),
            pltpu.VMEM((n_y, 2 * q_rows, LAT + LANE), BF16),
            pltpu.VMEM((n_y, 2 * q_rows, LAT + LANE), BF16),
            pltpu.VMEM((2, q_rows, LAT), F32),
            pltpu.VMEM((2, q_rows, LAT), BF16),
            pltpu.VMEM((q_rows, LAT), BF16),
            dma((4,)),
            dma((160,)),
            dma((160,)),
            dma((n_seq,)),
            dma((n_seq,)),
            dma((n_seq,)),
            dma((n_seq,)),
            dma((n_seq,)),
            dma((n_seq,)),
        ],
        compiler_params=pltpu.CompilerParams(
            collective_id=0, has_side_effects=True, vmem_limit_bytes=56 * 1024 * 1024
        ),
        cost_estimate=pl.CostEstimate(flops=ffn, bytes_accessed=6 * 2**20, transcendentals=rows * 512),
    )(
        latent.transpose(0, 2, 1),
        queries.reshape(n_req * heads, width),
        w_gate[0],
        w_up[0],
        w_down[0],
        lengths,
        fresh_latent,
        tokens,
        routes.T,
        gates.T,
    )
    return context.reshape(n_req, heads, LAT), mixed


def solution(mesh):
    placed = (
        P("ep", "seq", None),
        P("ep", None),
        P("ep", "seq", None),
        P("ep", None),
        P("ep", "seq"),
        P("ep", None),
        P("ep", None),
        P("ep", None, "seq"),
        P("ep", None, "seq"),
        P("ep", "seq", None),
    )
    return jax.shard_map(
        on_device,
        mesh=mesh,
        in_specs=placed,
        out_specs=(P("ep", "seq", None), P("ep", "seq")),
        check_vma=False,
    )
```

```python
import functools
import heapq

import jax
import jax.numpy as jnp
from jax import lax
from jax.experimental import pallas as pl
from jax.experimental.pallas import tpu as pltpu
from jax.sharding import PartitionSpec as P

MESH = pl.DeviceIdType.MESH
LAT = 512
NX = 4
LANE = 128
HALF_TOK = 16
SCALE = 0.07216878364870322
NEG = -1.0e30
F32 = jnp.float32
BF16 = jnp.bfloat16

LINK_RATE = 45.0e3
HOP = 1.5


def mod(value, n):
    return lax.rem(value + n, n)


class Net:
    def __init__(self, send, recv):
        self.send, self.recv = send, recv
        self.count, self.now = 0, 0.0
        self.links, self.copies = {}, []

    def copy(self, src, dst, device, link):
        at = self.count
        self.count += 1
        made = pltpu.make_async_remote_copy(
            src_ref=src,
            dst_ref=dst,
            send_sem=self.send.at[at],
            recv_sem=self.recv.at[at],
            device_id=device,
            device_id_type=MESH,
        )
        made.start()
        size = 2
        for extent in src.shape:
            size *= extent
        begin = max(self.links.get(link, 0.0), self.now)
        self.links[link] = begin + size / LINK_RATE
        self.copies.append(made)
        return made, self.links[link] + HOP

    def run(self, tasks):
        self.heap, self.order = [], 0
        for task in tasks:
            self.add(self.now, task)
        while self.heap:
            at, _, task = heapq.heappop(self.heap)
            self.now = max(self.now, at)
            try:
                ready = next(task)
            except StopIteration:
                continue
            self.add(ready, task)

    def add(self, at, task):
        self.order += 1
        heapq.heappush(self.heap, (at, self.order, task))


def around(n):
    offsets = [0]
    for k in range(1, n // 2):
        offsets += [k, -k]
    return offsets + [n // 2]


def ring_gather(net, piece, cut, n, up, down, axis, landed):
    far = n // 2

    def pass_on(side, k):
        src, dst = piece((k, -k)[1 - side]), piece(far if k + 1 == far else (k + 1, -k - 1)[1 - side])
        if k + 1 == far:
            src, dst = cut(src, side), cut(dst, side)
        return net.copy(src, dst, (up, down)[side], axis + "+-"[side])

    cu, tu = pass_on(0, 0)
    cd, td = pass_on(1, 0)
    landed(0)
    for k in range(1, far):
        yield tu
        cu.wait_recv()
        cu, tu = pass_on(0, k)
        landed(-k)
        yield td
        cd.wait_recv()
        cd, td = pass_on(1, k)
        landed(k)
    yield max(tu, td)
    cu.wait_recv()
    cd.wait_recv()
    landed(far)


def add_into(ref, other):
    ref[...] = ref[...] + other[...]


def ring_scatter(net, piece, cut, arrived, n, up, down, axis, ready, finish):
    far = n // 2
    while not ready(far):
        yield net.now + 0.01
    cu, tu = net.copy(cut(piece(far), 0), cut(arrived(0, 0), 0), up, axis + "+")
    cd, td = net.copy(cut(piece(far), 1), cut(arrived(1, 0), 1), down, axis + "-")
    for k in range(1, far):
        d = far - k
        while not (ready(d) and ready(-d)):
            yield net.now + 0.01
        yield tu
        cu.wait_recv()
        mine, came = piece(d), arrived(0, k - 1)
        if k == 1:
            mine, came = cut(mine, 0), cut(came, 0)
        add_into(mine, came)
        cu, tu = net.copy(piece(d), arrived(0, k), up, axis + "+")
        yield td
        cd.wait_recv()
        mine, came = piece(-d), arrived(1, k - 1)
        if k == 1:
            mine, came = cut(mine, 1), cut(came, 1)
        add_into(mine, came)
        cd, td = net.copy(piece(-d), arrived(1, k), down, axis + "-")
    while not ready(0):
        yield net.now + 0.01
    yield max(tu, td)
    cu.wait_recv()
    cd.wait_recv()
    if far == 1:
        add_into(cut(piece(0), 0), cut(arrived(0, 0), 0))
        add_into(cut(piece(0), 1), cut(arrived(1, 0), 1))
        finish(piece(0)[...].astype(F32))
    else:
        finish(
            piece(0)[...].astype(F32)
            + arrived(0, far - 1)[...].astype(F32)
            + arrived(1, far - 1)[...].astype(F32)
        )


def kernel(
    cfg,
    latent, queries, wg, wu, wd, lengths, fresh, tokens, routes, gates,
    ctx_out, mix_out,
    tokpad, tokbuf, line, square, xa, xb, wcat, wdcat, acc, hid, ya, yb,
    ra, rax, rbx, rb, ebuf, erecv,
    lbuf, qbuf, qf, obuf, orecv, cf, cb, crecv,
    local_sem, send_sem, recv_sem, t_send, t_recv, q_send, q_recv, e_send, e_recv,
):
    n_seq, n_z, wide_a, wide_b, share, heads = cfg
    n_y = n_seq // 2
    s, e = lax.axis_index("seq"), lax.axis_index("ep")
    y, c = s // 2, lax.rem(s, 2)
    z, x = e // NX, lax.rem(e, NX)
    other = 1 - c
    sibling = (2 * y + other, e)
    experts = n_z * NX
    n_req = lengths.shape[1]
    half_req = n_req // 2
    q_rows = half_req * heads
    x_up, x_down = (s, z * NX + mod(x + 1, NX)), (s, z * NX + mod(x - 1, NX))
    z_up, z_down = (s, mod(z + 1, n_z) * NX + x), (s, mod(z - 1, n_z) * NX + x)
    slot_z = {d: i for i, d in enumerate(around(n_z))}
    slot_x = {d: i for i, d in enumerate(around(NX))}

    def local(src, dst, i):
        made = pltpu.make_async_copy(src, dst, local_sem.at[i])
        made.start()
        return made

    barrier = pltpu.get_barrier_semaphore()

    def greet(j, carry):
        pl.semaphore_signal(
            barrier, inc=1, device_id=(lax.rem(s + j, n_seq), e), device_id_type=MESH
        )
        return carry

    lax.fori_loop(1, n_seq, greet, 0)
    for who in (x_up, x_down, z_up, z_down):
        pl.semaphore_signal(barrier, inc=1, device_id=who, device_id_type=MESH)

    for half in range(2):
        tokpad[half] = jnp.zeros_like(tokpad[half])
        tokpad[half, :, 0:share] = tokens[half * HALF_TOK:(half + 1) * HALF_TOK, :]

    mine_q = queries.at[pl.ds(pl.multiple_of(c * q_rows, q_rows), q_rows)]
    loads = [
        local(mine_q, qbuf.at[s], 0),
        local(latent.at[pl.ds(c * half_req, half_req)], lbuf.at[0], 1),
        local(wg, wcat.at[:, pl.ds(0, LANE)], 2),
        local(wu, wcat.at[:, pl.ds(2 * LANE, LANE)], 3),
        local(wd, wdcat.at[pl.ds(0, LANE)], 4),
    ]

    row = lax.broadcasted_iota(jnp.int32, (LANE, routes.shape[1]), 0)
    named = jnp.where(row < experts, row, row - experts)
    weight = jnp.zeros(named.shape, F32)
    for k in range(routes.shape[0]):
        weight = weight + jnp.where(named == routes[k:k + 1, :], gates[k:k + 1, :], 0.0)
    high = weight.astype(BF16).astype(F32)
    weight = jnp.where(row < experts, high, jnp.where(row < 2 * experts, weight - high, 0.0))
    square[...] = jnp.zeros_like(square)
    square[:, 0:routes.shape[1]] = weight
    square[...] = jnp.transpose(square[...])

    pl.semaphore_wait(barrier, n_seq - 1 + 4)

    def token_copy(j):
        to = lax.rem(s + j, n_seq)
        return pltpu.make_async_remote_copy(
            src_ref=tokpad.at[lax.rem(to, 2)],
            dst_ref=tokbuf.at[s],
            send_sem=t_send.at[j],
            recv_sem=t_recv.at[j],
            device_id=(to, e),
            device_id_type=MESH,
        )

    def query_copy(j):
        to = lax.rem(s + j, n_seq)
        begin = pl.multiple_of(lax.rem(to, 2) * q_rows, q_rows)
        return pltpu.make_async_remote_copy(
            src_ref=queries.at[pl.ds(begin, q_rows)],
            dst_ref=qbuf.at[s],
            send_sem=q_send.at[j],
            recv_sem=q_recv.at[j],
            device_id=(to, e),
            device_id_type=MESH,
        )

    def end_copy(j):
        to = lax.rem(s + j, n_seq)
        return pltpu.make_async_remote_copy(
            src_ref=ebuf.at[to],
            dst_ref=erecv.at[s],
            send_sem=e_send.at[j],
            recv_sem=e_recv.at[j],
            device_id=(to, e),
            device_id_type=MESH,
        )

    def each(act):
        def body(j, carry):
            act(j)
            return carry

        lax.fori_loop(1, n_seq, body, 0)

    net = Net(send_sem, recv_sem)
    each(lambda j: token_copy(j).start())
    each(lambda j: query_copy(j).start())
    lat_copy, _ = net.copy(latent.at[pl.ds(other * half_req, half_req)], lbuf.at[1], sibling, "core")

    tokbuf[s] = tokpad[c]
    line[...] = jnp.zeros_like(line)
    first_row = pl.multiple_of(c * HALF_TOK, HALF_TOK)
    xb[0, 0, :, wide_b:wide_b + LANE] = square[pl.ds(first_row, HALF_TOK), :].astype(BF16)
    each(lambda j: token_copy(j).wait_recv())
    for i in range(n_seq):
        begin, turn = share * i // LANE * LANE, share * i % LANE
        span = tokpad.shape[2] + LANE
        value = jnp.concatenate(
            [tokbuf[i].astype(F32), jnp.zeros((HALF_TOK, LANE), F32)], axis=1
        )
        if turn:
            value = pltpu.roll(value, turn, 1)
        line[:, begin:begin + span] = line[:, begin:begin + span] + value
    xa[0, 0] = line[:, 0:wide_a].astype(BF16)
    xb[0, 0, :, 0:wide_b] = line[:, wide_a:wide_a + wide_b].astype(BF16)

    position = lax.broadcasted_iota(jnp.int32, (n_seq * heads, LANE), 1)

    def one_request(i, carry):
        head_rows = pl.ds(pl.multiple_of(i * heads, heads), heads)
        q = qf[:, head_rows, :].reshape(n_seq * heads, qf.shape[2]).astype(BF16)
        length = lengths[0, c * half_req + i]
        parts = []
        for side, base in ((0, s), (1, 2 * y + other)):
            score = jnp.dot(q, lbuf[side, i], preferred_element_type=F32) * SCALE
            valid = position + base * LANE < length
            parts.append((jnp.where(valid, score, NEG), valid))
        top = jnp.maximum(
            jnp.max(parts[0][0], axis=1, keepdims=True),
            jnp.max(parts[1][0], axis=1, keepdims=True),
        ).astype(BF16).astype(F32)
        total = jnp.zeros((n_seq * heads, 1), F32)
        context = jnp.zeros((n_seq * heads, LAT), F32)
        for side in range(2):
            score, valid = parts[side]
            w = jnp.where(valid, jnp.exp(score - top), 0.0)
            total = total + jnp.sum(w, axis=1, keepdims=True)
            context = context + lax.dot_general(
                w.astype(BF16), lbuf[side, i, 0:LAT, :], (((1,), (1,)), ((), ())),
                preferred_element_type=F32,
            )
        total_high = total.astype(BF16).astype(F32)
        note = jnp.where(
            position == 0,
            top,
            jnp.where(position == 1, total_high, jnp.where(position == 2, total - total_high, 0.0)),
        )
        at = pl.ds(pl.multiple_of(2 * heads * i, 2 * heads), 2 * heads)
        obuf[:, at, 0:LAT] = context.astype(BF16).reshape(n_y, 2 * heads, LAT)
        obuf[:, at, LAT:LAT + LANE] = note.astype(BF16).reshape(n_y, 2 * heads, LANE)
        return carry

    def one_context(i, carry):
        at = pl.ds(pl.multiple_of(2 * heads * i, 2 * heads), 2 * heads)
        head_rows = pl.ds(pl.multiple_of(i * heads, heads), heads)
        line_of = lax.broadcasted_iota(jnp.int32, fresh.shape, 0)
        chosen = jnp.where(line_of == c * half_req + i, fresh[...].astype(F32), 0.0)
        key = jnp.sum(chosen, axis=0, keepdims=True)
        q = qf[pl.ds(2 * y, 2), head_rows, :].reshape(2 * heads, qf.shape[2])
        own = jnp.sum(q * key, axis=1, keepdims=True) * SCALE
        notes = [orecv[j, at, LAT:LAT + LANE].astype(F32) for j in range(n_y)]
        top = own
        for note in notes:
            top = jnp.maximum(top, note[:, 0:1])
        w = jnp.exp(own - top)
        total, context = w, w * key[:, 0:LAT]
        for j, note in enumerate(notes):
            w = jnp.exp(note[:, 0:1] - top)
            total = total + w * (note[:, 1:2] + note[:, 2:3])
            context = context + w * orecv[j, at, 0:LAT].astype(F32)
        context = context / total
        for core in range(2):
            cf[core, head_rows, :] = context[core * heads:(core + 1) * heads]
        return carry

    def attend():
        yield net.now + 8.0
        loads[0].wait()
        loads[1].wait()
        each(lambda j: query_copy(j).wait_recv())
        lat_copy.wait_recv()
        qf[...] = qbuf[...].astype(F32)
        lax.fori_loop(0, half_req // 2, one_request, 0)
        net.now += 2.0
        yield net.now + 0.5
        lax.fori_loop(half_req // 2, half_req, one_request, 0)
        net.now += 2.0
        came = []
        for j in range(1, n_y):
            to = lax.rem(y + j, n_y)
            came.append(net.copy(obuf.at[to], orecv.at[y], (2 * to + c, e), "y"))
        orecv[y] = obuf[y]
        yield net.now + 25.0
        for one, _ in came:
            one.wait_recv()
        lax.fori_loop(0, half_req, one_context, 0)
        net.now += 1.0
        cb[...] = cf[...].astype(BF16)
        back, when = net.copy(cb.at[other], crecv, sibling, "core")
        ctx_out[pl.ds(pl.multiple_of(c * q_rows, q_rows), q_rows), :] = cb[c]
        yield when + 5.0
        back.wait_recv()
        ctx_out[pl.ds(pl.multiple_of(other * q_rows, q_rows), q_rows), :] = crecv[...]

    half_a, half_b = wide_a // 2, wide_b // 2

    def cut_a(ref, side):
        lead = (slice(None),) * (len(ref.shape) - 1)
        return ref.at[lead + (pl.ds(side * half_a, half_a),)]

    def cut_b(ref, side):
        lead = (slice(None),) * (len(ref.shape) - 1)
        size = half_b if side == 0 else ref.shape[-1] - half_b
        return ref.at[lead + (pl.ds(side * half_b, size),)]

    teams = [(0,)] + [(d, -d) for d in range(1, n_z // 2)] + [(n_z // 2,)]

    def slots(team):
        return pl.ds(slot_z[team[0]], len(team))

    landed = {d: 0 for d in slot_z}

    def count(team):
        for d in team:
            landed[d] += 1

    def gather_a():
        yield from ring_gather(
            net, lambda d: xa.at[0, slot_x[d]], cut_a, NX, x_up, x_down, "x", lambda d: None
        )
        yield from ring_gather(
            net, lambda d: xa.at[slot_z[d]], cut_a, n_z, z_up, z_down, "z", lambda d: count((d,))
        )

    def gather_b():
        here = set()

        def start(dz):
            here.add(dz)
            team = [team for team in teams if dz in team][0]
            if here.issuperset(team):
                net.add(net.now, ring_gather(
                    net, lambda d: xb.at[slots(team), slot_x[d]], cut_b, NX, x_up, x_down, "x",
                    lambda d: count(team),
                ))

        yield from ring_gather(
            net, lambda d: xb.at[slot_z[d], 0], cut_b, n_z, z_up, z_down, "z", start
        )

    step_a, step_b = wide_a // 3, wide_b // 4
    weights = []

    def load_weights():
        yield net.now + 0.5
        for src, dst in (
            (wg, wcat.at[:, pl.ds(LANE, LANE)]),
            (wu, wcat.at[:, pl.ds(3 * LANE, LANE)]),
            (wd, wdcat.at[pl.ds(LANE, LANE)]),
        ):
            weights.append(net.copy(src, dst, sibling, "core")[0])

    def experts_of(first, last):
        rows = (last - first) * NX * HALF_TOK

        def up_a(k, carry):
            cols = pl.ds(pl.multiple_of(k * step_a, step_a), step_a)
            value = xa[first:last, :, :, cols].reshape(rows, step_a)
            acc[0:rows, :] += jnp.dot(value, wcat[cols, :], preferred_element_type=F32)
            return carry

        def up_b(k, carry):
            cols = pl.ds(pl.multiple_of(k * step_b, step_b), step_b)
            down = pl.ds(pl.multiple_of(wide_a + k * step_b, step_b), step_b)
            value = xb[first:last, :, :, cols].reshape(rows, step_b)
            acc[0:rows, :] += jnp.dot(value, wcat[down, :], preferred_element_type=F32)
            return carry

        def down_a(k, carry):
            cols = pl.ds(pl.multiple_of(k * step_a, step_a), step_a)
            value = jnp.dot(hid[0:rows, :], wdcat[:, cols], preferred_element_type=F32)
            ya[first:last, :, :, cols] = value.astype(BF16).reshape(last - first, NX, HALF_TOK, step_a)
            return carry

        def down_b(k, carry):
            cols = pl.ds(pl.multiple_of(k * step_b, step_b), step_b)
            down = pl.ds(pl.multiple_of(wide_a + k * step_b, step_b), step_b)
            value = jnp.dot(hid[0:rows, :], wdcat[:, down], preferred_element_type=F32)
            yb[first:last, :, :, cols] = value.astype(BF16).reshape(last - first, NX, HALF_TOK, step_b)
            return carry

        acc[0:rows, :] = jnp.zeros((rows, 4 * LANE), F32)
        lax.fori_loop(0, 3, up_a, 0)
        lax.fori_loop(0, 4, up_b, 0)
        tile = xb[first:last, :, :, wide_b:wide_b + LANE].reshape(rows, LANE).astype(F32)
        lane = lax.broadcasted_iota(jnp.int32, (rows, LANE), 1)
        gate = jnp.sum(
            jnp.where((lane == e) | (lane == e + experts), tile, 0.0), axis=1, keepdims=True
        )
        g = acc[0:rows, 0:2 * LANE]
        value = g / (1.0 + jnp.exp(-g)) * acc[0:rows, 2 * LANE:4 * LANE] * gate
        hid[0:rows, :] = value.astype(BF16)
        lax.fori_loop(0, 4, down_b, 0)
        lax.fori_loop(0, 3, down_a, 0)

    def compute():
        offsets = around(n_z)
        groups = [(0, 5), (5, 8)] if n_z == 8 else [(0, len(offsets))]
        for first, last in groups:
            while any(landed[d] < 1 + NX for d in offsets[first:last]):
                yield net.now + 0.01
            if first == 0:
                for load in loads[2:]:
                    load.wait()
                for made in weights:
                    made.wait_recv()
            experts_of(first, last)
            net.now += 1.0

    attention = attend()
    net.run([gather_a(), gather_b(), load_weights(), sample(attention, 3), compute()])

    net.links, net.now = {}, 0.0
    ended = set()

    def always(d):
        return True

    def row_sum(team):
        at = slots(team)

        def finish(total):
            yb[at, 0] = total.astype(BF16)
            ended.update(team)

        return ring_scatter(
            net, lambda d: yb.at[at, slot_x[d]], cut_b, lambda way, k: rbx.at[way, k, at],
            NX, x_up, x_down, "x", always, finish,
        )

    def keep_a(total):
        ya[0] = total.astype(BF16)

    def end_a(total):
        line[:, 0:wide_a] = total

    def end_b(total):
        line[:, wide_a:wide_a + wide_b] = total

    def sum_a():
        yield from ring_scatter(
            net, lambda d: ya.at[slot_z[d]], cut_a, lambda way, k: ra.at[way, k],
            n_z, z_up, z_down, "z", always, keep_a,
        )
        yield from ring_scatter(
            net, lambda d: ya.at[0, slot_x[d]], cut_a, lambda way, k: rax.at[way, k],
            NX, x_up, x_down, "x", always, end_a,
        )

    sum_b = ring_scatter(
        net, lambda d: yb.at[slot_z[d], 0], cut_b, lambda way, k: rb.at[way, k],
        n_z, z_up, z_down, "z", lambda d: d in ended, end_b,
    )
    before = list(net.copies)

    def settle():
        yield net.now + 1.0
        each(lambda j: token_copy(j).wait_send())
        each(lambda j: query_copy(j).wait_send())
        for made in before:
            made.wait_send()

    first_rows = [row_sum(team) for team in reversed(teams)]
    net.run(first_rows[:1] + [sum_a()] + first_rows[1:] + [sum_b, sample(attention, 9), settle()])

    for i in range(n_seq):
        begin, turn = share * i // LANE * LANE, share * i % LANE
        span = tokpad.shape[2] + LANE
        value = line[:, begin:begin + span]
        if turn:
            value = pltpu.roll(value, span - turn, 1)
        ebuf[i] = value[:, 0:tokpad.shape[2]].astype(BF16)
    each(lambda j: end_copy(j).start())
    erecv[s] = ebuf[s]
    each(lambda j: end_copy(j).wait_recv())
    for half in range(2):
        total = erecv[half].astype(F32)
        for i in range(1, n_y):
            total = total + erecv[2 * i + half].astype(F32)
        mix_out[half * HALF_TOK:(half + 1) * HALF_TOK, :] = total[:, 0:share].astype(BF16)

    each(lambda j: end_copy(j).wait_send())
    for made in net.copies[len(before):]:
        made.wait_send()


def sample(task, most):
    for _ in range(most):
        try:
            ready = next(task)
        except StopIteration:
            return
        yield ready


def on_device(latent, lengths, queries, fresh_latent, tokens, routes, gates, w_gate, w_up, w_down):
    n_seq, n_ep = lax.axis_size("seq"), lax.axis_size("ep")
    n_z, n_y = n_ep // NX, n_seq // 2
    n_req, heads, width = queries.shape
    share = tokens.shape[1]
    features = share * n_seq
    wide_a = features // 7 * 3
    wide_b = features - wide_a
    padded = -(-share // LANE) * LANE
    rows = n_ep * HALF_TOK
    half_req = n_req // 2
    q_rows = half_req * heads
    far_z, far_x = n_z // 2, NX // 2
    cfg = (n_seq, n_z, wide_a, wide_b, share, heads)
    vmem = pl.BlockSpec(memory_space=pltpu.VMEM)
    hbm = pl.BlockSpec(memory_space=pl.ANY)
    dma = pltpu.SemaphoreType.DMA
    ffn = 2 * rows * features * 6 * LANE
    context, mixed = pl.pallas_call(
        functools.partial(kernel, cfg),
        out_shape=(
            jax.ShapeDtypeStruct((n_req * heads, LAT), BF16),
            jax.ShapeDtypeStruct(tokens.shape, BF16),
        ),
        in_specs=[hbm, hbm, hbm, hbm, hbm, pl.BlockSpec(memory_space=pltpu.SMEM), vmem, vmem, vmem, vmem],
        out_specs=(vmem, vmem),
        scratch_shapes=[
            pltpu.VMEM((2, HALF_TOK, padded), BF16),
            pltpu.VMEM((n_seq, HALF_TOK, padded), BF16),
            pltpu.VMEM((HALF_TOK, features + 2 * LANE), F32),
            pltpu.VMEM((LANE, LANE), F32),
            pltpu.VMEM((n_z, NX, HALF_TOK, wide_a), BF16),
            pltpu.VMEM((n_z, NX, HALF_TOK, wide_b + LANE), BF16),
            pltpu.VMEM((features, 4 * LANE), BF16),
            pltpu.VMEM((2 * LANE, features), BF16),
            pltpu.VMEM((rows, 4 * LANE), F32),
            pltpu.VMEM((rows, 2 * LANE), BF16),
            pltpu.VMEM((n_z, NX, HALF_TOK, wide_a), BF16),
            pltpu.VMEM((n_z, NX, HALF_TOK, wide_b), BF16),
            pltpu.VMEM((2, far_z, NX, HALF_TOK, wide_a), BF16),
            pltpu.VMEM((2, far_x, HALF_TOK, wide_a), BF16),
            pltpu.VMEM((2, far_x, n_z, HALF_TOK, wide_b), BF16),
            pltpu.VMEM((2, far_z, HALF_TOK, wide_b), BF16),
            pltpu.VMEM((n_seq, HALF_TOK, padded), BF16),
            pltpu.VMEM((n_seq, HALF_TOK, padded), BF16),
            pltpu.VMEM((2, half_req, width, LANE), BF16),
            pltpu.VMEM((n_seq, q_rows, width), BF16),
            pltpu.VMEM((n_seq, q_rows, width), F32),
            pltpu.VMEM((n_y, 2 * q_rows, LAT + LANE), BF16),
            pltpu.VMEM((n_y, 2 * q_rows, LAT + LANE), BF16),
            pltpu.VMEM((2, q_rows, LAT), F32),
            pltpu.VMEM((2, q_rows, LAT), BF16),
            pltpu.VMEM((q_rows, LAT), BF16),
            dma((5,)),
            dma((120,)),
            dma((120,)),
            dma((n_seq,)),
            dma((n_seq,)),
            dma((n_seq,)),
            dma((n_seq,)),
            dma((n_seq,)),
            dma((n_seq,)),
        ],
        compiler_params=pltpu.CompilerParams(
            collective_id=0, has_side_effects=True, vmem_limit_bytes=56 * 1024 * 1024
        ),
        cost_estimate=pl.CostEstimate(flops=ffn, bytes_accessed=6 * 2**20, transcendentals=rows * 512),
    )(
        latent.transpose(0, 2, 1),
        queries.reshape(n_req * heads, width),
        w_gate[0],
        w_up[0],
        w_down[0],
        lengths,
        fresh_latent,
        tokens,
        routes.T,
        gates.T,
    )
    return context.reshape(n_req, heads, LAT), mixed


def solution(mesh):
    placed = (
        P("ep", "seq", None),
        P("ep", None),
        P("ep", "seq", None),
        P("ep", None),
        P("ep", "seq"),
        P("ep", None),
        P("ep", None),
        P("ep", None, "seq"),
        P("ep", None, "seq"),
        P("ep", "seq", None),
    )
    return jax.shard_map(
        on_device,
        mesh=mesh,
        in_specs=placed,
        out_specs=(P("ep", "seq", None), P("ep", "seq")),
        check_vma=False,
    )
```
